256 devices in a mesh: ctx: 64 (over x, y_lo, z), head: 4 (over y_hi, core).
Axes of the slice: x: 4, y: 4 (y_hi: 2, y_lo: 2; y = y_hi * 2 + y_lo), z: 8, core: 2. Of those that a mesh axis runs over, the one named last changes fastest.
Arguments:
- query: bfloat16 [16384, 16, 128], P('ctx', 'head'), may hold values from -24 to 24
- key_proj: bfloat16 [16384, 4, 128], P('ctx', 'head'), may hold values from -24 to 24
- value: bfloat16 [16384, 4, 128], P('ctx', 'head'), may hold values from -6 to 6
- output: bfloat16 [16384, 16, 128], P('ctx', 'head'), may hold values from -6 to 6
- lse: float32 [16384, 16], P('ctx', 'head')
- d_output: bfloat16 [16384, 16, 128], P('ctx', 'head'), may hold values from -6 to 6
- block_order: int32 [128], replicated, may hold values from 0 to 127, as said below
Outputs:
- d_query: float32 [16384, 16, 128], P('ctx', 'head')
- d_key: float32 [16384, 4, 128], P('ctx', 'head')
- d_value: float32 [16384, 4, 128], P('ctx', 'head')
The draws below stay inside these ranges and needn't reach their ends.
Inputs may be any that keep to these rules, and one draw needn't show every extreme that they name: `block_order`: a permutation of the 128 blocks: for some permutation s of the ctx indices, either every ctx index d holds blocks s(d) and 127 - s(d) in its two slots, or every one holds blocks 2 s(d) and 2 s(d) + 1.
All inputs are finite; a program needn't handle non-finite values.
Results may differ from the reference program's by a relative error of at most 0.008.
Values may be sent and summed in bfloat16 or wider, within the bound.
A program may use at most 64 MiB of HBM per device.

```python
import jax
import jax.numpy as jnp
from jax import lax

D_HEAD = 128
GROUP = 4
TOK_DEV = 256
TOKENS = 16384
BLOCK = 128
HEADS_KV = 4
HEADS_Q = 16
N_CTX = 64


def hot_pairs(key):
    chosen = jax.random.randint(jax.random.fold_in(key, 11), (TOKENS // 2,), 0, 32) == 0
    strength = jax.random.uniform(jax.random.fold_in(key, 12), (TOKENS // 2,), jnp.float32, 3.3, 5.5)
    heading = jnp.clip(jax.random.normal(jax.random.fold_in(key, 13), (TOKENS // 2, HEADS_KV, D_HEAD), jnp.float32), -4.0, 4.0)
    return (chosen, strength, heading)


def query_field(key, mixing):
    chosen, strength, heading = hot_pairs(key)
    inner = jax.random.fold_in(key, 1)
    gauss = jax.random.normal(inner, (TOKENS, HEADS_KV, GROUP, D_HEAD), jnp.float32)
    base = gauss
    hot_value = jnp.repeat((strength[:, None, None] * heading)[:, :, None, :], 2, axis=0)
    hot_row = jnp.stack([jnp.zeros_like(chosen), chosen], axis=1).reshape(TOKENS)
    hot_row = jnp.logical_and(hot_row, mixing > 0.5)
    mixed = jnp.where(hot_row[:, None, None, None], hot_value, base)
    return mixed.reshape(TOKENS, HEADS_Q, D_HEAD).astype(jnp.bfloat16)


def key_field(key, mixing):
    chosen, strength, heading = hot_pairs(key)
    inner = jax.random.fold_in(key, 2)
    gauss = jax.random.normal(inner, (TOKENS, HEADS_KV, D_HEAD), jnp.float32)
    base = gauss
    later = strength[:, None, None] * heading
    shrink = 1.0 - 2.0 / (11.3 * strength * strength)
    earlier = later * shrink[:, None, None]
    hot_value = jnp.stack([earlier, later], axis=1).reshape(TOKENS, HEADS_KV, D_HEAD)
    hot_row = jnp.logical_and(jnp.repeat(chosen, 2, axis=0), mixing > 0.5)
    return jnp.where(hot_row[:, None, None], hot_value, base).astype(jnp.bfloat16)


def order_field(key):
    inner = jax.random.fold_in(key, 5)
    layout = jax.random.randint(jax.random.fold_in(inner, 1), (), 0, 2)
    owner = jax.random.permutation(jax.random.fold_in(inner, 2), N_CTX).astype(jnp.int32)
    slot_ids = jnp.arange(2 * N_CTX, dtype=jnp.int32)
    device = slot_ids // 2
    slot_index = slot_ids % 2
    placed = owner[device]
    folded = jnp.where(slot_index == 0, placed, 2 * N_CTX - 1 - placed)
    contiguous = 2 * placed + slot_index
    return jnp.where(layout == 0, folded, contiguous).astype(jnp.int32)


def lse_field(key, mixing):
    queries = query_field(key, mixing).astype(jnp.float32).reshape(TOKENS, HEADS_KV, GROUP, D_HEAD)
    keys = key_field(key, mixing).astype(jnp.float32)
    order = order_field(key)
    row_ids = jnp.arange(TOKENS, dtype=jnp.int32)
    positions = order[2 * (row_ids // TOK_DEV) + row_ids % TOK_DEV // BLOCK] * BLOCK + row_ids % BLOCK
    block_rows = 256
    query_blocks = queries.reshape(TOKENS // block_rows, block_rows, HEADS_KV, GROUP, D_HEAD)
    pos_blocks = positions.reshape(TOKENS // block_rows, block_rows)

    def one_block(pair):
        query_block, pos_block = pair
        scores = D_HEAD ** (-0.5) * jnp.einsum('ihgd,jhd->ihgj', query_block, keys, precision=lax.Precision.HIGHEST)
        causal = positions[None, None, None, :] <= pos_block[:, None, None, None]
        masked = jnp.where(causal, scores, -1e+30)
        peak = jnp.max(masked, axis=3)
        total = jnp.sum(jnp.where(causal, jnp.exp(masked - peak[..., None]), 0.0), axis=3)
        return peak + jnp.log(total)
    result = lax.map(one_block, (query_blocks, pos_blocks))
    return result.reshape(TOKENS, HEADS_Q)


def draw_query(key, part):
    key = jax.random.fold_in(key, 0)
    return query_field(key, 0.0)


def draw_key_proj(key, part):
    key = jax.random.fold_in(key, 0)
    return key_field(key, 0.0)


def draw_lse(key, part):
    key = jax.random.fold_in(key, 0)
    return lse_field(key, 0.0)


def draw_block_order(key, part):
    key = jax.random.fold_in(key, 0)
    return order_field(key)


def block_scale(key, dims, cuts, least, high):
    def one(dim, blocks):
        steps = jax.random.uniform(jax.random.fold_in(jax.random.fold_in(key, 6), dim), (blocks,), jnp.float32, least / len(cuts), high / len(cuts))
        return jnp.repeat(jnp.exp(steps), dims[dim] // blocks).reshape((-1,) + (1,) * (len(dims) - dim - 1))

    factor_of = one(*cuts[0])
    for cut in cuts[1:]:
        factor_of = factor_of * one(*cut)
    return factor_of


def normal_values(stream_key, dims, scale, most, pieces=(), kind=jnp.bfloat16):
    gain = block_scale(stream_key, dims, pieces, -0.22, 0.18) if pieces else 1.0
    entries = jax.random.normal(stream_key, dims, jnp.float32) * scale * gain
    return jnp.minimum(jnp.maximum(entries, -most), most).astype(kind)


def setup_inputs(seed: int = 0) -> dict:
    arg_keys = jax.random.split(jax.random.key(seed), 8)
    return {
        "query": draw_query(jax.random.fold_in(arg_keys[7], 71), 0),
        "key_proj": draw_key_proj(jax.random.fold_in(arg_keys[7], 71), 0),
        "value": normal_values(arg_keys[2], (TOKENS, HEADS_KV, D_HEAD), 1.0, 6.0, ((0, 64), (1, 4))),
        "output": normal_values(arg_keys[3], (TOKENS, HEADS_Q, D_HEAD), 1.0, 6.0, ((0, 64), (1, 4))),
        "lse": draw_lse(jax.random.fold_in(arg_keys[7], 71), 0),
        "d_output": normal_values(arg_keys[5], (TOKENS, HEADS_Q, D_HEAD), 1.0, 6.0, ((0, 64), (1, 4))),
        "block_order": draw_block_order(jax.random.fold_in(arg_keys[7], 71), 0),
    }


def reference(query, key_proj, value, output, lse, d_output, block_order):
    row_ids = jnp.arange(TOKENS, dtype=jnp.int32)
    slot_ids = (2 * (row_ids // TOK_DEV) + (row_ids % TOK_DEV) // BLOCK).astype(jnp.int32)
    positions = block_order[slot_ids] * BLOCK + row_ids % BLOCK
    score_scale = D_HEAD ** -0.5
    keys_wide = key_proj.astype(jnp.float32)
    values_wide = value.astype(jnp.float32)
    grouped_query = query.reshape(TOKENS, HEADS_KV, GROUP, D_HEAD)
    grouped_output = output.reshape(TOKENS, HEADS_KV, GROUP, D_HEAD)
    grouped_grad = d_output.reshape(TOKENS, HEADS_KV, GROUP, D_HEAD)
    grouped_lse = lse.reshape(TOKENS, HEADS_KV, GROUP)
    block_rows = 256

    def block_step(carried, block_index):
        key_grad, value_grad = carried
        start = (block_index * block_rows).astype(jnp.int32)
        query_block = lax.dynamic_slice_in_dim(grouped_query, start, block_rows, 0).astype(jnp.float32)
        output_block = lax.dynamic_slice_in_dim(grouped_output, start, block_rows, 0).astype(jnp.float32)
        grad_block = lax.dynamic_slice_in_dim(grouped_grad, start, block_rows, 0).astype(jnp.float32)
        lse_block = lax.dynamic_slice_in_dim(grouped_lse, start, block_rows, 0)
        query_pos = lax.dynamic_slice_in_dim(positions, start, block_rows, 0)
        scores = score_scale * jnp.einsum('ihgd,jhd->hgij', query_block, keys_wide)
        causal = positions[None, None, None, :] <= query_pos[None, None, :, None]
        log_total = jnp.transpose(lse_block, (1, 2, 0))[..., None]
        probs = jnp.where(causal, jnp.exp(jnp.where(causal, scores - log_total, 0.0)), 0.0)
        probs_low = lax.optimization_barrier(probs.astype(jnp.bfloat16)).astype(jnp.float32)
        grad_probs = jnp.einsum('ihgd,jhd->hgij', grad_block, values_wide)
        delta = jnp.transpose(jnp.sum(grad_block * output_block, axis=3), (1, 2, 0))[..., None]
        grad_scores = probs * (grad_probs - delta)
        grad_low = lax.optimization_barrier(grad_scores.astype(jnp.bfloat16)).astype(jnp.float32)
        query_grad = score_scale * jnp.einsum('hgij,jhd->ihgd', grad_low, keys_wide)
        key_grad = key_grad + score_scale * jnp.einsum('hgij,ihgd->jhd', grad_low, query_block)
        value_grad = value_grad + jnp.einsum('hgij,ihgd->jhd', probs_low, grad_block)
        return (key_grad, value_grad), query_grad

    zeros_kv = jnp.zeros((TOKENS, HEADS_KV, D_HEAD), jnp.float32)
    (key_grad, value_grad), query_grads = lax.scan(block_step, (zeros_kv, zeros_kv), jnp.arange(TOKENS // block_rows, dtype=jnp.int32))
    d_query = query_grads.reshape(TOKENS, HEADS_Q, D_HEAD)
    return d_query, key_grad, value_grad
```

```python
import functools

import jax
import jax.numpy as jnp
from jax import lax
from jax.experimental import pallas as pl
from jax.experimental.pallas import tpu as pltpu
from jax.sharding import PartitionSpec as P

MESH = pl.DeviceIdType.MESH
LOG2E = 1.4426950408889634
F32 = jnp.float32
BF16 = jnp.bfloat16
BLK = 128
TOK = 256
ROWS = 512
SCALE = BLK ** (-0.5)
NX, NY, NZ = 4, 2, 8
OWN, LEFT, RIGHT, OPP = range(4)


def dot(a, b):
    return lax.dot_general(a, b, (((1,), (0,)), ((), ())), preferred_element_type=F32)


def tile_grads(q, do, qt, dot_t, lse2, delta, k, v, kt, keep=None):
    e = dot(k, qt) * (SCALE * LOG2E) - lse2
    if keep is not None:
        e = jnp.where(keep, e, -jnp.inf)
    p = jnp.exp2(e)
    ds = (p * (dot(v, dot_t) - delta)).astype(BF16)
    return dot(kt, ds), dot(ds, q), dot(p.astype(BF16), do)


def kernel(
    fold, order, q_in, do_in, out_in, lse_in, k_in, v_in, dq_out, dk_out, dv_out,
    qd0, qd1, qd2, qd3, qt0, qt1, qt2, qt3, rw0, rw1, rw2, rw3,
    kv, kt, dqa, dka, ktx, kup, kdn, ytx, yrx, qtx, qrx, orx, ssem, rsem,
):
    ctx = lax.axis_index("ctx")
    x, plane = ctx // (NY * NZ), ctx % (NY * NZ)
    y, z = plane // NZ, plane % NZ
    right = (x + 1) % NX * (NY * NZ) + plane
    left = (x + NX - 1) % NX * (NY * NZ) + plane
    opp = (x + 2) % NX * (NY * NZ) + plane
    partner = x * (NY * NZ) + (1 - y) * NZ + z
    up = ctx - z + (z + 1) % NZ
    down = ctx - z + (z + NZ - 1) % NZ
    qds, qts, rws = (qd0, qd1, qd2, qd3), (qt0, qt1, qt2, qt3), (rw0, rw1, rw2, rw3)
    owners = (ctx, left, right, opp)
    used = []

    def send(src, dst, device):
        index = len(used)
        used.append(index)
        copy = pltpu.make_async_remote_copy(
            src_ref=src, dst_ref=dst, send_sem=ssem.at[index], recv_sem=rsem.at[index],
            device_id={"ctx": device}, device_id_type=MESH,
        )
        return copy

    def begin(*copies):
        for copy in copies:
            copy.start()

    def arrive(*copies):
        for copy in copies:
            copy.wait_recv()

    to_right = [send(qd0.at[j], qd1.at[j], right) for j in range(2)]
    to_right += [send(rw0, rw1, right)]
    to_left = [send(qd0.at[j], qd2.at[j], left) for j in range(2)]
    to_left += [send(rw0, rw2, left)]
    far_right = [send(qd1.at[0], qd3.at[0], right), send(rw1.at[0], rw3.at[0], right)]
    far_left = [send(qd2.at[1], qd3.at[1], left), send(rw2.at[1], rw3.at[1], left)]
    across = send(kv.at[0, 0], kv.at[0, 1], partner)
    up_kv = [[send(kv.at[0, j], kv.at[7, j], up) for j in range(2)]]
    up_kv += [[send(kv.at[8 - s], kv.at[7 - s], up)] for s in (1, 2)] + [[send(kv.at[5, 0], kv.at[4, 0], up)]]
    down_kv = [[send(kv.at[0, j], kv.at[1, j], down) for j in range(2)]]
    down_kv += [[send(kv.at[s], kv.at[s + 1], down)] for s in (1, 2)] + [[send(kv.at[3, 1], kv.at[4, 1], down)]]
    up_sum = {4: send(ktx.at[4, 0], kup.at[3, 0], up)}
    up_sum.update({o: send(ktx.at[o], kup.at[o - 1], up) for o in (3, 2, 1)})
    down_sum = {4: send(ktx.at[4, 1], kdn.at[3, 1], down)}
    down_sum.update({o: send(ktx.at[8 - o], kdn.at[o - 1], down) for o in (3, 2, 1)})
    across_sum = send(ytx, yrx, partner)
    opp_sum = [send(qtx.at[OPP, 0], orx.at[0], right), send(qtx.at[OPP, 1], orx.at[1], left)]
    right_sum = [send(qtx.at[RIGHT, j], qrx.at[0, j], right) for j in (1, 0)]
    left_sum = [send(qtx.at[LEFT, j], qrx.at[1, j], left) for j in (0, 1)]

    kv[0, 0, 0] = k_in[...]
    kv[0, 0, 1] = v_in[...]
    for j in range(2):
        qd0[j, 0] = q_in[j]
        qd0[j, 1] = do_in[j]
        product = do_in[j].astype(F32) * out_in[j].astype(F32)
        rw0[j, 0] = lse_in[j] * LOG2E
        rw0[j, 1] = jnp.sum(product.T, axis=0, keepdims=True)

    barrier = pltpu.get_barrier_semaphore()
    for device in (right, left, partner, up, down):
        pl.semaphore_signal(barrier, inc=1, device_id={"ctx": device}, device_id_type=MESH)
    pl.semaphore_wait(barrier, 5)

    begin(across, up_kv[0][0], down_kv[0][0])
    begin(to_right[0], to_left[1], to_right[2], to_left[2], to_right[1], to_left[0])

    def turn_queries(i):
        for j in range(2):
            for part in range(2):
                qts[i][j, part] = qds[i][j, part].T

    def turn_keys(o):
        for j in range(2):
            kt[o, j] = kv[o, j, 0].T

    turn_queries(OWN)
    kt[0, 0] = kv[0, 0, 0].T
    dqa[...] = jnp.zeros_like(dqa)
    dka[...] = jnp.zeros_like(dka)

    def query_side(i, j):
        return qds[i][j, 0], qds[i][j, 1], qts[i][j, 0], qts[i][j, 1]

    for j in range(2):
        keys = BLK * (j + 1)
        shape = (keys, ROWS)
        keep = lax.broadcasted_iota(jnp.int32, shape, 0) <= (
            lax.broadcasted_iota(jnp.int32, shape, 1) // 4 + j * BLK
        )
        dqt, dk, dv = tile_grads(
            *query_side(OWN, j), rw0[j, 0], rw0[j, 1],
            kv[0, 0, 0, :keys], kv[0, 0, 1, :keys], kt[0, 0, :, :keys], keep,
        )
        dqa[OWN, j] += dqt
        dka[0, 0, 0, :keys] += dk
        dka[0, 0, 1, :keys] += dv

    def first_block(i, o, j):
        owner = x * (NY * NZ) + (y + j) % NY * NZ + (z + o) % NZ
        return order[2 * owners[i]], order[2 * owner]

    def folded(i, o, parts):
        lo = [kv[o, j, :, :BLK] for j in parts]
        dqt, dk, dv = tile_grads(
            *query_side(i, 1), rws[i][1, 0], rws[i][1, 1],
            jnp.concatenate([part[0] for part in lo], axis=0),
            jnp.concatenate([part[1] for part in lo], axis=0),
            jnp.concatenate([kt[o, j, :, :BLK] for j in parts], axis=1),
        )
        early = jnp.zeros((BLK, ROWS), F32)
        for n, j in enumerate(parts):
            query_first, key_first = first_block(i, o, j)
            later = query_first < key_first
            slot = later.astype(jnp.int32)
            weight = later.astype(F32)
            dqb, dkb, dvb = tile_grads(
                *query_side(i, slot), rws[i][slot, 0], rws[i][slot, 1],
                lax.select(later, kv[o, j, 0, BLK:], kv[o, j, 0, :BLK]),
                lax.select(later, kv[o, j, 1, BLK:], kv[o, j, 1, :BLK]),
                lax.select(later, kt[o, j, :, BLK:], kt[o, j, :, :BLK]),
            )
            dqt = dqt + weight * dqb
            early = early + (1.0 - weight) * dqb
            rows = slice(n * BLK, n * BLK + BLK)
            dka[o, j, 0, :BLK] += dk[rows] + (1.0 - weight) * dkb
            dka[o, j, 1, :BLK] += dv[rows] + (1.0 - weight) * dvb
            dka[o, j, 0, BLK:] += weight * dkb
            dka[o, j, 1, BLK:] += weight * dvb
        dqa[i, 0] += early
        dqa[i, 1] += dqt

    def whole(i, o, parts):
        for j in parts:
            query_first, key_first = first_block(i, o, j)
            hidden = jnp.where(query_first > key_first, 0.0, 1e30).astype(F32)
            for slot in range(2):
                dqt, dk, dv = tile_grads(
                    *query_side(i, slot), rws[i][slot, 0] + hidden, rws[i][slot, 1],
                    kv[o, j, 0], kv[o, j, 1], kt[o, j],
                )
                dqa[i, slot] += dqt
                dka[o, j, 0] += dk
                dka[o, j, 1] += dv

    work = folded if fold else whole

    arrive(across)
    begin(up_kv[0][1], down_kv[0][1])
    kt[0, 1] = kv[0, 1, 0].T
    work(OWN, 0, (1,))

    def near(s, carry):
        for hop in (1, 2):
            @pl.when(s == hop)
            def _():
                arrive(*up_kv[hop - 1], *down_kv[hop - 1])
                begin(*up_kv[hop], *down_kv[hop])

        def side(t, carry):
            o = s + t * (NZ - 2 * s)
            turn_keys(o)
            work(OWN, o, (0, 1))
            return carry

        return lax.fori_loop(0, 2, side, carry)

    lax.fori_loop(1, 3, near, jnp.int32(0))

    arrive(to_right[0], to_right[2], to_left[1], to_left[2])
    begin(*far_right, *far_left)
    arrive(to_right[1], to_left[0])
    turn_queries(LEFT)
    turn_queries(RIGHT)

    def sides(t, carry):
        @pl.when(t == 2)
        def _():
            arrive(*up_kv[2], *down_kv[2])
            begin(*up_kv[3], *down_kv[3])

        s = 1 + t // 2
        o = s + t % 2 * (NZ - 2 * s)
        work(LEFT, o, (0, 1))
        work(RIGHT, o, (0, 1))
        return carry

    lax.fori_loop(0, 4, sides, jnp.int32(0))

    arrive(*far_right, *far_left)
    turn_queries(OPP)
    arrive(*up_kv[3], *down_kv[3])
    turn_keys(4)
    turn_keys(3)
    turn_keys(5)

    def last(t, carry):
        s = 4 - (t + 1) // 2
        o = s + (1 - t % 2) * (NZ - 2 * s)

        @pl.when(t < 3)
        def _():
            work(OWN, o, (0, 1))
            work(LEFT, o, (0, 1))
            work(RIGHT, o, (0, 1))

        work(OPP, o, (0, 1))

        @pl.when(t == 0)
        def _():
            ktx[4] = dka[4].astype(BF16)
            begin(up_sum[4], down_sum[4])

        @pl.when(t == 1)
        def _():
            ktx[3, 1] = dka[3, 1].astype(BF16)
            arrive(up_sum[4])
            ktx[3, 0] = (dka[3, 0] + kup[3, 0].astype(F32)).astype(BF16)
            begin(up_sum[3])

        @pl.when(t == 2)
        def _():
            ktx[5, 0] = dka[5, 0].astype(BF16)
            arrive(down_sum[4])
            ktx[5, 1] = (dka[5, 1] + kdn[3, 1].astype(F32)).astype(BF16)
            begin(down_sum[3])

        for hop in (2, 1):
            @pl.when(t == 7 - 2 * hop)
            def _():
                arrive(up_sum[hop + 1])
                ktx[hop] = (dka[hop] + kup[hop].astype(F32)).astype(BF16)
                begin(up_sum[hop])

            @pl.when(t == 8 - 2 * hop)
            def _():
                arrive(down_sum[hop + 1])
                ktx[8 - hop] = (dka[8 - hop] + kdn[hop].astype(F32)).astype(BF16)
                begin(down_sum[hop])

        return carry

    lax.fori_loop(0, 7, last, jnp.int32(0))
    work(OPP, 0, (0, 1))
    qtx[OPP] = dqa[OPP].astype(BF16)
    begin(*opp_sum)
    work(LEFT, 0, (0, 1))
    work(RIGHT, 0, (0, 1))

    qtx[RIGHT, 1] = dqa[RIGHT, 1].astype(BF16)
    qtx[LEFT, 0] = dqa[LEFT, 0].astype(BF16)
    begin(right_sum[0], left_sum[0])
    arrive(*opp_sum)
    qtx[RIGHT, 0] = (dqa[RIGHT, 0] + orx[0].astype(F32)).astype(BF16)
    qtx[LEFT, 1] = (dqa[LEFT, 1] + orx[1].astype(F32)).astype(BF16)
    begin(right_sum[1], left_sum[1])
    arrive(up_sum[1], down_sum[1])
    ytx[...] = (dka[0, 1] + kup[0, 1].astype(F32) + kdn[0, 1].astype(F32)).astype(BF16)
    begin(across_sum)
    total = dka[0, 0] + kup[0, 0].astype(F32) + kdn[0, 0].astype(F32)
    arrive(across_sum)
    total = total + yrx[...].astype(F32)
    dk_out[...] = total[0] * SCALE
    dv_out[...] = total[1]
    for j, (a, b) in enumerate(((1, 0), (0, 1))):
        arrive(right_sum[a], left_sum[b])
        dq = dqa[OWN, j] + qrx[0, j].astype(F32) + qrx[1, j].astype(F32)
        dq_out[j] = dq.T * SCALE

    for copy in to_right + to_left + far_right + far_left + [across, across_sum]:
        copy.wait_send()
    for group in up_kv + down_kv:
        for copy in group:
            copy.wait_send()
    for copy in list(up_sum.values()) + list(down_sum.values()) + opp_sum + right_sum + left_sum:
        copy.wait_send()


N_COPIES = 3 + 3 + 2 + 2 + 1 + 5 + 5 + 4 + 4 + 1 + 2 + 2 + 2


def grads(fold, order, q, do, out, lse, k, v):
    smem = pl.BlockSpec(memory_space=pltpu.SMEM)
    vmem = pl.BlockSpec(memory_space=pltpu.VMEM)
    queries = [pltpu.VMEM((2, 2, ROWS, BLK), BF16)] * 4
    turned = [pltpu.VMEM((2, 2, BLK, ROWS), BF16)] * 4
    rows = [pltpu.VMEM((2, 2, 1, ROWS), F32)] * 4
    return pl.pallas_call(
        functools.partial(kernel, fold),
        out_shape=(
            jax.ShapeDtypeStruct((2, ROWS, BLK), F32),
            jax.ShapeDtypeStruct((TOK, BLK), F32),
            jax.ShapeDtypeStruct((TOK, BLK), F32),
        ),
        in_specs=[smem] + [vmem] * 6,
        out_specs=(vmem, vmem, vmem),
        scratch_shapes=queries + turned + rows + [
            pltpu.VMEM((NZ, NY, 2, TOK, BLK), BF16),
            pltpu.VMEM((NZ, NY, BLK, TOK), BF16),
            pltpu.VMEM((4, 2, BLK, ROWS), F32),
            pltpu.VMEM((NZ, NY, 2, TOK, BLK), F32),
            pltpu.VMEM((NZ, NY, 2, TOK, BLK), BF16),
            pltpu.VMEM((4, NY, 2, TOK, BLK), BF16),
            pltpu.VMEM((4, NY, 2, TOK, BLK), BF16),
            pltpu.VMEM((2, TOK, BLK), BF16),
            pltpu.VMEM((2, TOK, BLK), BF16),
            pltpu.VMEM((4, 2, BLK, ROWS), BF16),
            pltpu.VMEM((2, 2, BLK, ROWS), BF16),
            pltpu.VMEM((2, BLK, ROWS), BF16),
            pltpu.SemaphoreType.DMA((N_COPIES,)),
            pltpu.SemaphoreType.DMA((N_COPIES,)),
        ],
        compiler_params=pltpu.CompilerParams(
            collective_id=0 if fold else 1, has_side_effects=True, vmem_limit_bytes=48 * 1024 * 1024
        ),
        name="folded" if fold else "whole",
    )(order, q, do, out, lse, k, v)


def per_device(query, key_proj, value, output, lse, d_output, block_order):
    args = (
        block_order,
        query.reshape(2, ROWS, BLK),
        d_output.reshape(2, ROWS, BLK),
        output.reshape(2, ROWS, BLK),
        lse.reshape(2, 1, ROWS),
        key_proj.reshape(TOK, BLK),
        value.reshape(TOK, BLK),
    )
    is_folded = block_order[0] + block_order[1] == 2 * NX * NY * NZ - 1
    dq, dk, dv = lax.cond(is_folded, functools.partial(grads, True), functools.partial(grads, False), *args)
    return dq.reshape(query.shape), dk.reshape(key_proj.shape), dv.reshape(value.shape)


def solution(mesh):
    in_specs = (
        P("ctx", "head", None),
        P("ctx", "head", None),
        P("ctx", "head", None),
        P("ctx", "head", None),
        P("ctx", "head"),
        P("ctx", "head", None),
        P(),
    )
    out_specs = (P("ctx", "head", None), P("ctx", "head", None), P("ctx", "head", None))
    return jax.shard_map(
        per_device, mesh=mesh, in_specs=in_specs, out_specs=out_specs, check_vma=False
    )
```

```python
import functools

import jax
import jax.numpy as jnp
from jax import lax
from jax.experimental import pallas as pl
from jax.experimental.pallas import tpu as pltpu
from jax.sharding import PartitionSpec as P

MESH = pl.DeviceIdType.MESH
LOG2E = 1.4426950408889634
F32 = jnp.float32
BF16 = jnp.bfloat16
BLK = 128
TOK = 256
ROWS = 512
SCALE = BLK ** (-0.5)
NX, NY, NZ = 4, 2, 8
OWN, LEFT, RIGHT, OPP = range(4)


def dot(a, b):
    return lax.dot_general(a, b, (((1,), (0,)), ((), ())), preferred_element_type=F32)


def pipelined(chunks):
    made = chunks[0][0]()
    for n, (_, middle, end) in enumerate(chunks):
        following = chunks[n + 1][0]() if n + 1 < len(chunks) else None
        end(middle(*made))
        made = following


def chunk(q, do, qt, dot_t, lse2, delta, k, v, end, keep=None):
    def first():
        return dot(k(), qt()), dot(v(), dot_t())

    def middle(s, dp):
        e = s * (SCALE * LOG2E) - lse2()
        if keep is not None:
            e = jnp.where(keep, e, -jnp.inf)
        p = jnp.exp2(e)
        return p.astype(BF16), (p * (dp - delta())).astype(BF16)

    return first, middle, end


def kernel(
    fold, order, q_in, do_in, out_in, lse_in, k_in, v_in, dq_out, dk_out, dv_out,
    qd0, qd1, qd2, qd3, qt0, qt1, qt2, qt3, rw0, rw1, rw2, rw3,
    kv, kt, dqa, dka, ktx, kup, kdn, ytx, yrx, qtx, qrx, orx, ssem, rsem,
):
    ctx = lax.axis_index("ctx")
    x, plane = ctx // (NY * NZ), ctx % (NY * NZ)
    y, z = plane // NZ, plane % NZ
    right = (x + 1) % NX * (NY * NZ) + plane
    left = (x + NX - 1) % NX * (NY * NZ) + plane
    opp = (x + 2) % NX * (NY * NZ) + plane
    partner = x * (NY * NZ) + (1 - y) * NZ + z
    up = ctx - z + (z + 1) % NZ
    down = ctx - z + (z + NZ - 1) % NZ
    qds, qts, rws = (qd0, qd1, qd2, qd3), (qt0, qt1, qt2, qt3), (rw0, rw1, rw2, rw3)
    owners = (ctx, left, right, opp)
    used = []

    def send(src, dst, device):
        index = len(used)
        used.append(index)
        copy = pltpu.make_async_remote_copy(
            src_ref=src, dst_ref=dst, send_sem=ssem.at[index], recv_sem=rsem.at[index],
            device_id={"ctx": device}, device_id_type=MESH,
        )
        return copy

    def begin(*copies):
        for copy in copies:
            copy.start()

    def arrive(*copies):
        for copy in copies:
            copy.wait_recv()

    to_right = [send(qd0.at[j], qd1.at[j], right) for j in range(2)]
    to_right += [send(rw0, rw1, right)]
    to_left = [send(qd0.at[j], qd2.at[j], left) for j in range(2)]
    to_left += [send(rw0, rw2, left)]
    far_right = [send(qd1.at[0], qd3.at[0], right), send(rw1.at[0], rw3.at[0], right)]
    far_left = [send(qd2.at[1], qd3.at[1], left), send(rw2.at[1], rw3.at[1], left)]
    across = send(kv.at[0, 0], kv.at[0, 1], partner)
    up_kv = [[send(kv.at[0, j], kv.at[7, j], up) for j in range(2)]]
    up_kv += [[send(kv.at[8 - s], kv.at[7 - s], up)] for s in (1, 2)] + [[send(kv.at[5, 0], kv.at[4, 0], up)]]
    down_kv = [[send(kv.at[0, j], kv.at[1, j], down) for j in range(2)]]
    down_kv += [[send(kv.at[s], kv.at[s + 1], down)] for s in (1, 2)] + [[send(kv.at[3, 1], kv.at[4, 1], down)]]
    up_sum = {4: send(ktx.at[4, 0], kup.at[3, 0], up)}
    up_sum.update({o: send(ktx.at[o], kup.at[o - 1], up) for o in (3, 2, 1)})
    down_sum = {4: send(ktx.at[4, 1], kdn.at[3, 1], down)}
    down_sum.update({o: send(ktx.at[8 - o], kdn.at[o - 1], down) for o in (3, 2, 1)})
    across_sum = send(ytx, yrx, partner)
    opp_sum = [send(qtx.at[OPP, 0], orx.at[0], right), send(qtx.at[OPP, 1], orx.at[1], left)]
    right_sum = [send(qtx.at[RIGHT, j], qrx.at[0, j], right) for j in (1, 0)]
    left_sum = [send(qtx.at[LEFT, j], qrx.at[1, j], left) for j in (0, 1)]

    def lse_row(columns):
        shape = (BLK, ROWS)
        column = lax.broadcasted_iota(jnp.int32, shape, 1)
        spread = jnp.broadcast_to(columns[:, 0:1], shape)
        for head in range(1, 4):
            spread = jnp.where(column % 4 == head, jnp.broadcast_to(columns[:, head : head + 1], shape), spread)
        mine = column // 4 == lax.broadcasted_iota(jnp.int32, shape, 0)
        return jnp.sum(jnp.where(mine, spread, 0.0), axis=0, keepdims=True)

    kv[0, 0, 0] = k_in[...]
    kv[0, 0, 1] = v_in[...]
    for j in range(2):
        qd0[j, 0] = q_in[j]
        qd0[j, 1] = do_in[j]
        product = do_in[j].astype(F32) * out_in[j].astype(F32)
        rw0[j, 0] = lse_row(lse_in[:, j * BLK : j * BLK + BLK].T) * LOG2E
        rw0[j, 1] = jnp.sum(product.T, axis=0, keepdims=True)

    barrier = pltpu.get_barrier_semaphore()
    for device in (right, left, partner, up, down):
        pl.semaphore_signal(barrier, inc=1, device_id={"ctx": device}, device_id_type=MESH)
    pl.semaphore_wait(barrier, 5)

    begin(across, up_kv[0][0], down_kv[0][0])
    begin(to_right[0], to_left[1], to_right[2], to_left[2], to_right[1], to_left[0])

    def turn_queries(i):
        for j in range(2):
            for part in range(2):
                qts[i][j, part] = qds[i][j, part].T

    def turn_keys(o):
        for j in range(2):
            kt[o, j] = kv[o, j, 0].T

    turn_queries(OWN)
    kt[0, 0] = kv[0, 0, 0].T
    dqa[...] = jnp.zeros_like(dqa)
    dka[...] = jnp.zeros_like(dka)

    def halves(i, j, h):
        cut = slice(h * TOK, h * TOK + TOK)
        return (
            lambda: qds[i][j, 0, cut], lambda: qds[i][j, 1, cut],
            lambda: qts[i][j, 0, :, cut], lambda: qts[i][j, 1, :, cut],
        )

    def row(i, j, kind, h):
        return lambda: rws[i][j, kind, :, h * TOK : h * TOK + TOK]

    def own_chunks():
        chunks = []
        for j in range(2):
            keys = BLK * (j + 1)
            for h in range(2):
                shape = (keys, TOK)
                keep = lax.broadcasted_iota(jnp.int32, shape, 0) <= (
                    (lax.broadcasted_iota(jnp.int32, shape, 1) + h * TOK) // 4 + j * BLK
                )

                def end(made, j=j, h=h, keys=keys):
                    p, ds = made
                    cut = slice(h * TOK, h * TOK + TOK)
                    dqa[OWN, j, :, cut] += dot(kt[0, 0, :, :keys], ds)
                    dka[0, 0, 0, :keys] += dot(ds, qd0[j, 0, cut])
                    dka[0, 0, 1, :keys] += dot(p, qd0[j, 1, cut])

                chunks.append(
                    chunk(
                        *halves(OWN, j, h), row(OWN, j, 0, h), row(OWN, j, 1, h),
                        lambda keys=keys: kv[0, 0, 0, :keys], lambda keys=keys: kv[0, 0, 1, :keys], end, keep,
                    )
                )
        return chunks

    def first_block(i, o, j):
        owner = x * (NY * NZ) + (y + j) % NY * NZ + (z + o) % NZ
        return order[2 * owners[i]], order[2 * owner]

    def folded(i, o, parts):
        size = BLK * len(parts)
        state = {"p": [], "ds": [], "dsb": []}
        chunks = []

        def stack(index):
            return lambda: jnp.concatenate([kv[o, j, index, :BLK] for j in parts], axis=0)

        def end_later(made, h):
            state["p"].append(made[0])
            state["ds"].append(made[1])
            if h == 1:
                p = jnp.concatenate(state["p"], axis=1)
                ds = jnp.concatenate(state["ds"], axis=1)
                state["dv"] = dot(p, qds[i][1, 1])
                state["dk"] = dot(ds, qds[i][1, 0])
                state["dq"] = dot(jnp.concatenate([kt[o, j, :, :BLK] for j in parts], axis=1), ds)

        for h in range(2):
            chunks.append(
                chunk(
                    *halves(i, 1, h), row(i, 1, 0, h), row(i, 1, 1, h), stack(0), stack(1),
                    functools.partial(end_later, h=h),
                )
            )

        weights = []
        for n, j in enumerate(parts):
            query_first, key_first = first_block(i, o, j)
            later = query_first < key_first
            slot = later.astype(jnp.int32)
            weight = later.astype(F32)
            weights.append(weight)

            def pick(index, later=later, j=j):
                return lambda: lax.select(later, kv[o, j, index, BLK:], kv[o, j, index, :BLK])

            def end_same(made, n=n, j=j, slot=slot, weight=weight, later=later):
                p, ds = made
                dv, dk = dot(p, qds[i][slot, 1]), dot(ds, qds[i][slot, 0])
                rows = slice(n * BLK, n * BLK + BLK)
                late_dk, late_dv = weight * dk, weight * dv
                dka[o, j, 0, :BLK] += state["dk"][rows] + (dk - late_dk)
                dka[o, j, 1, :BLK] += state["dv"][rows] + (dv - late_dv)
                dka[o, j, 0, BLK:] += late_dk
                dka[o, j, 1, BLK:] += late_dv
                state["dsb"].append(ds)
                if n == len(parts) - 1:
                    turned = []
                    for m, (jm, wm) in enumerate(zip(parts, weights)):
                        late = kt[o, jm, :, BLK:] * wm.astype(BF16)
                        early = kt[o, jm, :, :BLK] * (1.0 - wm).astype(BF16)
                        turned.append(jnp.concatenate([late, early], axis=0))
                    both = dot(jnp.concatenate(turned, axis=1), jnp.concatenate(state["dsb"], axis=0))
                    dqa[i, 1] += state["dq"] + both[:BLK]
                    dqa[i, 0] += both[BLK:]

            chunks.append(
                chunk(
                    None, None,
                    lambda slot=slot: qts[i][slot, 0], lambda slot=slot: qts[i][slot, 1],
                    lambda slot=slot: rws[i][slot, 0], lambda slot=slot: rws[i][slot, 1],
                    pick(0), pick(1), end_same,
                )
            )
        return chunks

    def whole(i, o, parts):
        chunks = []
        for j in parts:
            query_first, key_first = first_block(i, o, j)
            hidden = jnp.where(query_first > key_first, 0.0, 1e30).astype(F32)
            state = {"p": [], "ds": []}
            for slot in range(2):
                for h in range(2):
                    def end(made, slot=slot, h=h, j=j, state=state):
                        state["p"].append(made[0])
                        state["ds"].append(made[1])
                        if h == 1:
                            ds = jnp.concatenate(state["ds"][-2:], axis=1)
                            dqa[i, slot] += dot(kt[o, j], ds)
                        if h == 1 and slot == 1:
                            p = jnp.concatenate(state["p"], axis=1)
                            ds = jnp.concatenate(state["ds"], axis=1)
                            dka[o, j, 1] += dot(p, jnp.concatenate([qds[i][0, 1], qds[i][1, 1]], axis=0))
                            dka[o, j, 0] += dot(ds, jnp.concatenate([qds[i][0, 0], qds[i][1, 0]], axis=0))

                    lse2 = row(i, slot, 0, h)
                    chunks.append(
                        chunk(
                            *halves(i, slot, h), lambda lse2=lse2, hidden=hidden: lse2() + hidden, row(i, slot, 1, h),
                            lambda j=j: kv[o, j, 0], lambda j=j: kv[o, j, 1], end,
                        )
                    )
        return chunks

    step = folded if fold else whole

    def work(*steps):
        pipelined([c for i, o, parts in steps for c in step(i, o, parts)])

    pipelined(own_chunks())

    arrive(across)
    begin(up_kv[0][1], down_kv[0][1])
    kt[0, 1] = kv[0, 1, 0].T
    work((OWN, 0, (1,)))

    def near(s, carry):
        for hop in (1, 2):
            @pl.when(s == hop)
            def _():
                arrive(*up_kv[hop - 1], *down_kv[hop - 1])
                begin(*up_kv[hop], *down_kv[hop])

        turn_keys(s)
        turn_keys(NZ - s)
        work((OWN, s, (0, 1)), (OWN, NZ - s, (0, 1)))
        return carry

    lax.fori_loop(1, 3, near, jnp.int32(0))

    arrive(to_right[0], to_right[2], to_left[1], to_left[2])
    begin(*far_right, *far_left)
    arrive(to_right[1], to_left[0])
    turn_queries(LEFT)
    turn_queries(RIGHT)

    def sides(t, carry):
        @pl.when(t == 2)
        def _():
            arrive(*up_kv[2], *down_kv[2])
            begin(*up_kv[3], *down_kv[3])

        s = 1 + t // 2
        o = s + t % 2 * (NZ - 2 * s)
        work((LEFT, o, (0, 1)), (RIGHT, o, (0, 1)))
        return carry

    lax.fori_loop(0, 4, sides, jnp.int32(0))

    arrive(*far_right, *far_left)
    turn_queries(OPP)
    arrive(*up_kv[3], *down_kv[3])
    turn_keys(4)
    turn_keys(3)
    turn_keys(5)

    def far(t, carry):
        o = 4 - t + t // 2 * 3
        work((OWN, o, (0, 1)), (LEFT, o, (0, 1)), (RIGHT, o, (0, 1)), (OPP, o, (0, 1)))

        @pl.when(t == 0)
        def _():
            ktx[4] = dka[4].astype(BF16)
            begin(up_sum[4], down_sum[4])

        @pl.when(t == 1)
        def _():
            ktx[3, 1] = dka[3, 1].astype(BF16)
            arrive(up_sum[4])
            ktx[3, 0] = (dka[3, 0] + kup[3, 0].astype(F32)).astype(BF16)
            begin(up_sum[3])

        @pl.when(t == 2)
        def _():
            ktx[5, 0] = dka[5, 0].astype(BF16)
            arrive(down_sum[4])
            ktx[5, 1] = (dka[5, 1] + kdn[3, 1].astype(F32)).astype(BF16)
            begin(down_sum[3])

        return carry

    lax.fori_loop(0, 3, far, jnp.int32(0))

    def opposite(t, carry):
        s = 2 - t
        work((OPP, s, (0, 1)), (OPP, NZ - s, (0, 1)))
        for hop in (2, 1):
            @pl.when(s == hop)
            def _():
                arrive(up_sum[hop + 1])
                ktx[hop] = (dka[hop] + kup[hop].astype(F32)).astype(BF16)
                begin(up_sum[hop])
                arrive(down_sum[hop + 1])
                ktx[8 - hop] = (dka[8 - hop] + kdn[hop].astype(F32)).astype(BF16)
                begin(down_sum[hop])

        return carry

    lax.fori_loop(0, 2, opposite, jnp.int32(0))
    work((OPP, 0, (0, 1)))
    qtx[OPP] = dqa[OPP].astype(BF16)
    begin(*opp_sum)
    work((LEFT, 0, (0, 1)), (RIGHT, 0, (0, 1)))

    qtx[RIGHT, 1] = dqa[RIGHT, 1].astype(BF16)
    qtx[LEFT, 0] = dqa[LEFT, 0].astype(BF16)
    begin(right_sum[0], left_sum[0])
    arrive(*opp_sum)
    qtx[RIGHT, 0] = (dqa[RIGHT, 0] + orx[0].astype(F32)).astype(BF16)
    qtx[LEFT, 1] = (dqa[LEFT, 1] + orx[1].astype(F32)).astype(BF16)
    begin(right_sum[1], left_sum[1])
    arrive(up_sum[1], down_sum[1])
    ytx[...] = (dka[0, 1] + kup[0, 1].astype(F32) + kdn[0, 1].astype(F32)).astype(BF16)
    begin(across_sum)
    total = dka[0, 0] + kup[0, 0].astype(F32) + kdn[0, 0].astype(F32)
    arrive(across_sum)
    total = total + yrx[...].astype(F32)
    dk_out[...] = total[0] * SCALE
    dv_out[...] = total[1]
    for j, (a, b) in enumerate(((1, 0), (0, 1))):
        arrive(right_sum[a], left_sum[b])
        dq = dqa[OWN, j] + qrx[0, j].astype(F32) + qrx[1, j].astype(F32)
        dq_out[j] = dq.T * SCALE

    for copy in to_right + to_left + far_right + far_left + [across, across_sum]:
        copy.wait_send()
    for group in up_kv + down_kv:
        for copy in group:
            copy.wait_send()
    for copy in list(up_sum.values()) + list(down_sum.values()) + opp_sum + right_sum + left_sum:
        copy.wait_send()


N_COPIES = 3 + 3 + 2 + 2 + 1 + 5 + 5 + 4 + 4 + 1 + 2 + 2 + 2


def grads(fold, order, q, do, out, lse, k, v):
    smem = pl.BlockSpec(memory_space=pltpu.SMEM)
    vmem = pl.BlockSpec(memory_space=pltpu.VMEM)
    queries = [pltpu.VMEM((2, 2, ROWS, BLK), BF16)] * 4
    turned = [pltpu.VMEM((2, 2, BLK, ROWS), BF16)] * 4
    rows = [pltpu.VMEM((2, 2, 1, ROWS), F32)] * 4
    return pl.pallas_call(
        functools.partial(kernel, fold),
        out_shape=(
            jax.ShapeDtypeStruct((2, ROWS, BLK), F32),
            jax.ShapeDtypeStruct((TOK, BLK), F32),
            jax.ShapeDtypeStruct((TOK, BLK), F32),
        ),
        in_specs=[smem] + [vmem] * 6,
        out_specs=(vmem, vmem, vmem),
        scratch_shapes=queries + turned + rows + [
            pltpu.VMEM((NZ, NY, 2, TOK, BLK), BF16),
            pltpu.VMEM((NZ, NY, BLK, TOK), BF16),
            pltpu.VMEM((4, 2, BLK, ROWS), F32),
            pltpu.VMEM((NZ, NY, 2, TOK, BLK), F32),
            pltpu.VMEM((NZ, NY, 2, TOK, BLK), BF16),
            pltpu.VMEM((4, NY, 2, TOK, BLK), BF16),
            pltpu.VMEM((4, NY, 2, TOK, BLK), BF16),
            pltpu.VMEM((2, TOK, BLK), BF16),
            pltpu.VMEM((2, TOK, BLK), BF16),
            pltpu.VMEM((4, 2, BLK, ROWS), BF16),
            pltpu.VMEM((2, 2, BLK, ROWS), BF16),
            pltpu.VMEM((2, BLK, ROWS), BF16),
            pltpu.SemaphoreType.DMA((N_COPIES,)),
            pltpu.SemaphoreType.DMA((N_COPIES,)),
        ],
        compiler_params=pltpu.CompilerParams(
            collective_id=0 if fold else 1, has_side_effects=True, vmem_limit_bytes=48 * 1024 * 1024
        ),
        name="folded" if fold else "whole",
    )(order, q, do, out, lse, k, v)


def per_device(query, key_proj, value, output, lse, d_output, block_order):
    args = (
        block_order,
        query.reshape(2, ROWS, BLK),
        d_output.reshape(2, ROWS, BLK),
        output.reshape(2, ROWS, BLK),
        lse.T,
        key_proj.reshape(TOK, BLK),
        value.reshape(TOK, BLK),
    )
    is_folded = block_order[0] + block_order[1] == 2 * NX * NY * NZ - 1
    dq, dk, dv = lax.cond(is_folded, functools.partial(grads, True), functools.partial(grads, False), *args)
    return dq.reshape(query.shape), dk.reshape(key_proj.shape), dv.reshape(value.shape)


def solution(mesh):
    in_specs = (
        P("ctx", "head", None),
        P("ctx", "head", None),
        P("ctx", "head", None),
        P("ctx", "head", None),
        P("ctx", "head"),
        P("ctx", "head", None),
        P(),
    )
    out_specs = (P("ctx", "head", None), P("ctx", "head", None), P("ctx", "head", None))
    return jax.shard_map(
        per_device, mesh=mesh, in_specs=in_specs, out_specs=out_specs, check_vma=False
    )
```

```python
import functools

import jax
import jax.numpy as jnp
from jax import lax
from jax.experimental import pallas as pl
from jax.experimental.pallas import tpu as pltpu
from jax.sharding import PartitionSpec as P

MESH = pl.DeviceIdType.MESH
LOG2E = 1.4426950408889634
F32 = jnp.float32
BF16 = jnp.bfloat16
BLK = 128
TOK = 256
ROWS = 512
SCALE = BLK ** (-0.5)
NX, NY, NZ = 4, 2, 8
OWN, RIGHT, OPP, LEFT = range(4)


def dot(a, b):
    return lax.dot_general(a, b, (((1,), (0,)), ((), ())), preferred_element_type=F32)


def pipelined(chunks):
    made = chunks[0][0]()
    for n, (_, middle, end) in enumerate(chunks):
        following = chunks[n + 1][0]() if n + 1 < len(chunks) else None
        end(middle(*made))
        made = following


def chunk(qt, dot_t, lse2, delta, k, v, end, keep=None):
    def first():
        return dot(k(), qt()), dot(v(), dot_t())

    def middle(s, dp):
        e = s * (SCALE * LOG2E) - lse2()
        if keep is not None:
            e = jnp.where(keep, e, -jnp.inf)
        p = jnp.exp2(e)
        return p.astype(BF16), (p * (dp - delta())).astype(BF16)

    return first, middle, end


def kernel(
    fold, order, q_in, do_in, out_in, lse_in, k_in, v_in, dq_out, dk_out, dv_out,
    from_right, from_opp, from_left, rows_right, rows_opp, rows_left, qn, qt, rw,
    kv, kt, dqa, dka, ktx, kup, kdn, ytx, yrx, qtx, qrx, orx, ssem, rsem,
):
    ctx = lax.axis_index("ctx")
    x, plane = ctx // (NY * NZ), ctx % (NY * NZ)
    y, z = plane // NZ, plane % NZ
    right = (x + 1) % NX * (NY * NZ) + plane
    left = (x + NX - 1) % NX * (NY * NZ) + plane
    partner = x * (NY * NZ) + (1 - y) * NZ + z
    up = ctx - z + (z + 1) % NZ
    down = ctx - z + (z + NZ - 1) % NZ
    used = []

    def send(src, dst, device):
        index = len(used)
        used.append(index)
        copy = pltpu.make_async_remote_copy(
            src_ref=src, dst_ref=dst, send_sem=ssem.at[index], recv_sem=rsem.at[index],
            device_id={"ctx": device}, device_id_type=MESH,
        )
        return copy

    def begin(*copies):
        for copy in copies:
            copy.start()

    def arrive(*copies):
        for copy in copies:
            copy.wait_recv()

    to_right = [send(qn.at[OWN, j], from_left.at[j], right) for j in range(2)]
    to_right += [send(rw.at[OWN], rows_left, right)]
    to_left = [send(qn.at[OWN, j], from_right.at[j], left) for j in range(2)]
    to_left += [send(rw.at[OWN], rows_right, left)]
    far_right = [send(from_left.at[0], from_opp.at[0], right), send(rows_left.at[0], rows_opp.at[0], right)]
    far_left = [send(from_right.at[1], from_opp.at[1], left), send(rows_right.at[1], rows_opp.at[1], left)]
    across = send(kv.at[0, 0], kv.at[0, 1], partner)
    up_kv = [[send(kv.at[0, j], kv.at[7, j], up) for j in range(2)]]
    up_kv += [[send(kv.at[8 - s], kv.at[7 - s], up)] for s in (1, 2)] + [[send(kv.at[5, 0], kv.at[4, 0], up)]]
    down_kv = [[send(kv.at[0, j], kv.at[1, j], down) for j in range(2)]]
    down_kv += [[send(kv.at[s], kv.at[s + 1], down)] for s in (1, 2)] + [[send(kv.at[3, 1], kv.at[4, 1], down)]]
    up_sum = {4: send(ktx.at[4, 0], kup.at[3, 0], up)}
    up_sum.update({o: send(ktx.at[o], kup.at[o - 1], up) for o in (3, 2, 1)})
    down_sum = {4: send(ktx.at[4, 1], kdn.at[3, 1], down)}
    down_sum.update({o: send(ktx.at[8 - o], kdn.at[o - 1], down) for o in (3, 2, 1)})
    across_sum = send(ytx, yrx, partner)
    opp_sum = [send(qtx.at[OPP, 0], orx.at[0], right), send(qtx.at[OPP, 1], orx.at[1], left)]
    right_sum = [send(qtx.at[RIGHT, j], qrx.at[0, j], right) for j in (1, 0)]
    left_sum = [send(qtx.at[LEFT, j], qrx.at[1, j], left) for j in (0, 1)]

    def lse_row(columns):
        shape = (BLK, ROWS)
        column = lax.broadcasted_iota(jnp.int32, shape, 1)
        spread = jnp.broadcast_to(columns[:, 0:1], shape)
        for head in range(1, 4):
            spread = jnp.where(column % 4 == head, jnp.broadcast_to(columns[:, head : head + 1], shape), spread)
        mine = column // 4 == lax.broadcasted_iota(jnp.int32, shape, 0)
        return jnp.sum(jnp.where(mine, spread, 0.0), axis=0, keepdims=True)

    kv[0, 0, 0] = k_in[...]
    kv[0, 0, 1] = v_in[...]
    for j in range(2):
        qn[OWN, j, 0] = q_in[j]
        qn[OWN, j, 1] = do_in[j]
        product = do_in[j].astype(F32) * out_in[j].astype(F32)
        rw[OWN, j, 0] = lse_row(lse_in[:, j * BLK : j * BLK + BLK].T) * LOG2E
        rw[OWN, j, 1] = jnp.sum(product.T, axis=0, keepdims=True)

    barrier = pltpu.get_barrier_semaphore()
    for device in (right, left, partner, up, down):
        pl.semaphore_signal(barrier, inc=1, device_id={"ctx": device}, device_id_type=MESH)
    pl.semaphore_wait(barrier, 5)

    begin(across, up_kv[0][0], down_kv[0][0])
    begin(to_right[0], to_left[1], to_right[2], to_left[2], to_right[1], to_left[0])

    def turn_queries(i, landed, landed_rows):
        for j in range(2):
            for part in range(2):
                if landed is not None:
                    qn[i, j, part] = landed[j, part]
                    rw[i, j, part] = landed_rows[j, part]
                qt[i, j, part] = qn[i, j, part].T

    def turn_keys(o):
        for j in range(2):
            kt[o, j] = kv[o, j, 0].T

    turn_queries(OWN, None, None)
    kt[0, 0] = kv[0, 0, 0].T
    dqa[...] = jnp.zeros_like(dqa)
    dka[...] = jnp.zeros_like(dka)

    def halves(i, j, h):
        cut = slice(h * TOK, h * TOK + TOK)
        return (
            lambda: qt[i, j, 0, :, cut], lambda: qt[i, j, 1, :, cut],
        )

    def row(i, j, kind, h):
        return lambda: rw[i, j, kind, :, h * TOK : h * TOK + TOK]

    def own_chunks():
        chunks = []
        for j in range(2):
            keys = BLK * (j + 1)
            for h in range(2):
                shape = (keys, TOK)
                keep = lax.broadcasted_iota(jnp.int32, shape, 0) <= (
                    (lax.broadcasted_iota(jnp.int32, shape, 1) + h * TOK) // 4 + j * BLK
                )

                def end(made, j=j, h=h, keys=keys):
                    p, ds = made
                    cut = slice(h * TOK, h * TOK + TOK)
                    dqa[OWN, j, :, cut] += dot(kt[0, 0, :, :keys], ds)
                    dka[0, 0, 0, :keys] += dot(ds, qn[OWN, j, 0, cut])
                    dka[0, 0, 1, :keys] += dot(p, qn[OWN, j, 1, cut])

                chunks.append(
                    chunk(
                        *halves(OWN, j, h), row(OWN, j, 0, h), row(OWN, j, 1, h),
                        lambda keys=keys: kv[0, 0, 0, :keys], lambda keys=keys: kv[0, 0, 1, :keys], end, keep,
                    )
                )
        return chunks

    def first_block(i, o, j):
        owner = x * (NY * NZ) + (y + j) % NY * NZ + (z + o) % NZ
        return order[2 * ((x + i) % NX * (NY * NZ) + plane)], order[2 * owner]

    def folded(i, o, parts):
        size = BLK * len(parts)
        state = {"p": [], "ds": [], "dsb": []}
        chunks = []

        def stack(index):
            return lambda: jnp.concatenate([kv[o, j, index, :BLK] for j in parts], axis=0)

        def end_later(made, h):
            state["p"].append(made[0])
            state["ds"].append(made[1])
            if h == 1:
                p = jnp.concatenate(state["p"], axis=1)
                ds = jnp.concatenate(state["ds"], axis=1)
                state["dv"] = dot(p, qn[i, 1, 1])
                state["dk"] = dot(ds, qn[i, 1, 0])
                state["dq"] = dot(jnp.concatenate([kt[o, j, :, :BLK] for j in parts], axis=1), ds)

        for h in range(2):
            chunks.append(
                chunk(
                    *halves(i, 1, h), row(i, 1, 0, h), row(i, 1, 1, h), stack(0), stack(1),
                    functools.partial(end_later, h=h),
                )
            )

        weights = []
        for n, j in enumerate(parts):
            query_first, key_first = first_block(i, o, j)
            later = query_first < key_first
            slot = later.astype(jnp.int32)
            weight = later.astype(F32)
            weights.append(weight)

            def pick(index, later=later, j=j):
                return lambda: lax.select(later, kv[o, j, index, BLK:], kv[o, j, index, :BLK])

            def end_same(made, n=n, j=j, slot=slot, weight=weight, later=later):
                p, ds = made
                dv, dk = dot(p, qn[i, slot, 1]), dot(ds, qn[i, slot, 0])
                rows = slice(n * BLK, n * BLK + BLK)
                late_dk, late_dv = weight * dk, weight * dv
                dka[o, j, 0, :BLK] += state["dk"][rows] + (dk - late_dk)
                dka[o, j, 1, :BLK] += state["dv"][rows] + (dv - late_dv)
                dka[o, j, 0, BLK:] += late_dk
                dka[o, j, 1, BLK:] += late_dv
                state["dsb"].append(ds)
                if n == len(parts) - 1:
                    turned = []
                    for m, (jm, wm) in enumerate(zip(parts, weights)):
                        late = kt[o, jm, :, BLK:] * wm.astype(BF16)
                        early = kt[o, jm, :, :BLK] * (1.0 - wm).astype(BF16)
                        turned.append(jnp.concatenate([late, early], axis=0))
                    both = dot(jnp.concatenate(turned, axis=1), jnp.concatenate(state["dsb"], axis=0))
                    dqa[i, 1] += state["dq"] + both[:BLK]
                    dqa[i, 0] += both[BLK:]

            chunks.append(
                chunk(
                    lambda slot=slot: qt[i, slot, 0], lambda slot=slot: qt[i, slot, 1],
                    lambda slot=slot: rw[i, slot, 0], lambda slot=slot: rw[i, slot, 1],
                    pick(0), pick(1), end_same,
                )
            )
        return chunks

    def whole(i, o, parts):
        hidden = []
        for j in parts:
            query_first, key_first = first_block(i, o, j)
            hidden.append(jnp.where(query_first > key_first, 0.0, 1e30).astype(F32))
        chunks = []

        def stack(index):
            return lambda: jnp.concatenate([kv[o, j, index] for j in parts], axis=0)

        for slot in range(2):
            state = {"p": [], "ds": []}
            for h in range(2):
                lse2 = row(i, slot, 0, h)

                def penalised(lse2=lse2):
                    return jnp.concatenate([jnp.broadcast_to(lse2() + up, (TOK, TOK)) for up in hidden], axis=0)

                def end(made, slot=slot, h=h, state=state):
                    state["p"].append(made[0])
                    state["ds"].append(made[1])
                    cut = slice(h * TOK, h * TOK + TOK)
                    dqa[i, slot, :, cut] += dot(jnp.concatenate([kt[o, j] for j in parts], axis=1), made[1])
                    if h == 1:
                        dv = dot(jnp.concatenate(state["p"], axis=1), qn[i, slot, 1])
                        dk = dot(jnp.concatenate(state["ds"], axis=1), qn[i, slot, 0])
                        for n, j in enumerate(parts):
                            dka[o, j, 0] += dk[n * TOK : n * TOK + TOK]
                            dka[o, j, 1] += dv[n * TOK : n * TOK + TOK]

                chunks.append(chunk(*halves(i, slot, h), penalised, row(i, slot, 1, h), stack(0), stack(1), end))
        return chunks

    step = folded if fold else whole

    def work(*steps):
        pipelined([c for i, o, parts in steps for c in step(i, o, parts)])

    pipelined(own_chunks())

    arrive(across)
    begin(up_kv[0][1], down_kv[0][1])
    kt[0, 1] = kv[0, 1, 0].T
    work((OWN, 0, (1,)))

    table = [
        (OWN, 1, OWN, 7), (OWN, 2, OWN, 6),
        (LEFT, 1, RIGHT, 1), (LEFT, 7, RIGHT, 7), (LEFT, 2, RIGHT, 2), (LEFT, 6, RIGHT, 6),
        (OWN, 4, LEFT, 4), (RIGHT, 4, OPP, 4), (OWN, 3, LEFT, 3), (RIGHT, 3, OPP, 3), (OWN, 5, LEFT, 5), (RIGHT, 5, OPP, 5),
        (OPP, 2, OPP, 6), (OPP, 1, OPP, 7), (OPP, 0, LEFT, 0),
    ]

    def before(t):
        @pl.when(t == 0)
        def _():
            arrive(*up_kv[0], *down_kv[0])
            begin(*up_kv[1], *down_kv[1])
            turn_keys(1)
            turn_keys(7)

        @pl.when(t == 1)
        def _():
            arrive(*up_kv[1], *down_kv[1])
            begin(*up_kv[2], *down_kv[2])
            turn_keys(2)
            turn_keys(6)

        @pl.when(t == 2)
        def _():
            arrive(to_right[0], to_right[2], to_left[1], to_left[2])
            begin(*far_right, *far_left)
            arrive(to_right[1], to_left[0])
            turn_queries(LEFT, from_left, rows_left)
            turn_queries(RIGHT, from_right, rows_right)

        @pl.when(t == 4)
        def _():
            arrive(*up_kv[2], *down_kv[2])
            begin(*up_kv[3], *down_kv[3])
            turn_keys(3)
            turn_keys(5)

        @pl.when(t == 6)
        def _():
            arrive(*far_right, *far_left)
            turn_queries(OPP, from_opp, rows_opp)
            arrive(*up_kv[3], *down_kv[3])
            turn_keys(4)

    def after(t):
        @pl.when(t == 7)
        def _():
            ktx[4] = dka[4].astype(BF16)
            begin(up_sum[4], down_sum[4])

        @pl.when(t == 9)
        def _():
            ktx[3, 1] = dka[3, 1].astype(BF16)
            arrive(up_sum[4])
            ktx[3, 0] = (dka[3, 0] + kup[3, 0].astype(F32)).astype(BF16)
            begin(up_sum[3])

        @pl.when(t == 11)
        def _():
            ktx[5, 0] = dka[5, 0].astype(BF16)
            arrive(down_sum[4])
            ktx[5, 1] = (dka[5, 1] + kdn[3, 1].astype(F32)).astype(BF16)
            begin(down_sum[3])

        for hop in (2, 1):
            @pl.when(t == 14 - hop)
            def _():
                arrive(up_sum[hop + 1])
                ktx[hop] = (dka[hop] + kup[hop].astype(F32)).astype(BF16)
                begin(up_sum[hop])
                arrive(down_sum[hop + 1])
                ktx[8 - hop] = (dka[8 - hop] + kdn[hop].astype(F32)).astype(BF16)
                begin(down_sum[hop])

        @pl.when(t == 14)
        def _():
            qtx[OPP] = dqa[OPP].astype(BF16)
            begin(*opp_sum)

    def both(t, carry):
        packed = jnp.int32(0)
        for n, (ia, oa, ib, ob) in enumerate(table):
            packed = jnp.where(t == n, jnp.int32(ia + 4 * oa + 32 * ib + 128 * ob), packed)
        pl.when(t < 7)(lambda: before(t))
        work(
            (packed % 4, packed // 4 % 8, (0, 1)),
            (packed // 32 % 4, packed // 128, (0, 1)),
        )
        pl.when(t > 6)(lambda: after(t))
        return carry

    lax.fori_loop(0, len(table), both, jnp.int32(0))
    work((RIGHT, 0, (0, 1)))

    qtx[RIGHT, 1] = dqa[RIGHT, 1].astype(BF16)
    qtx[LEFT, 0] = dqa[LEFT, 0].astype(BF16)
    begin(right_sum[0], left_sum[0])
    arrive(*opp_sum)
    qtx[RIGHT, 0] = (dqa[RIGHT, 0] + orx[0].astype(F32)).astype(BF16)
    qtx[LEFT, 1] = (dqa[LEFT, 1] + orx[1].astype(F32)).astype(BF16)
    begin(right_sum[1], left_sum[1])
    arrive(up_sum[1], down_sum[1])
    ytx[...] = (dka[0, 1] + kup[0, 1].astype(F32) + kdn[0, 1].astype(F32)).astype(BF16)
    begin(across_sum)
    total = dka[0, 0] + kup[0, 0].astype(F32) + kdn[0, 0].astype(F32)
    arrive(across_sum)
    total = total + yrx[...].astype(F32)
    dk_out[...] = total[0] * SCALE
    dv_out[...] = total[1]
    for j, (a, b) in enumerate(((1, 0), (0, 1))):
        arrive(right_sum[a], left_sum[b])
        dq = dqa[OWN, j] + qrx[0, j].astype(F32) + qrx[1, j].astype(F32)
        dq_out[j] = dq.T * SCALE

    for copy in to_right + to_left + far_right + far_left + [across, across_sum]:
        copy.wait_send()
    for group in up_kv + down_kv:
        for copy in group:
            copy.wait_send()
    for copy in list(up_sum.values()) + list(down_sum.values()) + opp_sum + right_sum + left_sum:
        copy.wait_send()


N_COPIES = 3 + 3 + 2 + 2 + 1 + 5 + 5 + 4 + 4 + 1 + 2 + 2 + 2


def grads(fold, order, q, do, out, lse, k, v):
    smem = pl.BlockSpec(memory_space=pltpu.SMEM)
    vmem = pl.BlockSpec(memory_space=pltpu.VMEM)
    landing = [pltpu.VMEM((2, 2, ROWS, BLK), BF16)] * 3 + [pltpu.VMEM((2, 2, 1, ROWS), F32)] * 3
    queries = [
        pltpu.VMEM((4, 2, 2, ROWS, BLK), BF16),
        pltpu.VMEM((4, 2, 2, BLK, ROWS), BF16),
        pltpu.VMEM((4, 2, 2, 1, ROWS), F32),
    ]
    return pl.pallas_call(
        functools.partial(kernel, fold),
        out_shape=(
            jax.ShapeDtypeStruct((2, ROWS, BLK), F32),
            jax.ShapeDtypeStruct((TOK, BLK), F32),
            jax.ShapeDtypeStruct((TOK, BLK), F32),
        ),
        in_specs=[smem] + [vmem] * 6,
        out_specs=(vmem, vmem, vmem),
        scratch_shapes=landing + queries + [
            pltpu.VMEM((NZ, NY, 2, TOK, BLK), BF16),
            pltpu.VMEM((NZ, NY, BLK, TOK), BF16),
            pltpu.VMEM((4, 2, BLK, ROWS), F32),
            pltpu.VMEM((NZ, NY, 2, TOK, BLK), F32),
            pltpu.VMEM((NZ, NY, 2, TOK, BLK), BF16),
            pltpu.VMEM((4, NY, 2, TOK, BLK), BF16),
            pltpu.VMEM((4, NY, 2, TOK, BLK), BF16),
            pltpu.VMEM((2, TOK, BLK), BF16),
            pltpu.VMEM((2, TOK, BLK), BF16),
            pltpu.VMEM((4, 2, BLK, ROWS), BF16),
            pltpu.VMEM((2, 2, BLK, ROWS), BF16),
            pltpu.VMEM((2, BLK, ROWS), BF16),
            pltpu.SemaphoreType.DMA((N_COPIES,)),
            pltpu.SemaphoreType.DMA((N_COPIES,)),
        ],
        compiler_params=pltpu.CompilerParams(
            collective_id=0 if fold else 1, has_side_effects=True, vmem_limit_bytes=48 * 1024 * 1024
        ),
        name="folded" if fold else "whole",
    )(order, q, do, out, lse, k, v)


def per_device(query, key_proj, value, output, lse, d_output, block_order):
    args = (
        block_order,
        query.reshape(2, ROWS, BLK),
        d_output.reshape(2, ROWS, BLK),
        output.reshape(2, ROWS, BLK),
        lse.T,
        key_proj.reshape(TOK, BLK),
        value.reshape(TOK, BLK),
    )
    is_folded = block_order[0] + block_order[1] == 2 * NX * NY * NZ - 1
    dq, dk, dv = lax.cond(is_folded, functools.partial(grads, True), functools.partial(grads, False), *args)
    return dq.reshape(query.shape), dk.reshape(key_proj.shape), dv.reshape(value.shape)


def solution(mesh):
    in_specs = (
        P("ctx", "head", None),
        P("ctx", "head", None),
        P("ctx", "head", None),
        P("ctx", "head", None),
        P("ctx", "head"),
        P("ctx", "head", None),
        P(),
    )
    out_specs = (P("ctx", "head", None), P("ctx", "head", None), P("ctx", "head", None))
    return jax.shard_map(
        per_device, mesh=mesh, in_specs=in_specs, out_specs=out_specs, check_vma=False
    )
```

```python
import functools

import jax
import jax.numpy as jnp
from jax import lax
from jax.experimental import pallas as pl
from jax.experimental.pallas import tpu as pltpu
from jax.sharding import PartitionSpec as P

MESH = pl.DeviceIdType.MESH
LOG2E = 1.4426950408889634
F32 = jnp.float32
BF16 = jnp.bfloat16
BLK = 128
TOK = 256
ROWS = 512
SCALE = BLK ** (-0.5)
NX, NY, NZ = 4, 2, 8
OWN, RIGHT, OPP, LEFT = range(4)


def dot(a, b):
    return lax.dot_general(a, b, (((1,), (0,)), ((), ())), preferred_element_type=F32)


def pipelined(chunks):
    made = chunks[0][1](*chunks[0][0]())
    for n, (_, _, end) in enumerate(chunks):
        following = None
        if n + 1 < len(chunks):
            following = chunks[n + 1][1](*chunks[n + 1][0]())
        end(made)
        made = following


def chunk(qt, dot_t, lse2, delta, k, v, end, keep=None):
    def first():
        return dot(k(), qt()), dot(v(), dot_t())

    def middle(s, dp):
        e = s * (SCALE * LOG2E) - lse2()
        if keep is not None:
            e = jnp.where(keep, e, -jnp.inf)
        p = jnp.exp2(e)
        return p.astype(BF16), (p * (dp - delta())).astype(BF16)

    return first, middle, end


def kernel(
    fold, order, q_in, do_in, out_in, lse_in, k_in, v_in, dq_out, dk_out, dv_out,
    from_right, from_opp, from_left, rows_right, rows_opp, rows_left, qn, qt, rw,
    kv, kt, dqa, dka, ktx, kup, kdn, ytx, yrx, qtx, qrx, orx, out_own, lse_own, ssem, rsem, osem,
):
    ctx = lax.axis_index("ctx")
    x, plane = ctx // (NY * NZ), ctx % (NY * NZ)
    y, z = plane // NZ, plane % NZ
    right = (x + 1) % NX * (NY * NZ) + plane
    left = (x + NX - 1) % NX * (NY * NZ) + plane
    partner = x * (NY * NZ) + (1 - y) * NZ + z
    up = ctx - z + (z + 1) % NZ
    down = ctx - z + (z + NZ - 1) % NZ
    used = []

    def send(src, dst, device):
        index = len(used)
        used.append(index)
        copy = pltpu.make_async_remote_copy(
            src_ref=src, dst_ref=dst, send_sem=ssem.at[index], recv_sem=rsem.at[index],
            device_id={"ctx": device}, device_id_type=MESH,
        )
        return copy

    def begin(*copies):
        for copy in copies:
            copy.start()

    def arrive(*copies):
        for copy in copies:
            copy.wait_recv()

    to_right = [send(qn.at[OWN, j], from_left.at[j], right) for j in range(2)]
    to_right += [send(rw.at[OWN], rows_left, right)]
    to_left = [send(qn.at[OWN, j], from_right.at[j], left) for j in range(2)]
    to_left += [send(rw.at[OWN], rows_right, left)]
    far_right = [send(from_left.at[0], from_opp.at[0], right), send(rows_left.at[0], rows_opp.at[0], right)]
    far_left = [send(from_right.at[1], from_opp.at[1], left), send(rows_right.at[1], rows_opp.at[1], left)]
    across = send(kv.at[0, 0], kv.at[0, 1], partner)
    up_kv = [[send(kv.at[-s % NZ, j], kv.at[7 - s, j], up) for j in range(2)] for s in range(3)]
    up_kv += [[send(kv.at[5, 0], kv.at[4, 0], up)]]
    down_kv = [[send(kv.at[s, j], kv.at[s + 1, j], down) for j in range(2)] for s in range(3)]
    down_kv += [[send(kv.at[3, 1], kv.at[4, 1], down)]]
    up_sum = {4: [send(ktx.at[4, 0], kup.at[3, 0], up)]}
    up_sum.update({o: [send(ktx.at[o, j], kup.at[o - 1, j], up) for j in range(2)] for o in (3, 2, 1)})
    down_sum = {4: [send(ktx.at[4, 1], kdn.at[3, 1], down)]}
    down_sum.update({o: [send(ktx.at[8 - o, j], kdn.at[o - 1, j], down) for j in range(2)] for o in (3, 2, 1)})
    across_sum = send(ytx, yrx, partner)
    opp_sum = [send(qtx.at[OPP, 0], orx.at[0], right), send(qtx.at[OPP, 1], orx.at[1], left)]
    right_sum = [send(qtx.at[RIGHT, j], qrx.at[0, j], right) for j in (1, 0)]
    left_sum = [send(qtx.at[LEFT, j], qrx.at[1, j], left) for j in (0, 1)]

    def lse_row(columns):
        shape = (BLK, ROWS)
        column = lax.broadcasted_iota(jnp.int32, shape, 1)
        spread = jnp.broadcast_to(columns[:, 0:1], shape)
        for head in range(1, 4):
            spread = jnp.where(column % 4 == head, jnp.broadcast_to(columns[:, head : head + 1], shape), spread)
        mine = column // 4 == lax.broadcasted_iota(jnp.int32, shape, 0)
        return jnp.sum(jnp.where(mine, spread, 0.0), axis=0, keepdims=True)

    barrier = pltpu.get_barrier_semaphore()
    for device in (right, left, partner, up, down):
        pl.semaphore_signal(barrier, inc=1, device_id={"ctx": device}, device_id_type=MESH)
    own = [
        (k_in, kv.at[0, 0, 0]), (v_in, kv.at[0, 0, 1]),
        (q_in.at[1], qn.at[OWN, 1, 0]), (do_in.at[1], qn.at[OWN, 1, 1]),
        (q_in.at[0], qn.at[OWN, 0, 0]), (do_in.at[0], qn.at[OWN, 0, 1]),
        (out_in, out_own), (lse_in, lse_own),
    ]
    own = [pltpu.make_async_copy(src, dst, osem.at[n]) for n, (src, dst) in enumerate(own)]
    begin(*own)
    own[0].wait()
    own[1].wait()
    pl.semaphore_wait(barrier, 5)
    begin(across, up_kv[0][0], down_kv[0][0])
    own[2].wait()
    own[3].wait()
    begin(to_left[1], to_right[1])
    own[4].wait()
    own[5].wait()
    begin(to_right[0], to_left[0])

    own[6].wait()
    own[7].wait()
    for j in range(2):
        product = qn[OWN, j, 1].astype(F32) * out_own[j].astype(F32)
        rw[OWN, j, 0] = lse_row(lse_own[:, j * BLK : j * BLK + BLK].T) * LOG2E
        rw[OWN, j, 1] = jnp.sum(product.T, axis=0, keepdims=True)
    begin(to_right[2], to_left[2])

    def turn_queries(i, landed, landed_rows):
        for j in range(2):
            for part in range(2):
                if landed is not None:
                    qn[i, j, part] = landed[j, part]
                    rw[i, j, part] = landed_rows[j, part]
                qt[i, j, part] = qn[i, j, part].T

    def turn_keys(o):
        for j in range(2):
            kt[o, j] = kv[o, j, 0].T

    turn_queries(OWN, None, None)
    kt[0, 0] = kv[0, 0, 0].T
    dqa[...] = jnp.zeros_like(dqa)
    dka[...] = jnp.zeros_like(dka)

    def halves(i, j, h):
        cut = slice(h * TOK, h * TOK + TOK)
        return (
            lambda: qt[i, j, 0, :, cut], lambda: qt[i, j, 1, :, cut],
        )

    def row(i, j, kind, h):
        return lambda: rw[i, j, kind, :, h * TOK : h * TOK + TOK]

    def own_chunks():
        chunks = []
        for j in range(2):
            keys = BLK * (j + 1)
            for h in range(2):
                shape = (keys, TOK)
                keep = lax.broadcasted_iota(jnp.int32, shape, 0) <= (
                    (lax.broadcasted_iota(jnp.int32, shape, 1) + h * TOK) // 4 + j * BLK
                )

                def end(made, j=j, h=h, keys=keys):
                    p, ds = made
                    cut = slice(h * TOK, h * TOK + TOK)
                    dqa[OWN, j, :, cut] += dot(kt[0, 0, :, :keys], ds)
                    dka[0, 0, 0, :keys] += dot(ds, qn[OWN, j, 0, cut])
                    dka[0, 0, 1, :keys] += dot(p, qn[OWN, j, 1, cut])

                chunks.append(
                    chunk(
                        *halves(OWN, j, h), row(OWN, j, 0, h), row(OWN, j, 1, h),
                        lambda keys=keys: kv[0, 0, 0, :keys], lambda keys=keys: kv[0, 0, 1, :keys], end, keep,
                    )
                )
        return chunks

    def first_block(i, o, j):
        owner = x * (NY * NZ) + (y + j) % NY * NZ + (z + o) % NZ
        return order[2 * ((x + i) % NX * (NY * NZ) + plane)], order[2 * owner]

    def folded(i, o, parts):
        size = BLK * len(parts)
        state = {"p": [], "ds": [], "dsb": []}
        chunks = []

        def stack(index):
            return lambda: jnp.concatenate([kv[o, j, index, :BLK] for j in parts], axis=0)

        def end_later(made, h):
            state["p"].append(made[0])
            state["ds"].append(made[1])
            if h == 1:
                p = jnp.concatenate(state["p"], axis=1)
                ds = jnp.concatenate(state["ds"], axis=1)
                state["dv"] = dot(p, qn[i, 1, 1])
                state["dk"] = dot(ds, qn[i, 1, 0])
                state["dq"] = dot(jnp.concatenate([kt[o, j, :, :BLK] for j in parts], axis=1), ds)

        for h in range(2):
            chunks.append(
                chunk(
                    *halves(i, 1, h), row(i, 1, 0, h), row(i, 1, 1, h), stack(0), stack(1),
                    functools.partial(end_later, h=h),
                )
            )

        weights = []
        for n, j in enumerate(parts):
            query_first, key_first = first_block(i, o, j)
            later = query_first < key_first
            slot = later.astype(jnp.int32)
            weight = later.astype(F32)
            weights.append(weight)

            def pick(index, later=later, j=j):
                return lambda: lax.select(later, kv[o, j, index, BLK:], kv[o, j, index, :BLK])

            def end_same(made, n=n, j=j, slot=slot, weight=weight, later=later):
                p, ds = made
                dv, dk = dot(p, qn[i, slot, 1]), dot(ds, qn[i, slot, 0])
                rows = slice(n * BLK, n * BLK + BLK)
                late_dk, late_dv = weight * dk, weight * dv
                dka[o, j, 0, :BLK] += state["dk"][rows] + (dk - late_dk)
                dka[o, j, 1, :BLK] += state["dv"][rows] + (dv - late_dv)
                dka[o, j, 0, BLK:] += late_dk
                dka[o, j, 1, BLK:] += late_dv
                state["dsb"].append(ds)
                if n == len(parts) - 1:
                    turned = []
                    for m, (jm, wm) in enumerate(zip(parts, weights)):
                        late = kt[o, jm, :, BLK:] * wm.astype(BF16)
                        early = kt[o, jm, :, :BLK] * (1.0 - wm).astype(BF16)
                        turned.append(jnp.concatenate([late, early], axis=0))
                    both = dot(jnp.concatenate(turned, axis=1), jnp.concatenate(state["dsb"], axis=0))
                    dqa[i, 1] += state["dq"] + both[:BLK]
                    dqa[i, 0] += both[BLK:]

            chunks.append(
                chunk(
                    lambda slot=slot: qt[i, slot, 0], lambda slot=slot: qt[i, slot, 1],
                    lambda slot=slot: rw[i, slot, 0], lambda slot=slot: rw[i, slot, 1],
                    pick(0), pick(1), end_same,
                )
            )
        return chunks

    def whole(i, o, parts):
        hidden = []
        for j in parts:
            query_first, key_first = first_block(i, o, j)
            hidden.append(jnp.where(query_first > key_first, 0.0, 1e30).astype(F32))
        chunks = []

        def stack(index):
            return lambda: jnp.concatenate([kv[o, j, index] for j in parts], axis=0)

        for slot in range(2):
            state = {"p": [], "ds": []}
            for h in range(2):
                lse2 = row(i, slot, 0, h)

                def penalised(lse2=lse2):
                    return jnp.concatenate([jnp.broadcast_to(lse2() + up, (TOK, TOK)) for up in hidden], axis=0)

                def end(made, slot=slot, h=h, state=state):
                    state["p"].append(made[0])
                    state["ds"].append(made[1])
                    cut = slice(h * TOK, h * TOK + TOK)
                    dqa[i, slot, :, cut] += dot(jnp.concatenate([kt[o, j] for j in parts], axis=1), made[1])
                    if h == 1:
                        dv = dot(jnp.concatenate(state["p"], axis=1), qn[i, slot, 1])
                        dk = dot(jnp.concatenate(state["ds"], axis=1), qn[i, slot, 0])
                        for n, j in enumerate(parts):
                            dka[o, j, 0] += dk[n * TOK : n * TOK + TOK]
                            dka[o, j, 1] += dv[n * TOK : n * TOK + TOK]

                chunks.append(chunk(*halves(i, slot, h), penalised, row(i, slot, 1, h), stack(0), stack(1), end))
        return chunks

    step = folded if fold else whole

    def work(*steps):
        pipelined([c for i, o, parts in steps for c in step(i, o, parts)])

    pipelined(own_chunks())

    arrive(across)
    begin(up_kv[0][1], down_kv[0][1])
    arrive(up_kv[0][0], down_kv[0][0])
    begin(up_kv[1][0], down_kv[1][0])
    kt[0, 1] = kv[0, 1, 0].T
    work((OWN, 0, (1,)))

    table = [
        (OWN, 1, OWN, 7), (OWN, 2, OWN, 6),
        (LEFT, 1, RIGHT, 1), (LEFT, 7, RIGHT, 7), (LEFT, 2, RIGHT, 2), (LEFT, 6, RIGHT, 6),
        (OWN, 4, LEFT, 4), (RIGHT, 4, OPP, 4), (OWN, 3, LEFT, 3), (RIGHT, 3, OPP, 3), (OWN, 5, LEFT, 5), (RIGHT, 5, OPP, 5),
        (OPP, 2, OPP, 6), (OPP, 1, OPP, 7), (OPP, 0, LEFT, 0),
    ]

    def before(t):
        @pl.when(t == 0)
        def _():
            arrive(up_kv[0][1], down_kv[0][1])
            begin(up_kv[1][1], down_kv[1][1])
            turn_keys(1)
            turn_keys(7)

        @pl.when(t == 1)
        def _():
            for j in range(2):
                arrive(up_kv[1][j], down_kv[1][j])
                begin(up_kv[2][j], down_kv[2][j])
            turn_keys(2)
            turn_keys(6)

        @pl.when(t == 2)
        def _():
            arrive(to_right[0], to_right[2], to_left[1], to_left[2])
            begin(*far_right, *far_left)
            arrive(to_right[1], to_left[0])
            turn_queries(LEFT, from_left, rows_left)
            turn_queries(RIGHT, from_right, rows_right)

        @pl.when(t == 4)
        def _():
            arrive(up_kv[2][0])
            begin(*up_kv[3])
            arrive(down_kv[2][0], down_kv[2][1])
            begin(*down_kv[3])
            arrive(up_kv[2][1])
            turn_keys(3)
            turn_keys(5)

        @pl.when(t == 6)
        def _():
            arrive(*far_right, *far_left)
            turn_queries(OPP, from_opp, rows_opp)
            arrive(*up_kv[3], *down_kv[3])
            turn_keys(4)

    def after(t):
        @pl.when(t == 7)
        def _():
            ktx[4] = dka[4].astype(BF16)
            begin(*up_sum[4], *down_sum[4])

        @pl.when(t == 9)
        def _():
            ktx[3, 1] = dka[3, 1].astype(BF16)
            begin(up_sum[3][1])
            arrive(*up_sum[4])
            ktx[3, 0] = (dka[3, 0] + kup[3, 0].astype(F32)).astype(BF16)
            begin(up_sum[3][0])

        @pl.when(t == 11)
        def _():
            ktx[5, 0] = dka[5, 0].astype(BF16)
            begin(down_sum[3][0])
            arrive(*down_sum[4])
            ktx[5, 1] = (dka[5, 1] + kdn[3, 1].astype(F32)).astype(BF16)
            begin(down_sum[3][1])

        for hop in (2, 1):
            @pl.when(t == 14 - hop)
            def _():
                for j in range(2):
                    arrive(up_sum[hop + 1][1 - j])
                    ktx[hop, 1 - j] = (dka[hop, 1 - j] + kup[hop, 1 - j].astype(F32)).astype(BF16)
                    begin(up_sum[hop][1 - j])
                    arrive(down_sum[hop + 1][j])
                    ktx[8 - hop, j] = (dka[8 - hop, j] + kdn[hop, j].astype(F32)).astype(BF16)
                    begin(down_sum[hop][j])

        @pl.when(t == 14)
        def _():
            qtx[OPP] = dqa[OPP].astype(BF16)
            begin(*opp_sum)

    def both(t, carry):
        packed = jnp.int32(0)
        for n, (ia, oa, ib, ob) in enumerate(table):
            packed = jnp.where(t == n, jnp.int32(ia + 4 * oa + 32 * ib + 128 * ob), packed)
        pl.when(t < 7)(lambda: before(t))
        work(
            (packed % 4, packed // 4 % 8, (0, 1)),
            (packed // 32 % 4, packed // 128, (0, 1)),
        )
        pl.when(t > 6)(lambda: after(t))
        return carry

    lax.fori_loop(0, len(table), both, jnp.int32(0))
    work((RIGHT, 0, (0, 1)))

    qtx[RIGHT, 1] = dqa[RIGHT, 1].astype(BF16)
    qtx[LEFT, 0] = dqa[LEFT, 0].astype(BF16)
    begin(right_sum[0], left_sum[0])
    arrive(*opp_sum)
    qtx[RIGHT, 0] = (dqa[RIGHT, 0] + orx[0].astype(F32)).astype(BF16)
    qtx[LEFT, 1] = (dqa[LEFT, 1] + orx[1].astype(F32)).astype(BF16)
    begin(right_sum[1], left_sum[1])
    arrive(up_sum[1][1], down_sum[1][1])
    ytx[...] = (dka[0, 1] + kup[0, 1].astype(F32) + kdn[0, 1].astype(F32)).astype(BF16)
    begin(across_sum)
    arrive(up_sum[1][0], down_sum[1][0])
    total = dka[0, 0] + kup[0, 0].astype(F32) + kdn[0, 0].astype(F32)
    arrive(across_sum)
    total = total + yrx[...].astype(F32)
    dk_out[...] = total[0] * SCALE
    dv_out[...] = total[1]
    for j, (a, b) in enumerate(((1, 0), (0, 1))):
        arrive(right_sum[a], left_sum[b])
        dq = dqa[OWN, j] + qrx[0, j].astype(F32) + qrx[1, j].astype(F32)
        dq_out[j] = dq.T * SCALE

    for copy in to_right + to_left + far_right + far_left + [across, across_sum]:
        copy.wait_send()
    for group in up_kv + down_kv + list(up_sum.values()) + list(down_sum.values()):
        for copy in group:
            copy.wait_send()
    for copy in opp_sum + right_sum + left_sum:
        copy.wait_send()


N_COPIES = 3 + 3 + 2 + 2 + 1 + 7 + 7 + 7 + 7 + 1 + 2 + 2 + 2


def grads(fold, order, q, do, out, lse, k, v):
    smem = pl.BlockSpec(memory_space=pltpu.SMEM)
    vmem = pl.BlockSpec(memory_space=pltpu.VMEM)
    landing = [pltpu.VMEM((2, 2, ROWS, BLK), BF16)] * 3 + [pltpu.VMEM((2, 2, 1, ROWS), F32)] * 3
    queries = [
        pltpu.VMEM((4, 2, 2, ROWS, BLK), BF16),
        pltpu.VMEM((4, 2, 2, BLK, ROWS), BF16),
        pltpu.VMEM((4, 2, 2, 1, ROWS), F32),
    ]
    return pl.pallas_call(
        functools.partial(kernel, fold),
        out_shape=(
            jax.ShapeDtypeStruct((2, ROWS, BLK), F32),
            jax.ShapeDtypeStruct((TOK, BLK), F32),
            jax.ShapeDtypeStruct((TOK, BLK), F32),
        ),
        in_specs=[smem] + [pl.BlockSpec(memory_space=pltpu.HBM)] * 6,
        out_specs=(vmem, vmem, vmem),
        scratch_shapes=landing + queries + [
            pltpu.VMEM((NZ, NY, 2, TOK, BLK), BF16),
            pltpu.VMEM((NZ, NY, BLK, TOK), BF16),
            pltpu.VMEM((4, 2, BLK, ROWS), F32),
            pltpu.VMEM((NZ, NY, 2, TOK, BLK), F32),
            pltpu.VMEM((NZ, NY, 2, TOK, BLK), BF16),
            pltpu.VMEM((4, NY, 2, TOK, BLK), BF16),
            pltpu.VMEM((4, NY, 2, TOK, BLK), BF16),
            pltpu.VMEM((2, TOK, BLK), BF16),
            pltpu.VMEM((2, TOK, BLK), BF16),
            pltpu.VMEM((4, 2, BLK, ROWS), BF16),
            pltpu.VMEM((2, 2, BLK, ROWS), BF16),
            pltpu.VMEM((2, BLK, ROWS), BF16),
            pltpu.VMEM((2, ROWS, BLK), BF16),
            pltpu.VMEM((4, TOK), F32),
            pltpu.SemaphoreType.DMA((N_COPIES,)),
            pltpu.SemaphoreType.DMA((N_COPIES,)),
            pltpu.SemaphoreType.DMA((8,)),
        ],
        compiler_params=pltpu.CompilerParams(
            collective_id=0 if fold else 1, has_side_effects=True, vmem_limit_bytes=48 * 1024 * 1024
        ),
        name="folded" if fold else "whole",
    )(order, q, do, out, lse, k, v)


def per_device(query, key_proj, value, output, lse, d_output, block_order):
    args = (
        block_order,
        query.reshape(2, ROWS, BLK),
        d_output.reshape(2, ROWS, BLK),
        output.reshape(2, ROWS, BLK),
        lse.T,
        key_proj.reshape(TOK, BLK),
        value.reshape(TOK, BLK),
    )
    is_folded = block_order[0] + block_order[1] == 2 * NX * NY * NZ - 1
    dq, dk, dv = lax.cond(is_folded, functools.partial(grads, True), functools.partial(grads, False), *args)
    return dq.reshape(query.shape), dk.reshape(key_proj.shape), dv.reshape(value.shape)


def solution(mesh):
    in_specs = (
        P("ctx", "head", None),
        P("ctx", "head", None),
        P("ctx", "head", None),
        P("ctx", "head", None),
        P("ctx", "head"),
        P("ctx", "head", None),
        P(),
    )
    out_specs = (P("ctx", "head", None), P("ctx", "head", None), P("ctx", "head", None))
    return jax.shard_map(
        per_device, mesh=mesh, in_specs=in_specs, out_specs=out_specs, check_vma=False
    )
```

```python
import functools

import jax
import jax.numpy as jnp
from jax import lax
from jax.experimental import pallas as pl
from jax.experimental.pallas import tpu as pltpu
from jax.sharding import PartitionSpec as P

MESH = pl.DeviceIdType.MESH
LOG2E = 1.4426950408889634
F32 = jnp.float32
BF16 = jnp.bfloat16
BLK = 128
TOK = 256
ROWS = 512
SCALE = BLK ** (-0.5)
NX, NY, NZ = 4, 2, 8
OWN, RIGHT, OPP, LEFT = range(4)


def dot(a, b):
    return lax.dot_general(a, b, (((1,), (0,)), ((), ())), preferred_element_type=F32)


def pipelined(chunks):
    made = chunks[0][1](*chunks[0][0]())
    for n, (_, _, end) in enumerate(chunks):
        following = None
        if n + 1 < len(chunks):
            following = chunks[n + 1][1](*chunks[n + 1][0]())
        end(made)
        made = following


def chunk(qt, dot_t, lse2, delta, k, v, end, keep=None):
    def first():
        return dot(k(), qt()), dot(v(), dot_t())

    def middle(s, dp):
        e = s * (SCALE * LOG2E) - lse2()
        if keep is not None:
            e = jnp.where(keep, e, -jnp.inf)
        p = jnp.exp2(e)
        return p.astype(BF16), (p * (dp - delta())).astype(BF16)

    return first, middle, end


def kernel(
    fold, order, q_in, do_in, out_in, lse_in, k_in, v_in, dq_out, dk_out, dv_out,
    from_right, from_opp, from_left, rows_right, rows_opp, rows_left, qn, qt, rw,
    kv, kt, dqa, dka, ktx, kup, kdn, vrx, yrx, qtx, qrx, orx, out_own, lse_own, ssem, rsem, osem,
):
    ctx = lax.axis_index("ctx")
    x, plane = ctx // (NY * NZ), ctx % (NY * NZ)
    y, z = plane // NZ, plane % NZ
    right = (x + 1) % NX * (NY * NZ) + plane
    left = (x + NX - 1) % NX * (NY * NZ) + plane
    partner = x * (NY * NZ) + (1 - y) * NZ + z
    up = ctx - z + (z + 1) % NZ
    down = ctx - z + (z + NZ - 1) % NZ
    used = []

    def send(src, dst, device):
        index = len(used)
        used.append(index)
        copy = pltpu.make_async_remote_copy(
            src_ref=src, dst_ref=dst, send_sem=ssem.at[index], recv_sem=rsem.at[index],
            device_id={"ctx": device}, device_id_type=MESH,
        )
        return copy

    def begin(*copies):
        for copy in copies:
            copy.start()

    def arrive(*copies):
        for copy in copies:
            copy.wait_recv()

    to_right = [send(qn.at[OWN, j], from_left.at[j], right) for j in range(2)]
    to_right += [send(rw.at[OWN], rows_left, right)]
    to_left = [send(qn.at[OWN, j], from_right.at[j], left) for j in range(2)]
    to_left += [send(rw.at[OWN], rows_right, left)]
    far_right = [send(from_left.at[0], from_opp.at[0], right), send(rows_left.at[0], rows_opp.at[0], right)]
    far_left = [send(from_right.at[1], from_opp.at[1], left), send(rows_right.at[1], rows_opp.at[1], left)]
    across = send(kv.at[0, 0], kv.at[0, 1], partner)
    values = {o: send(kv.at[o, 0, 1], kv.at[o, 1, 1], partner) for o in range(1, NZ)}
    up_kv = [
        [send(kv.at[-s % NZ, 0], kv.at[7 - s, 0], up), send(kv.at[-s % NZ, 1, 0], kv.at[7 - s, 1, 0], up)]
        for s in range(3)
    ]
    up_kv += [[send(kv.at[5, 0], kv.at[4, 0], up)]]
    down_kv = [
        [send(kv.at[s, 0], kv.at[s + 1, 0], down), send(kv.at[s, 1, 0], kv.at[s + 1, 1, 0], down)] for s in range(3)
    ]
    down_kv += [[send(kv.at[3, 1, 0], kv.at[4, 1, 0], down)]]
    up_mine = {o: send(ktx.at[o, 0], kup.at[o - 1, 0], up) for o in (4, 3, 2, 1)}
    up_other = {o: send(ktx.at[o, 1, 0], kup.at[o - 1, 1, 0], up) for o in (3, 2, 1)}
    down_mine = {o: send(ktx.at[NZ - o, 0], kdn.at[o - 1, 0], down) for o in (3, 2, 1)}
    down_other = {o: send(ktx.at[NZ - o, 1, 0], kdn.at[o - 1, 1, 0], down) for o in (4, 3, 2, 1)}
    value_sum = {o: send(ktx.at[o, 1, 1], vrx.at[o], partner) for o in range(NZ)}
    across_sum = send(ktx.at[0, 1, 0], yrx, partner)
    opp_sum = [send(qtx.at[OPP, 0], orx.at[0], right), send(qtx.at[OPP, 1], orx.at[1], left)]
    right_sum = [send(qtx.at[RIGHT, j], qrx.at[0, j], right) for j in (1, 0)]
    left_sum = [send(qtx.at[LEFT, j], qrx.at[1, j], left) for j in (0, 1)]

    def lse_row(columns):
        shape = (BLK, ROWS)
        column = lax.broadcasted_iota(jnp.int32, shape, 1)
        spread = jnp.broadcast_to(columns[:, 0:1], shape)
        for head in range(1, 4):
            spread = jnp.where(column % 4 == head, jnp.broadcast_to(columns[:, head : head + 1], shape), spread)
        mine = column // 4 == lax.broadcasted_iota(jnp.int32, shape, 0)
        return jnp.sum(jnp.where(mine, spread, 0.0), axis=0, keepdims=True)

    barrier = pltpu.get_barrier_semaphore()
    for device in (right, left, partner, up, down):
        pl.semaphore_signal(barrier, inc=1, device_id={"ctx": device}, device_id_type=MESH)
    own = [
        (k_in, kv.at[0, 0, 0]), (v_in, kv.at[0, 0, 1]),
        (q_in.at[1], qn.at[OWN, 1, 0]), (do_in.at[1], qn.at[OWN, 1, 1]),
        (q_in.at[0], qn.at[OWN, 0, 0]), (do_in.at[0], qn.at[OWN, 0, 1]),
        (out_in, out_own), (lse_in, lse_own),
    ]
    own = [pltpu.make_async_copy(src, dst, osem.at[n]) for n, (src, dst) in enumerate(own)]
    begin(*own)
    own[0].wait()
    own[1].wait()
    pl.semaphore_wait(barrier, 5)
    begin(across, up_kv[0][0], down_kv[0][0])
    own[2].wait()
    own[3].wait()
    begin(to_left[1], to_right[1])
    own[4].wait()
    own[5].wait()
    begin(to_right[0], to_left[0])

    own[6].wait()
    own[7].wait()
    for j in range(2):
        product = qn[OWN, j, 1].astype(F32) * out_own[j].astype(F32)
        rw[OWN, j, 0] = lse_row(lse_own[:, j * BLK : j * BLK + BLK].T) * LOG2E
        rw[OWN, j, 1] = jnp.sum(product.T, axis=0, keepdims=True)
    begin(to_right[2], to_left[2])

    def turn_queries(i, landed, landed_rows):
        for j in range(2):
            for part in range(2):
                if landed is not None:
                    qn[i, j, part] = landed[j, part]
                    rw[i, j, part] = landed_rows[j, part]
                qt[i, j, part] = qn[i, j, part].T

    def turn_keys(o):
        for j in range(2):
            kt[o, j] = kv[o, j, 0].T

    turn_queries(OWN, None, None)
    kt[0, 0] = kv[0, 0, 0].T
    dqa[...] = jnp.zeros_like(dqa)
    dka[...] = jnp.zeros_like(dka)

    def halves(i, j, h):
        cut = slice(h * TOK, h * TOK + TOK)
        return (
            lambda: qt[i, j, 0, :, cut], lambda: qt[i, j, 1, :, cut],
        )

    def row(i, j, kind, h):
        return lambda: rw[i, j, kind, :, h * TOK : h * TOK + TOK]

    def own_chunks():
        chunks = []
        for j in range(2):
            keys = BLK * (j + 1)
            for h in range(2):
                shape = (keys, TOK)
                keep = lax.broadcasted_iota(jnp.int32, shape, 0) <= (
                    (lax.broadcasted_iota(jnp.int32, shape, 1) + h * TOK) // 4 + j * BLK
                )

                def end(made, j=j, h=h, keys=keys):
                    p, ds = made
                    cut = slice(h * TOK, h * TOK + TOK)
                    dqa[OWN, j, :, cut] += dot(kt[0, 0, :, :keys], ds)
                    dka[0, 0, 0, :keys] += dot(ds, qn[OWN, j, 0, cut])
                    dka[0, 0, 1, :keys] += dot(p, qn[OWN, j, 1, cut])

                chunks.append(
                    chunk(
                        *halves(OWN, j, h), row(OWN, j, 0, h), row(OWN, j, 1, h),
                        lambda keys=keys: kv[0, 0, 0, :keys], lambda keys=keys: kv[0, 0, 1, :keys], end, keep,
                    )
                )
        return chunks

    def first_block(i, o, j):
        owner = x * (NY * NZ) + (y + j) % NY * NZ + (z + o) % NZ
        return order[2 * ((x + i) % NX * (NY * NZ) + plane)], order[2 * owner]

    def folded(i, o, parts):
        size = BLK * len(parts)
        state = {"p": [], "ds": [], "dsb": []}
        chunks = []

        def stack(index):
            return lambda: jnp.concatenate([kv[o, j, index, :BLK] for j in parts], axis=0)

        def end_later(made, h):
            state["p"].append(made[0])
            state["ds"].append(made[1])
            if h == 1:
                p = jnp.concatenate(state["p"], axis=1)
                ds = jnp.concatenate(state["ds"], axis=1)
                state["dv"] = dot(p, qn[i, 1, 1])
                state["dk"] = dot(ds, qn[i, 1, 0])
                state["dq"] = dot(jnp.concatenate([kt[o, j, :, :BLK] for j in parts], axis=1), ds)

        for h in range(2):
            chunks.append(
                chunk(
                    *halves(i, 1, h), row(i, 1, 0, h), row(i, 1, 1, h), stack(0), stack(1),
                    functools.partial(end_later, h=h),
                )
            )

        weights = []
        for n, j in enumerate(parts):
            query_first, key_first = first_block(i, o, j)
            later = query_first < key_first
            slot = later.astype(jnp.int32)
            weight = later.astype(F32)
            weights.append(weight)

            def pick(index, later=later, j=j):
                return lambda: lax.select(later, kv[o, j, index, BLK:], kv[o, j, index, :BLK])

            def end_same(made, n=n, j=j, slot=slot, weight=weight, later=later):
                p, ds = made
                dv, dk = dot(p, qn[i, slot, 1]), dot(ds, qn[i, slot, 0])
                rows = slice(n * BLK, n * BLK + BLK)
                late_dk, late_dv = weight * dk, weight * dv
                dka[o, j, 0, :BLK] += state["dk"][rows] + (dk - late_dk)
                dka[o, j, 1, :BLK] += state["dv"][rows] + (dv - late_dv)
                dka[o, j, 0, BLK:] += late_dk
                dka[o, j, 1, BLK:] += late_dv
                state["dsb"].append(ds)
                if n == len(parts) - 1:
                    turned = []
                    for m, (jm, wm) in enumerate(zip(parts, weights)):
                        late = kt[o, jm, :, BLK:] * wm.astype(BF16)
                        early = kt[o, jm, :, :BLK] * (1.0 - wm).astype(BF16)
                        turned.append(jnp.concatenate([late, early], axis=0))
                    both = dot(jnp.concatenate(turned, axis=1), jnp.concatenate(state["dsb"], axis=0))
                    dqa[i, 1] += state["dq"] + both[:BLK]
                    dqa[i, 0] += both[BLK:]

            chunks.append(
                chunk(
                    lambda slot=slot: qt[i, slot, 0], lambda slot=slot: qt[i, slot, 1],
                    lambda slot=slot: rw[i, slot, 0], lambda slot=slot: rw[i, slot, 1],
                    pick(0), pick(1), end_same,
                )
            )
        return chunks

    def whole(i, o, parts):
        hidden = []
        for j in parts:
            query_first, key_first = first_block(i, o, j)
            hidden.append(jnp.where(query_first > key_first, 0.0, 1e30).astype(F32))
        chunks = []

        def stack(index):
            return lambda: jnp.concatenate([kv[o, j, index] for j in parts], axis=0)

        for slot in range(2):
            state = {"p": [], "ds": []}
            for h in range(2):
                lse2 = row(i, slot, 0, h)

                def penalised(lse2=lse2):
                    return jnp.concatenate([jnp.broadcast_to(lse2() + up, (TOK, TOK)) for up in hidden], axis=0)

                def end(made, slot=slot, h=h, state=state):
                    state["p"].append(made[0])
                    state["ds"].append(made[1])
                    cut = slice(h * TOK, h * TOK + TOK)
                    dqa[i, slot, :, cut] += dot(jnp.concatenate([kt[o, j] for j in parts], axis=1), made[1])
                    if h == 1:
                        dv = dot(jnp.concatenate(state["p"], axis=1), qn[i, slot, 1])
                        dk = dot(jnp.concatenate(state["ds"], axis=1), qn[i, slot, 0])
                        for n, j in enumerate(parts):
                            dka[o, j, 0] += dk[n * TOK : n * TOK + TOK]
                            dka[o, j, 1] += dv[n * TOK : n * TOK + TOK]

                chunks.append(chunk(*halves(i, slot, h), penalised, row(i, slot, 1, h), stack(0), stack(1), end))
        return chunks

    step = folded if fold else whole

    def work(*steps):
        pipelined([c for i, o, parts in steps for c in step(i, o, parts)])

    pipelined(own_chunks())

    arrive(across)
    begin(up_kv[0][1], down_kv[0][1])
    arrive(up_kv[0][0], down_kv[0][0])
    begin(up_kv[1][0], down_kv[1][0], values[7], values[1])
    kt[0, 1] = kv[0, 1, 0].T
    work((OWN, 0, (1,)))

    table = [
        (OWN, 1, OWN, 7), (OWN, 2, OWN, 6),
        (LEFT, 1, RIGHT, 1), (LEFT, 7, RIGHT, 7), (LEFT, 2, RIGHT, 2), (LEFT, 6, RIGHT, 6),
        (OWN, 4, LEFT, 4), (RIGHT, 4, OPP, 4), (OWN, 3, LEFT, 3), (RIGHT, 3, OPP, 3), (OWN, 5, LEFT, 5), (RIGHT, 5, OPP, 5),
        (OPP, 2, OPP, 6), (OPP, 1, OPP, 7), (OPP, 0, LEFT, 0),
    ]

    def before(t):
        @pl.when(t == 0)
        def _():
            arrive(up_kv[0][1], down_kv[0][1])
            begin(up_kv[1][1], down_kv[1][1])
            turn_keys(1)
            turn_keys(7)
            arrive(values[7], values[1])

        @pl.when(t == 1)
        def _():
            arrive(up_kv[1][0], down_kv[1][0])
            begin(up_kv[2][0], down_kv[2][0], values[6], values[2])
            arrive(up_kv[1][1], down_kv[1][1])
            begin(up_kv[2][1], down_kv[2][1])
            turn_keys(2)
            turn_keys(6)
            arrive(values[6], values[2])

        @pl.when(t == 2)
        def _():
            arrive(to_right[0], to_right[2], to_left[1], to_left[2])
            begin(*far_right, *far_left)
            arrive(to_right[1], to_left[0])
            turn_queries(LEFT, from_left, rows_left)
            turn_queries(RIGHT, from_right, rows_right)

        @pl.when(t == 3)
        def _():
            arrive(up_kv[2][0])
            begin(up_kv[3][0], values[5])
            arrive(down_kv[2][0], down_kv[2][1])
            begin(down_kv[3][0], values[3])

        @pl.when(t == 4)
        def _():
            arrive(up_kv[2][1])
            turn_keys(3)
            turn_keys(5)

        @pl.when(t == 5)
        def _():
            arrive(up_kv[3][0])
            begin(values[4])

        @pl.when(t == 6)
        def _():
            arrive(*far_right, *far_left)
            turn_queries(OPP, from_opp, rows_opp)
            arrive(down_kv[3][0])
            turn_keys(4)
            arrive(values[3], values[5], values[4])

    def start_values(o):
        ktx[o, 1, 1] = dka[o, 1, 1].astype(BF16)
        begin(value_sum[o])

    def pass_other(o, out, inbound=None, landed=None):
        total = dka[o, 1, 0]
        if inbound is not None:
            arrive(inbound)
            total = total + landed[1, 0].astype(F32)
        ktx[o, 1, 0] = total.astype(BF16)
        begin(out)

    def pass_mine(o, out, inbound=None, landed=None):
        arrive(value_sum[o])
        dk, dv = dka[o, 0, 0], dka[o, 0, 1] + vrx[o].astype(F32)
        if inbound is not None:
            arrive(inbound)
            dk, dv = dk + landed[0, 0].astype(F32), dv + landed[0, 1].astype(F32)
        ktx[o, 0, 0] = dk.astype(BF16)
        ktx[o, 0, 1] = dv.astype(BF16)
        begin(out)

    def after(t):
        @pl.when(t == 7)
        def _():
            start_values(4)
            pass_other(4, down_other[4])

        @pl.when(t == 8)
        def _():
            pass_mine(4, up_mine[4])

        @pl.when(t == 9)
        def _():
            start_values(3)
            pass_other(3, up_other[3])

        @pl.when(t == 10)
        def _():
            pass_mine(3, up_mine[3], up_mine[4], kup.at[3])

        @pl.when(t == 11)
        def _():
            start_values(5)
            pass_other(5, down_other[3], down_other[4], kdn.at[3])

        @pl.when(t == 12)
        def _():
            start_values(2)
            start_values(6)
            pass_mine(5, down_mine[3])
            pass_other(2, up_other[2], up_other[3], kup.at[2])
            pass_other(6, down_other[2], down_other[3], kdn.at[2])

        @pl.when(t == 13)
        def _():
            start_values(1)
            start_values(7)
            pass_mine(2, up_mine[2], up_mine[3], kup.at[2])
            pass_other(1, up_other[1], up_other[2], kup.at[1])
            pass_other(7, down_other[1], down_other[2], kdn.at[1])
            pass_mine(6, down_mine[2], down_mine[3], kdn.at[2])

        @pl.when(t == 14)
        def _():
            qtx[OPP] = dqa[OPP].astype(BF16)
            begin(*opp_sum)
            pass_mine(1, up_mine[1], up_mine[2], kup.at[1])
            pass_mine(7, down_mine[1], down_mine[2], kdn.at[1])

    def both(t, carry):
        packed = jnp.int32(0)
        for n, (ia, oa, ib, ob) in enumerate(table):
            packed = jnp.where(t == n, jnp.int32(ia + 4 * oa + 32 * ib + 128 * ob), packed)
        pl.when(t < 7)(lambda: before(t))
        work(
            (packed % 4, packed // 4 % 8, (0, 1)),
            (packed // 32 % 4, packed // 128, (0, 1)),
        )
        pl.when(t > 6)(lambda: after(t))
        return carry

    lax.fori_loop(0, len(table), both, jnp.int32(0))
    work((RIGHT, 0, (0, 1)))

    qtx[RIGHT, 1] = dqa[RIGHT, 1].astype(BF16)
    qtx[LEFT, 0] = dqa[LEFT, 0].astype(BF16)
    begin(right_sum[0], left_sum[0])
    arrive(*opp_sum)
    qtx[RIGHT, 0] = (dqa[RIGHT, 0] + orx[0].astype(F32)).astype(BF16)
    qtx[LEFT, 1] = (dqa[LEFT, 1] + orx[1].astype(F32)).astype(BF16)
    begin(right_sum[1], left_sum[1])
    start_values(0)
    arrive(up_other[1], down_other[1])
    ktx[0, 1, 0] = (dka[0, 1, 0] + kup[0, 1, 0].astype(F32) + kdn[0, 1, 0].astype(F32)).astype(BF16)
    begin(across_sum)
    arrive(up_mine[1], down_mine[1])
    dk = dka[0, 0, 0] + kup[0, 0, 0].astype(F32) + kdn[0, 0, 0].astype(F32)
    dv = dka[0, 0, 1] + kup[0, 0, 1].astype(F32) + kdn[0, 0, 1].astype(F32)
    arrive(value_sum[0], across_sum)
    dk_out[...] = (dk + yrx[...].astype(F32)) * SCALE
    dv_out[...] = dv + vrx[0].astype(F32)
    for j, (a, b) in enumerate(((1, 0), (0, 1))):
        arrive(right_sum[a], left_sum[b])
        dq = dqa[OWN, j] + qrx[0, j].astype(F32) + qrx[1, j].astype(F32)
        dq_out[j] = dq.T * SCALE

    for copy in to_right + to_left + far_right + far_left + [across, across_sum]:
        copy.wait_send()
    for group in up_kv + down_kv:
        for copy in group:
            copy.wait_send()
    for group in (values, up_mine, up_other, down_mine, down_other, value_sum):
        for copy in group.values():
            copy.wait_send()
    for copy in opp_sum + right_sum + left_sum:
        copy.wait_send()


N_COPIES = 16 + 22 + 23


def grads(fold, order, q, do, out, lse, k, v):
    smem = pl.BlockSpec(memory_space=pltpu.SMEM)
    vmem = pl.BlockSpec(memory_space=pltpu.VMEM)
    landing = [pltpu.VMEM((2, 2, ROWS, BLK), BF16)] * 3 + [pltpu.VMEM((2, 2, 1, ROWS), F32)] * 3
    queries = [
        pltpu.VMEM((4, 2, 2, ROWS, BLK), BF16),
        pltpu.VMEM((4, 2, 2, BLK, ROWS), BF16),
        pltpu.VMEM((4, 2, 2, 1, ROWS), F32),
    ]
    return pl.pallas_call(
        functools.partial(kernel, fold),
        out_shape=(
            jax.ShapeDtypeStruct((2, ROWS, BLK), F32),
            jax.ShapeDtypeStruct((TOK, BLK), F32),
            jax.ShapeDtypeStruct((TOK, BLK), F32),
        ),
        in_specs=[smem] + [pl.BlockSpec(memory_space=pltpu.HBM)] * 6,
        out_specs=(vmem, vmem, vmem),
        scratch_shapes=landing + queries + [
            pltpu.VMEM((NZ, NY, 2, TOK, BLK), BF16),
            pltpu.VMEM((NZ, NY, BLK, TOK), BF16),
            pltpu.VMEM((4, 2, BLK, ROWS), F32),
            pltpu.VMEM((NZ, NY, 2, TOK, BLK), F32),
            pltpu.VMEM((NZ, NY, 2, TOK, BLK), BF16),
            pltpu.VMEM((4, NY, 2, TOK, BLK), BF16),
            pltpu.VMEM((4, NY, 2, TOK, BLK), BF16),
            pltpu.VMEM((NZ, TOK, BLK), BF16),
            pltpu.VMEM((TOK, BLK), BF16),
            pltpu.VMEM((4, 2, BLK, ROWS), BF16),
            pltpu.VMEM((2, 2, BLK, ROWS), BF16),
            pltpu.VMEM((2, BLK, ROWS), BF16),
            pltpu.VMEM((2, ROWS, BLK), BF16),
            pltpu.VMEM((4, TOK), F32),
            pltpu.SemaphoreType.DMA((N_COPIES,)),
            pltpu.SemaphoreType.DMA((N_COPIES,)),
            pltpu.SemaphoreType.DMA((8,)),
        ],
        compiler_params=pltpu.CompilerParams(
            collective_id=0 if fold else 1, has_side_effects=True, vmem_limit_bytes=48 * 1024 * 1024
        ),
        name="folded" if fold else "whole",
    )(order, q, do, out, lse, k, v)


def per_device(query, key_proj, value, output, lse, d_output, block_order):
    args = (
        block_order,
        query.reshape(2, ROWS, BLK),
        d_output.reshape(2, ROWS, BLK),
        output.reshape(2, ROWS, BLK),
        lse.T,
        key_proj.reshape(TOK, BLK),
        value.reshape(TOK, BLK),
    )
    is_folded = block_order[0] + block_order[1] == 2 * NX * NY * NZ - 1
    dq, dk, dv = lax.cond(is_folded, functools.partial(grads, True), functools.partial(grads, False), *args)
    return dq.reshape(query.shape), dk.reshape(key_proj.shape), dv.reshape(value.shape)


def solution(mesh):
    in_specs = (
        P("ctx", "head", None),
        P("ctx", "head", None),
        P("ctx", "head", None),
        P("ctx", "head", None),
        P("ctx", "head"),
        P("ctx", "head", None),
        P(),
    )
    out_specs = (P("ctx", "head", None), P("ctx", "head", None), P("ctx", "head", None))
    return jax.shard_map(
        per_device, mesh=mesh, in_specs=in_specs, out_specs=out_specs, check_vma=False
    )
```

```python
import functools

import jax
import jax.numpy as jnp
from jax import lax
from jax.experimental import pallas as pl
from jax.experimental.pallas import tpu as pltpu
from jax.sharding import PartitionSpec as P

MESH = pl.DeviceIdType.MESH
LOG2E = 1.4426950408889634
F32 = jnp.float32
BF16 = jnp.bfloat16
BLK = 128
TOK = 256
ROWS = 512
SCALE = BLK ** (-0.5)
NX, NY, NZ = 4, 2, 8
OWN, RIGHT, OPP, LEFT = range(4)


def dot(a, b):
    return lax.dot_general(a, b, (((1,), (0,)), ((), ())), preferred_element_type=F32)


def pipelined(chunks):
    made = chunks[0][1](*chunks[0][0]())
    for n, (_, _, end) in enumerate(chunks):
        following = None
        if n + 1 < len(chunks):
            following = chunks[n + 1][1](*chunks[n + 1][0]())
        end(made)
        made = following


def chunk(qt, dot_t, lse2, delta, k, v, end, keep=None):
    def first():
        return dot(k(), qt()), dot(v(), dot_t())

    def middle(s, dp):
        e = s * (SCALE * LOG2E) - lse2()
        if keep is not None:
            e = jnp.where(keep, e, -jnp.inf)
        p = jnp.exp2(e)
        return p.astype(BF16), (p * (dp - delta())).astype(BF16)

    return first, middle, end


def kernel(
    fold, order, q_in, do_in, out_in, lse_in, k_in, v_in, dq_out, dk_out, dv_out,
    from_right, from_opp, from_left, rows_right, rows_opp, rows_left, qn, qt, rw,
    kv, kt, dqa, dka, ktx, kup, kdn, vrx, yrx, qtx, qrx, orx, out_own, lse_own, ssem, rsem, osem,
):
    ctx = lax.axis_index("ctx")
    x, plane = ctx // (NY * NZ), ctx % (NY * NZ)
    y, z = plane // NZ, plane % NZ
    right = (x + 1) % NX * (NY * NZ) + plane
    left = (x + NX - 1) % NX * (NY * NZ) + plane
    partner = x * (NY * NZ) + (1 - y) * NZ + z
    up = ctx - z + (z + 1) % NZ
    down = ctx - z + (z + NZ - 1) % NZ
    used = []

    def send(src, dst, device):
        index = len(used)
        used.append(index)
        copy = pltpu.make_async_remote_copy(
            src_ref=src, dst_ref=dst, send_sem=ssem.at[index], recv_sem=rsem.at[index],
            device_id={"ctx": device}, device_id_type=MESH,
        )
        return copy

    def begin(*copies):
        for copy in copies:
            copy.start()

    def arrive(*copies):
        for copy in copies:
            copy.wait_recv()

    to_right = [send(qn.at[OWN, j], from_left.at[j], right) for j in range(2)]
    to_right += [send(rw.at[OWN], rows_left, right)]
    to_left = [send(qn.at[OWN, j], from_right.at[j], left) for j in range(2)]
    to_left += [send(rw.at[OWN], rows_right, left)]
    far_right = [send(from_left.at[0], from_opp.at[0], right), send(rows_left.at[0], rows_opp.at[0], right)]
    far_left = [send(from_right.at[1], from_opp.at[1], left), send(rows_right.at[1], rows_opp.at[1], left)]
    across = send(kv.at[0, 0], kv.at[0, 1], partner)
    values = {o: send(kv.at[o, 0, 1], kv.at[o, 1, 1], partner) for o in range(1, NZ)}
    up_kv = [
        [send(kv.at[-s % NZ, 0], kv.at[7 - s, 0], up), send(kv.at[-s % NZ, 1, 0], kv.at[7 - s, 1, 0], up)]
        for s in range(3)
    ]
    up_kv += [[send(kv.at[5, 0], kv.at[4, 0], up)]]
    down_kv = [
        [send(kv.at[s, 0], kv.at[s + 1, 0], down), send(kv.at[s, 1, 0], kv.at[s + 1, 1, 0], down)] for s in range(3)
    ]
    down_kv += [[send(kv.at[3, 1, 0], kv.at[4, 1, 0], down)]]
    up_mine = {o: send(ktx.at[o, 0], kup.at[o - 1, 0], up) for o in (4, 3, 2, 1)}
    up_other = {o: send(ktx.at[o, 1, 0], kup.at[o - 1, 1, 0], up) for o in (3, 2, 1)}
    down_mine = {o: send(ktx.at[NZ - o, 0], kdn.at[o - 1, 0], down) for o in (3, 2, 1)}
    down_other = {o: send(ktx.at[NZ - o, 1, 0], kdn.at[o - 1, 1, 0], down) for o in (4, 3, 2, 1)}
    value_sum = {o: send(ktx.at[o, 1, 1], vrx.at[o], partner) for o in range(NZ)}
    across_sum = send(ktx.at[0, 1, 0], yrx, partner)
    opp_sum = [send(qtx.at[OPP, 0], orx.at[0], right), send(qtx.at[OPP, 1], orx.at[1], left)]
    right_sum = [send(qtx.at[RIGHT, j], qrx.at[0, j], right) for j in (1, 0)]
    left_sum = [send(qtx.at[LEFT, j], qrx.at[1, j], left) for j in (0, 1)]

    def lse_row(columns):
        shape = (BLK, ROWS)
        column = lax.broadcasted_iota(jnp.int32, shape, 1)
        spread = jnp.broadcast_to(columns[:, 0:1], shape)
        for head in range(1, 4):
            spread = jnp.where(column % 4 == head, jnp.broadcast_to(columns[:, head : head + 1], shape), spread)
        mine = column // 4 == lax.broadcasted_iota(jnp.int32, shape, 0)
        return jnp.sum(jnp.where(mine, spread, 0.0), axis=0, keepdims=True)

    barrier = pltpu.get_barrier_semaphore()
    for device in (right, left, partner, up, down):
        pl.semaphore_signal(barrier, inc=1, device_id={"ctx": device}, device_id_type=MESH)
    own = [
        (k_in, kv.at[0, 0, 0]), (v_in, kv.at[0, 0, 1]),
        (q_in.at[1], qn.at[OWN, 1, 0]), (do_in.at[1], qn.at[OWN, 1, 1]),
        (q_in.at[0], qn.at[OWN, 0, 0]), (do_in.at[0], qn.at[OWN, 0, 1]),
        (out_in, out_own), (lse_in, lse_own),
    ]
    own = [pltpu.make_async_copy(src, dst, osem.at[n]) for n, (src, dst) in enumerate(own)]
    begin(*own)
    own[0].wait()
    own[1].wait()
    pl.semaphore_wait(barrier, 5)
    begin(across, up_kv[0][0], down_kv[0][0])
    own[2].wait()
    own[3].wait()
    begin(to_left[1], to_right[1])
    own[4].wait()
    own[5].wait()
    begin(to_right[0], to_left[0])

    own[6].wait()
    own[7].wait()
    for j in range(2):
        product = qn[OWN, j, 1].astype(F32) * out_own[j].astype(F32)
        rw[OWN, j, 0] = lse_row(lse_own[:, j * BLK : j * BLK + BLK].T) * LOG2E
        rw[OWN, j, 1] = jnp.sum(product.T, axis=0, keepdims=True)
    begin(to_right[2], to_left[2])

    def turn_queries(i, landed, landed_rows):
        for j in range(2):
            for part in range(2):
                if landed is not None:
                    qn[i, j, part] = landed[j, part]
                    rw[i, j, part] = landed_rows[j, part]
                qt[i, j, part] = qn[i, j, part].T

    def turn_keys(o):
        for j in range(2):
            kt[o, j] = kv[o, j, 0].T

    turn_queries(OWN, None, None)
    kt[0, 0] = kv[0, 0, 0].T
    dqa[...] = jnp.zeros_like(dqa)
    dka[...] = jnp.zeros_like(dka)

    def halves(i, j, h):
        cut = slice(h * TOK, h * TOK + TOK)
        return (
            lambda: qt[i, j, 0, :, cut], lambda: qt[i, j, 1, :, cut],
        )

    def row(i, j, kind, h):
        return lambda: rw[i, j, kind, :, h * TOK : h * TOK + TOK]

    def own_chunks():
        chunks = []
        for j in range(2):
            keys = BLK * (j + 1)
            for h in range(2):
                shape = (keys, TOK)
                keep = lax.broadcasted_iota(jnp.int32, shape, 0) <= (
                    (lax.broadcasted_iota(jnp.int32, shape, 1) + h * TOK) // 4 + j * BLK
                )

                def end(made, j=j, h=h, keys=keys):
                    p, ds = made
                    cut = slice(h * TOK, h * TOK + TOK)
                    dqa[OWN, j, :, cut] += dot(kt[0, 0, :, :keys], ds)
                    dka[0, 0, 0, :keys] += dot(ds, qn[OWN, j, 0, cut])
                    dka[0, 0, 1, :keys] += dot(p, qn[OWN, j, 1, cut])

                chunks.append(
                    chunk(
                        *halves(OWN, j, h), row(OWN, j, 0, h), row(OWN, j, 1, h),
                        lambda keys=keys: kv[0, 0, 0, :keys], lambda keys=keys: kv[0, 0, 1, :keys], end, keep,
                    )
                )
        return chunks

    def first_block(i, o, j):
        owner = x * (NY * NZ) + (y + j) % NY * NZ + (z + o) % NZ
        return order[2 * ((x + i) % NX * (NY * NZ) + plane)], order[2 * owner]

    def folded(i, parts):
        state = {"p": [], "ds": [], "dsb": []}
        chunks = []

        def stack(index):
            return lambda: jnp.concatenate([kv[o, j, index, :BLK] for o, j in parts], axis=0)

        def end_later(made, h):
            state["p"].append(made[0])
            state["ds"].append(made[1])
            if h == 1:
                p = jnp.concatenate(state["p"], axis=1)
                ds = jnp.concatenate(state["ds"], axis=1)
                state["dv"] = dot(p, qn[i, 1, 1])
                state["dk"] = dot(ds, qn[i, 1, 0])
                state["dq"] = dot(jnp.concatenate([kt[o, j, :, :BLK] for o, j in parts], axis=1), ds)

        for h in range(2):
            chunks.append(
                chunk(
                    *halves(i, 1, h), row(i, 1, 0, h), row(i, 1, 1, h), stack(0), stack(1),
                    functools.partial(end_later, h=h),
                )
            )

        weights = []
        for n, (o, j) in enumerate(parts):
            query_first, key_first = first_block(i, o, j)
            later = query_first < key_first
            slot = later.astype(jnp.int32)
            weight = later.astype(F32)
            weights.append(weight)

            def pick(index, later=later, o=o, j=j):
                return lambda: lax.select(later, kv[o, j, index, BLK:], kv[o, j, index, :BLK])

            def end_same(made, n=n, o=o, j=j, slot=slot, weight=weight):
                p, ds = made
                dv, dk = dot(p, qn[i, slot, 1]), dot(ds, qn[i, slot, 0])
                rows = slice(n * BLK, n * BLK + BLK)
                late_dk, late_dv = weight * dk, weight * dv
                dka[o, j, 0, :BLK] += state["dk"][rows] + (dk - late_dk)
                dka[o, j, 1, :BLK] += state["dv"][rows] + (dv - late_dv)
                dka[o, j, 0, BLK:] += late_dk
                dka[o, j, 1, BLK:] += late_dv
                state["dsb"].append(ds)
                if n == len(parts) - 1:
                    turned = []
                    for (om, jm), wm in zip(parts, weights):
                        late = kt[om, jm, :, BLK:] * wm.astype(BF16)
                        early = kt[om, jm, :, :BLK] * (1.0 - wm).astype(BF16)
                        turned.append(jnp.concatenate([late, early], axis=0))
                    both = dot(jnp.concatenate(turned, axis=1), jnp.concatenate(state["dsb"], axis=0))
                    dqa[i, 1] += state["dq"] + both[:BLK]
                    dqa[i, 0] += both[BLK:]

            chunks.append(
                chunk(
                    lambda slot=slot: qt[i, slot, 0], lambda slot=slot: qt[i, slot, 1],
                    lambda slot=slot: rw[i, slot, 0], lambda slot=slot: rw[i, slot, 1],
                    pick(0), pick(1), end_same,
                )
            )
        return chunks

    def whole(i, parts):
        hidden = []
        for o, j in parts:
            query_first, key_first = first_block(i, o, j)
            hidden.append(jnp.where(query_first > key_first, 0.0, 1e30).astype(F32))
        chunks = []

        def stack(index):
            return lambda: jnp.concatenate([kv[o, j, index] for o, j in parts], axis=0)

        for slot in range(2):
            state = {"p": [], "ds": []}
            for h in range(2):
                lse2 = row(i, slot, 0, h)

                def penalised(lse2=lse2):
                    return jnp.concatenate([jnp.broadcast_to(lse2() + up, (TOK, TOK)) for up in hidden], axis=0)

                def end(made, slot=slot, h=h, state=state):
                    state["p"].append(made[0])
                    state["ds"].append(made[1])
                    cut = slice(h * TOK, h * TOK + TOK)
                    dqa[i, slot, :, cut] += dot(jnp.concatenate([kt[o, j] for o, j in parts], axis=1), made[1])
                    if h == 1:
                        dv = dot(jnp.concatenate(state["p"], axis=1), qn[i, slot, 1])
                        dk = dot(jnp.concatenate(state["ds"], axis=1), qn[i, slot, 0])
                        for n, (o, j) in enumerate(parts):
                            dka[o, j, 0] += dk[n * TOK : n * TOK + TOK]
                            dka[o, j, 1] += dv[n * TOK : n * TOK + TOK]

                chunks.append(chunk(*halves(i, slot, h), penalised, row(i, slot, 1, h), stack(0), stack(1), end))
        return chunks

    step = folded if fold else whole

    def work(*steps):
        pipelined([c for i, parts in steps for c in step(i, parts)])

    def both_y(o):
        return [(o, 0), (o, 1)]

    pipelined(own_chunks())

    arrive(across)
    begin(up_kv[0][1], down_kv[0][1])
    arrive(up_kv[0][0], down_kv[0][0])
    begin(up_kv[1][0], down_kv[1][0], values[7], values[1])
    kt[0, 1] = kv[0, 1, 0].T
    work((OWN, [(0, 1)]))

    def neighbours(j, carry):
        @pl.when(j == 1)
        def _():
            arrive(up_kv[0][1], down_kv[0][1])
            begin(up_kv[1][1], down_kv[1][1])
            arrive(values[7], values[1])

        for o in (1, 7):
            kt[o, j] = kv[o, j, 0].T
        work((OWN, [(1, j), (7, j)]))
        return carry

    lax.fori_loop(0, 2, neighbours, jnp.int32(0))

    table = [
        (OWN, 2), (LEFT, 1), (RIGHT, 1), (LEFT, 2), (RIGHT, 2),
        (OWN, 3), (LEFT, 3), (RIGHT, 3), (OPP, 3), (OPP, 2), (OPP, 1),
    ]

    def before(t):
        @pl.when(t == 0)
        def _():
            arrive(up_kv[1][0], down_kv[1][0])
            begin(up_kv[2][0], down_kv[2][0], values[6], values[2])
            arrive(up_kv[1][1], down_kv[1][1])
            begin(up_kv[2][1], down_kv[2][1])
            turn_keys(2)
            turn_keys(6)
            arrive(values[6], values[2])

        @pl.when(t == 1)
        def _():
            arrive(to_right[0], to_right[2], to_left[1], to_left[2])
            begin(*far_right, *far_left)
            arrive(to_right[1], to_left[0])
            turn_queries(LEFT, from_left, rows_left)
            turn_queries(RIGHT, from_right, rows_right)

        @pl.when(t == 2)
        def _():
            arrive(up_kv[2][0])
            begin(up_kv[3][0], values[5])
            arrive(down_kv[2][0], down_kv[2][1])
            begin(down_kv[3][0], values[3])

        @pl.when(t == 3)
        def _():
            arrive(up_kv[2][1])
            turn_keys(3)
            turn_keys(5)

        @pl.when(t == 4)
        def _():
            arrive(up_kv[3][0])
            begin(values[4])

        @pl.when(t == 5)
        def _():
            arrive(*far_right, *far_left)
            turn_queries(OPP, from_opp, rows_opp)
            arrive(down_kv[3][0])
            turn_keys(4)
            arrive(values[4])

            def farthest(n, carry):
                work((2 * n, both_y(4)), (2 * n + 1, both_y(4)))
                return carry

            lax.fori_loop(0, 2, farthest, jnp.int32(0))
            start_values(4)
            pass_other(4, down_other[4])
            arrive(values[3], values[5])

    def start_values(o):
        ktx[o, 1, 1] = dka[o, 1, 1].astype(BF16)
        begin(value_sum[o])

    def pass_other(o, out, inbound=None, landed=None):
        total = dka[o, 1, 0]
        if inbound is not None:
            arrive(inbound)
            total = total + landed[1, 0].astype(F32)
        ktx[o, 1, 0] = total.astype(BF16)
        begin(out)

    def pass_mine(o, out, inbound=None, landed=None):
        arrive(value_sum[o])
        dk, dv = dka[o, 0, 0], dka[o, 0, 1] + vrx[o].astype(F32)
        if inbound is not None:
            arrive(inbound)
            dk, dv = dk + landed[0, 0].astype(F32), dv + landed[0, 1].astype(F32)
        ktx[o, 0, 0] = dk.astype(BF16)
        ktx[o, 0, 1] = dv.astype(BF16)
        begin(out)

    def after(t):
        @pl.when(t == 5)
        def _():
            pass_mine(4, up_mine[4])

        @pl.when(t == 8)
        def _():
            start_values(3)
            start_values(5)
            pass_other(3, up_other[3])
            pass_other(5, down_other[3], down_other[4], kdn.at[3])

        @pl.when(t == 9)
        def _():
            start_values(2)
            start_values(6)
            pass_mine(3, up_mine[3], up_mine[4], kup.at[3])
            pass_mine(5, down_mine[3])
            pass_other(2, up_other[2], up_other[3], kup.at[2])
            pass_other(6, down_other[2], down_other[3], kdn.at[2])

        @pl.when(t == 10)
        def _():
            start_values(1)
            start_values(7)
            pass_mine(2, up_mine[2], up_mine[3], kup.at[2])
            pass_mine(6, down_mine[2], down_mine[3], kdn.at[2])
            pass_other(1, up_other[1], up_other[2], kup.at[1])
            pass_other(7, down_other[1], down_other[2], kdn.at[1])

    def both_ways(t, carry):
        packed = jnp.int32(0)
        for n, (i, distance) in enumerate(table):
            packed = jnp.where(t == n, jnp.int32(i + 4 * distance), packed)
        pl.when(t < 6)(lambda: before(t))
        distance = packed // 4
        work((packed % 4, both_y(distance) + both_y(NZ - distance)))
        pl.when(t > 4)(lambda: after(t))
        return carry

    lax.fori_loop(0, len(table), both_ways, jnp.int32(0))
    work((OPP, both_y(0)), (LEFT, both_y(0)))
    qtx[OPP] = dqa[OPP].astype(BF16)
    begin(*opp_sum)
    qtx[LEFT, 0] = dqa[LEFT, 0].astype(BF16)
    begin(left_sum[0])
    pass_mine(1, up_mine[1], up_mine[2], kup.at[1])
    pass_mine(7, down_mine[1], down_mine[2], kdn.at[1])
    work((RIGHT, both_y(0)))

    qtx[RIGHT, 1] = dqa[RIGHT, 1].astype(BF16)
    begin(right_sum[0])
    arrive(*opp_sum)
    qtx[RIGHT, 0] = (dqa[RIGHT, 0] + orx[0].astype(F32)).astype(BF16)
    qtx[LEFT, 1] = (dqa[LEFT, 1] + orx[1].astype(F32)).astype(BF16)
    begin(right_sum[1], left_sum[1])
    start_values(0)
    arrive(up_other[1], down_other[1])
    ktx[0, 1, 0] = (dka[0, 1, 0] + kup[0, 1, 0].astype(F32) + kdn[0, 1, 0].astype(F32)).astype(BF16)
    begin(across_sum)
    arrive(up_mine[1], down_mine[1])
    dk = dka[0, 0, 0] + kup[0, 0, 0].astype(F32) + kdn[0, 0, 0].astype(F32)
    dv = dka[0, 0, 1] + kup[0, 0, 1].astype(F32) + kdn[0, 0, 1].astype(F32)
    arrive(value_sum[0], across_sum)
    dk_out[...] = (dk + yrx[...].astype(F32)) * SCALE
    dv_out[...] = dv + vrx[0].astype(F32)
    for j, (a, b) in enumerate(((1, 0), (0, 1))):
        arrive(right_sum[a], left_sum[b])
        dq = dqa[OWN, j] + qrx[0, j].astype(F32) + qrx[1, j].astype(F32)
        dq_out[j] = dq.T * SCALE

    for copy in to_right + to_left + far_right + far_left + [across, across_sum]:
        copy.wait_send()
    for group in up_kv + down_kv:
        for copy in group:
            copy.wait_send()
    for group in (values, up_mine, up_other, down_mine, down_other, value_sum):
        for copy in group.values():
            copy.wait_send()
    for copy in opp_sum + right_sum + left_sum:
        copy.wait_send()


N_COPIES = 16 + 22 + 23


def grads(fold, order, q, do, out, lse, k, v):
    smem = pl.BlockSpec(memory_space=pltpu.SMEM)
    vmem = pl.BlockSpec(memory_space=pltpu.VMEM)
    landing = [pltpu.VMEM((2, 2, ROWS, BLK), BF16)] * 3 + [pltpu.VMEM((2, 2, 1, ROWS), F32)] * 3
    queries = [
        pltpu.VMEM((4, 2, 2, ROWS, BLK), BF16),
        pltpu.VMEM((4, 2, 2, BLK, ROWS), BF16),
        pltpu.VMEM((4, 2, 2, 1, ROWS), F32),
    ]
    return pl.pallas_call(
        functools.partial(kernel, fold),
        out_shape=(
            jax.ShapeDtypeStruct((2, ROWS, BLK), F32),
            jax.ShapeDtypeStruct((TOK, BLK), F32),
            jax.ShapeDtypeStruct((TOK, BLK), F32),
        ),
        in_specs=[smem] + [pl.BlockSpec(memory_space=pltpu.HBM)] * 6,
        out_specs=(vmem, vmem, vmem),
        scratch_shapes=landing + queries + [
            pltpu.VMEM((NZ, NY, 2, TOK, BLK), BF16),
            pltpu.VMEM((NZ, NY, BLK, TOK), BF16),
            pltpu.VMEM((4, 2, BLK, ROWS), F32),
            pltpu.VMEM((NZ, NY, 2, TOK, BLK), F32),
            pltpu.VMEM((NZ, NY, 2, TOK, BLK), BF16),
            pltpu.VMEM((4, NY, 2, TOK, BLK), BF16),
            pltpu.VMEM((4, NY, 2, TOK, BLK), BF16),
            pltpu.VMEM((NZ, TOK, BLK), BF16),
            pltpu.VMEM((TOK, BLK), BF16),
            pltpu.VMEM((4, 2, BLK, ROWS), BF16),
            pltpu.VMEM((2, 2, BLK, ROWS), BF16),
            pltpu.VMEM((2, BLK, ROWS), BF16),
            pltpu.VMEM((2, ROWS, BLK), BF16),
            pltpu.VMEM((4, TOK), F32),
            pltpu.SemaphoreType.DMA((N_COPIES,)),
            pltpu.SemaphoreType.DMA((N_COPIES,)),
            pltpu.SemaphoreType.DMA((8,)),
        ],
        compiler_params=pltpu.CompilerParams(
            collective_id=0 if fold else 1, has_side_effects=True, vmem_limit_bytes=48 * 1024 * 1024
        ),
        name="folded" if fold else "whole",
    )(order, q, do, out, lse, k, v)


def per_device(query, key_proj, value, output, lse, d_output, block_order):
    args = (
        block_order,
        query.reshape(2, ROWS, BLK),
        d_output.reshape(2, ROWS, BLK),
        output.reshape(2, ROWS, BLK),
        lse.T,
        key_proj.reshape(TOK, BLK),
        value.reshape(TOK, BLK),
    )
    is_folded = block_order[0] + block_order[1] == 2 * NX * NY * NZ - 1
    dq, dk, dv = lax.cond(is_folded, functools.partial(grads, True), functools.partial(grads, False), *args)
    return dq.reshape(query.shape), dk.reshape(key_proj.shape), dv.reshape(value.shape)


def solution(mesh):
    in_specs = (
        P("ctx", "head", None),
        P("ctx", "head", None),
        P("ctx", "head", None),
        P("ctx", "head", None),
        P("ctx", "head"),
        P("ctx", "head", None),
        P(),
    )
    out_specs = (P("ctx", "head", None), P("ctx", "head", None), P("ctx", "head", None))
    return jax.shard_map(
        per_device, mesh=mesh, in_specs=in_specs, out_specs=out_specs, check_vma=False
    )
```

```python
import functools

import jax
import jax.numpy as jnp
from jax import lax
from jax.experimental import pallas as pl
from jax.experimental.pallas import tpu as pltpu
from jax.sharding import PartitionSpec as P

MESH = pl.DeviceIdType.MESH
LOG2E = 1.4426950408889634
F32 = jnp.float32
BF16 = jnp.bfloat16
BLK = 128
TOK = 256
ROWS = 512
SCALE = BLK ** (-0.5)
NX, NY, NZ = 4, 2, 8
OWN, RIGHT, OPP, LEFT = range(4)


def dot(a, b):
    return lax.dot_general(a, b, (((1,), (0,)), ((), ())), preferred_element_type=F32)


def pipelined(chunks):
    made = chunks[0][1](*chunks[0][0]())
    for n, (_, _, end) in enumerate(chunks):
        following = None
        if n + 1 < len(chunks):
            following = chunks[n + 1][1](*chunks[n + 1][0]())
        end(made)
        made = following


def chunk(qt, dot_t, lse2, delta, k, v, end, keep=None):
    def first():
        return dot(k(), qt()), dot(v(), dot_t())

    def middle(s, dp):
        e = s * (SCALE * LOG2E) - lse2()
        if keep is not None:
            e = jnp.where(keep, e, -jnp.inf)
        p = jnp.exp2(e)
        return p.astype(BF16), (p * (dp - delta())).astype(BF16)

    return first, middle, end


def kernel(
    fold, order, q_in, do_in, out_in, lse_in, k_in, v_in, dq_out, dk_out, dv_out,
    from_right, from_opp, from_left, rows_right, rows_opp, rows_left, qn, qt, rw,
    kv, kt, dqa, dka, ktx, kup, kdn, vrx, yrx, qtx, qrx, orx, out_own, lse_own, ssem, rsem, osem,
):
    ctx = lax.axis_index("ctx")
    x, plane = ctx // (NY * NZ), ctx % (NY * NZ)
    y, z = plane // NZ, plane % NZ
    right = (x + 1) % NX * (NY * NZ) + plane
    left = (x + NX - 1) % NX * (NY * NZ) + plane
    partner = x * (NY * NZ) + (1 - y) * NZ + z
    up = ctx - z + (z + 1) % NZ
    down = ctx - z + (z + NZ - 1) % NZ
    used = []

    def send(src, dst, device):
        index = len(used)
        used.append(index)
        copy = pltpu.make_async_remote_copy(
            src_ref=src, dst_ref=dst, send_sem=ssem.at[index], recv_sem=rsem.at[index],
            device_id={"ctx": device}, device_id_type=MESH,
        )
        return copy

    def begin(*copies):
        for copy in copies:
            copy.start()

    def arrive(*copies):
        for copy in copies:
            copy.wait_recv()

    to_right = [send(qn.at[OWN, j], from_left.at[j], right) for j in range(2)]
    to_right += [send(rw.at[OWN], rows_left, right)]
    to_left = [send(qn.at[OWN, j], from_right.at[j], left) for j in range(2)]
    to_left += [send(rw.at[OWN], rows_right, left)]
    far_right = [send(from_left.at[0], from_opp.at[0], right), send(rows_left.at[0], rows_opp.at[0], right)]
    far_left = [send(from_right.at[1], from_opp.at[1], left), send(rows_right.at[1], rows_opp.at[1], left)]
    across = [send(k_in, kv.at[0, 1, 0], partner), send(v_in, kv.at[0, 1, 1], partner)]
    own_up = [send(k_in, kv.at[7, 0, 0], up), send(v_in, kv.at[7, 0, 1], up)]
    own_down = [send(k_in, kv.at[1, 0, 0], down), send(v_in, kv.at[1, 0, 1], down)]
    values = {o: send(kv.at[o, 0, 1], kv.at[o, 1, 1], partner) for o in range(1, NZ)}
    up_kv = [
        [
            send(kv.at[-s % NZ, 0], kv.at[7 - s, 0], up) if s else None,
            send(kv.at[-s % NZ, 1, 0], kv.at[7 - s, 1, 0], up),
        ]
        for s in range(3)
    ]
    up_kv += [[send(kv.at[5, 0], kv.at[4, 0], up)]]
    down_kv = [
        [
            send(kv.at[s, 0], kv.at[s + 1, 0], down) if s else None,
            send(kv.at[s, 1, 0], kv.at[s + 1, 1, 0], down),
        ]
        for s in range(3)
    ]
    down_kv += [[send(kv.at[3, 1, 0], kv.at[4, 1, 0], down)]]
    up_mine = {o: send(ktx.at[o, 0], kup.at[o - 1, 0], up) for o in (4, 3, 2, 1)}
    up_other = {o: send(ktx.at[o, 1, 0], kup.at[o - 1, 1, 0], up) for o in (3, 2, 1)}
    down_mine = {o: send(ktx.at[NZ - o, 0], kdn.at[o - 1, 0], down) for o in (3, 2, 1)}
    down_other = {o: send(ktx.at[NZ - o, 1, 0], kdn.at[o - 1, 1, 0], down) for o in (4, 3, 2, 1)}
    value_sum = {o: send(ktx.at[o, 1, 1], vrx.at[o], partner) for o in range(NZ)}
    across_sum = send(ktx.at[0, 1, 0], yrx, partner)
    opp_sum = [send(qtx.at[OPP, 0], orx.at[0], right), send(qtx.at[OPP, 1], orx.at[1], left)]
    right_sum = [send(qtx.at[RIGHT, j], qrx.at[0, j], right) for j in (1, 0)]
    left_sum = [send(qtx.at[LEFT, j], qrx.at[1, j], left) for j in (0, 1)]

    def lse_row(columns):
        shape = (BLK, ROWS)
        column = lax.broadcasted_iota(jnp.int32, shape, 1)
        spread = jnp.broadcast_to(columns[:, 0:1], shape)
        for head in range(1, 4):
            spread = jnp.where(column % 4 == head, jnp.broadcast_to(columns[:, head : head + 1], shape), spread)
        mine = column // 4 == lax.broadcasted_iota(jnp.int32, shape, 0)
        return jnp.sum(jnp.where(mine, spread, 0.0), axis=0, keepdims=True)

    barrier = pltpu.get_barrier_semaphore()
    for device in (right, left, partner, up, down):
        pl.semaphore_signal(barrier, inc=1, device_id={"ctx": device}, device_id_type=MESH)
    own = [
        (k_in, kv.at[0, 0, 0]), (v_in, kv.at[0, 0, 1]),
        (q_in.at[1], qn.at[OWN, 1, 0]), (do_in.at[1], qn.at[OWN, 1, 1]),
        (q_in.at[0], qn.at[OWN, 0, 0]), (do_in.at[0], qn.at[OWN, 0, 1]),
        (out_in, out_own), (lse_in, lse_own),
    ]
    own = [pltpu.make_async_copy(src, dst, osem.at[n]) for n, (src, dst) in enumerate(own)]
    begin(*own)
    pl.semaphore_wait(barrier, 5)
    begin(across[0], own_up[0], own_down[0], across[1], own_up[1], own_down[1])
    own[2].wait()
    own[3].wait()
    begin(to_left[1], to_right[1])
    own[4].wait()
    own[5].wait()
    begin(to_right[0], to_left[0])

    own[0].wait()
    own[1].wait()
    own[6].wait()
    own[7].wait()
    for j in range(2):
        product = qn[OWN, j, 1].astype(F32) * out_own[j].astype(F32)
        rw[OWN, j, 0] = lse_row(lse_own[:, j * BLK : j * BLK + BLK].T) * LOG2E
        rw[OWN, j, 1] = jnp.sum(product.T, axis=0, keepdims=True)
    begin(to_right[2], to_left[2])

    def turn_queries(i, landed, landed_rows):
        for j in range(2):
            for part in range(2):
                if landed is not None:
                    qn[i, j, part] = landed[j, part]
                    rw[i, j, part] = landed_rows[j, part]
                qt[i, j, part] = qn[i, j, part].T

    def turn_keys(o):
        for j in range(2):
            kt[o, j] = kv[o, j, 0].T

    turn_queries(OWN, None, None)
    kt[0, 0] = kv[0, 0, 0].T
    dqa[...] = jnp.zeros_like(dqa)
    dka[...] = jnp.zeros_like(dka)

    def halves(i, j, h):
        cut = slice(h * TOK, h * TOK + TOK)
        return (
            lambda: qt[i, j, 0, :, cut], lambda: qt[i, j, 1, :, cut],
        )

    def row(i, j, kind, h):
        return lambda: rw[i, j, kind, :, h * TOK : h * TOK + TOK]

    def own_chunks():
        chunks = []
        for j in range(2):
            keys = BLK * (j + 1)
            for h in range(2):
                shape = (keys, TOK)
                keep = lax.broadcasted_iota(jnp.int32, shape, 0) <= (
                    (lax.broadcasted_iota(jnp.int32, shape, 1) + h * TOK) // 4 + j * BLK
                )

                def end(made, j=j, h=h, keys=keys):
                    p, ds = made
                    cut = slice(h * TOK, h * TOK + TOK)
                    dqa[OWN, j, :, cut] += dot(kt[0, 0, :, :keys], ds)
                    dka[0, 0, 0, :keys] += dot(ds, qn[OWN, j, 0, cut])
                    dka[0, 0, 1, :keys] += dot(p, qn[OWN, j, 1, cut])

                chunks.append(
                    chunk(
                        *halves(OWN, j, h), row(OWN, j, 0, h), row(OWN, j, 1, h),
                        lambda keys=keys: kv[0, 0, 0, :keys], lambda keys=keys: kv[0, 0, 1, :keys], end, keep,
                    )
                )
        return chunks

    def first_block(i, o, j):
        owner = x * (NY * NZ) + (y + j) % NY * NZ + (z + o) % NZ
        return order[2 * ((x + i) % NX * (NY * NZ) + plane)], order[2 * owner]

    def folded(i, parts):
        state = {"p": [], "ds": [], "dsb": []}
        chunks = []

        def stack(index):
            return lambda: jnp.concatenate([kv[o, j, index, :BLK] for o, j in parts], axis=0)

        def end_later(made, h):
            state["p"].append(made[0])
            state["ds"].append(made[1])
            if h == 1:
                p = jnp.concatenate(state["p"], axis=1)
                ds = jnp.concatenate(state["ds"], axis=1)
                state["dv"] = dot(p, qn[i, 1, 1])
                state["dk"] = dot(ds, qn[i, 1, 0])
                state["dq"] = dot(jnp.concatenate([kt[o, j, :, :BLK] for o, j in parts], axis=1), ds)

        for h in range(2):
            chunks.append(
                chunk(
                    *halves(i, 1, h), row(i, 1, 0, h), row(i, 1, 1, h), stack(0), stack(1),
                    functools.partial(end_later, h=h),
                )
            )

        weights = []
        for n, (o, j) in enumerate(parts):
            query_first, key_first = first_block(i, o, j)
            later = query_first < key_first
            slot = later.astype(jnp.int32)
            weight = later.astype(F32)
            weights.append(weight)

            def pick(index, later=later, o=o, j=j):
                return lambda: lax.select(later, kv[o, j, index, BLK:], kv[o, j, index, :BLK])

            def end_same(made, n=n, o=o, j=j, slot=slot, weight=weight):
                p, ds = made
                dv, dk = dot(p, qn[i, slot, 1]), dot(ds, qn[i, slot, 0])
                rows = slice(n * BLK, n * BLK + BLK)
                late_dk, late_dv = weight * dk, weight * dv
                dka[o, j, 0, :BLK] += state["dk"][rows] + (dk - late_dk)
                dka[o, j, 1, :BLK] += state["dv"][rows] + (dv - late_dv)
                dka[o, j, 0, BLK:] += late_dk
                dka[o, j, 1, BLK:] += late_dv
                state["dsb"].append(ds)
                if n == len(parts) - 1:
                    turned = []
                    for (om, jm), wm in zip(parts, weights):
                        late = kt[om, jm, :, BLK:] * wm.astype(BF16)
                        early = kt[om, jm, :, :BLK] * (1.0 - wm).astype(BF16)
                        turned.append(jnp.concatenate([late, early], axis=0))
                    both = dot(jnp.concatenate(turned, axis=1), jnp.concatenate(state["dsb"], axis=0))
                    dqa[i, 1] += state["dq"] + both[:BLK]
                    dqa[i, 0] += both[BLK:]

            chunks.append(
                chunk(
                    lambda slot=slot: qt[i, slot, 0], lambda slot=slot: qt[i, slot, 1],
                    lambda slot=slot: rw[i, slot, 0], lambda slot=slot: rw[i, slot, 1],
                    pick(0), pick(1), end_same,
                )
            )
        return chunks

    def whole(i, parts, slots=(0, 1)):
        hidden = []
        for o, j in parts:
            query_first, key_first = first_block(i, o, j)
            hidden.append(jnp.where(query_first > key_first, 0.0, 1e30).astype(F32))
        chunks = []

        def stack(index):
            return lambda: jnp.concatenate([kv[o, j, index] for o, j in parts], axis=0)

        for slot in slots:
            state = {"p": [], "ds": []}
            for h in range(2):
                lse2 = row(i, slot, 0, h)

                def penalised(lse2=lse2):
                    return jnp.concatenate([jnp.broadcast_to(lse2() + up, (TOK, TOK)) for up in hidden], axis=0)

                def end(made, slot=slot, h=h, state=state):
                    state["p"].append(made[0])
                    state["ds"].append(made[1])
                    cut = slice(h * TOK, h * TOK + TOK)
                    dqa[i, slot, :, cut] += dot(jnp.concatenate([kt[o, j] for o, j in parts], axis=1), made[1])
                    if h == 1:
                        dv = dot(jnp.concatenate(state["p"], axis=1), qn[i, slot, 1])
                        dk = dot(jnp.concatenate(state["ds"], axis=1), qn[i, slot, 0])
                        for n, (o, j) in enumerate(parts):
                            dka[o, j, 0] += dk[n * TOK : n * TOK + TOK]
                            dka[o, j, 1] += dv[n * TOK : n * TOK + TOK]

                chunks.append(chunk(*halves(i, slot, h), penalised, row(i, slot, 1, h), stack(0), stack(1), end))
        return chunks

    step = folded if fold else whole

    def work(*steps):
        pipelined([c for at in steps for c in step(*at)])

    def both_y(o):
        return [(o, 0), (o, 1)]

    pipelined(own_chunks())

    arrive(*across)
    begin(up_kv[0][1], down_kv[0][1])
    arrive(*own_up, *own_down)
    begin(up_kv[1][0], down_kv[1][0], values[7], values[1])
    kt[0, 1] = kv[0, 1, 0].T
    work((OWN, [(0, 1)]))

    def neighbours(n, carry):
        @pl.when(n == 1)
        def _():
            arrive(up_kv[0][1], down_kv[0][1])
            begin(up_kv[1][1], down_kv[1][1])
            arrive(values[7], values[1])

        @pl.when(n == 2)
        def _():
            arrive(up_kv[1][0], down_kv[1][0])
            begin(up_kv[2][0], down_kv[2][0], values[6], values[2])

        @pl.when(n == 3)
        def _():
            arrive(up_kv[1][1], down_kv[1][1])
            begin(up_kv[2][1], down_kv[2][1])
            arrive(values[6], values[2])

        distance, j = 1 + n // 2, n % 2
        for o in (distance, NZ - distance):
            kt[o, j] = kv[o, j, 0].T
        work((OWN, [(distance, j), (NZ - distance, j)]))
        return carry

    lax.fori_loop(0, 4, neighbours, jnp.int32(0))

    table = [
        (LEFT, 1), (RIGHT, 1), (LEFT, 2), (RIGHT, 2),
        (OWN, 3), (LEFT, 3), (RIGHT, 3), (OPP, 3), (OPP, 2), (OPP, 1),
    ]

    def before(t):
        @pl.when(t == 0)
        def _():
            arrive(to_right[0], to_right[2], to_left[1], to_left[2])
            begin(*far_right, *far_left)
            arrive(to_right[1], to_left[0])
            turn_queries(LEFT, from_left, rows_left)
            turn_queries(RIGHT, from_right, rows_right)

        @pl.when(t == 1)
        def _():
            arrive(up_kv[2][0])
            begin(up_kv[3][0], values[5])
            arrive(down_kv[2][0], down_kv[2][1])
            begin(down_kv[3][0], values[3])

        @pl.when(t == 2)
        def _():
            arrive(up_kv[2][1])
            turn_keys(3)
            turn_keys(5)

        @pl.when(t == 3)
        def _():
            arrive(up_kv[3][0])
            begin(values[4])

        @pl.when(t == 4)
        def _():
            arrive(*far_right, *far_left)
            turn_queries(OPP, from_opp, rows_opp)
            arrive(down_kv[3][0])
            turn_keys(4)
            arrive(values[4])

            def farthest(n, carry):
                work((2 * n, both_y(4)), (2 * n + 1, both_y(4)))
                return carry

            lax.fori_loop(0, 2, farthest, jnp.int32(0))
            start_values(4)
            pass_other(4, down_other[4])
            arrive(values[3], values[5])

    def start_values(o):
        ktx[o, 1, 1] = dka[o, 1, 1].astype(BF16)
        begin(value_sum[o])

    def pass_other(o, out, inbound=None, landed=None):
        total = dka[o, 1, 0]
        if inbound is not None:
            arrive(inbound)
            total = total + landed[1, 0].astype(F32)
        ktx[o, 1, 0] = total.astype(BF16)
        begin(out)

    def pass_mine(o, out, inbound=None, landed=None):
        arrive(value_sum[o])
        dk, dv = dka[o, 0, 0], dka[o, 0, 1] + vrx[o].astype(F32)
        if inbound is not None:
            arrive(inbound)
            dk, dv = dk + landed[0, 0].astype(F32), dv + landed[0, 1].astype(F32)
        ktx[o, 0, 0] = dk.astype(BF16)
        ktx[o, 0, 1] = dv.astype(BF16)
        begin(out)

    def after(t):
        @pl.when(t == 4)
        def _():
            pass_mine(4, up_mine[4])

        @pl.when(t == 7)
        def _():
            start_values(3)
            start_values(5)
            pass_other(3, up_other[3])
            pass_other(5, down_other[3], down_other[4], kdn.at[3])

        @pl.when(t == 8)
        def _():
            start_values(2)
            start_values(6)
            pass_mine(3, up_mine[3], up_mine[4], kup.at[3])
            pass_mine(5, down_mine[3])
            pass_other(2, up_other[2], up_other[3], kup.at[2])
            pass_other(6, down_other[2], down_other[3], kdn.at[2])

        @pl.when(t == 9)
        def _():
            start_values(1)
            start_values(7)
            pass_mine(2, up_mine[2], up_mine[3], kup.at[2])
            pass_mine(6, down_mine[2], down_mine[3], kdn.at[2])
            pass_other(1, up_other[1], up_other[2], kup.at[1])
            pass_other(7, down_other[1], down_other[2], kdn.at[1])

    def both_ways(t, carry):
        packed = jnp.int32(0)
        for n, (i, distance) in enumerate(table):
            packed = jnp.where(t == n, jnp.int32(i + 4 * distance), packed)
        pl.when(t < 5)(lambda: before(t))

        @pl.when(t == 9)
        def _():
            work((OPP, both_y(0)))

        distance = packed // 4
        work((packed % 4, both_y(distance) + both_y(NZ - distance)))
        pl.when(t > 3)(lambda: after(t))
        return carry

    lax.fori_loop(0, len(table), both_ways, jnp.int32(0))
    qtx[OPP] = dqa[OPP].astype(BF16)
    begin(*opp_sum)
    if fold:
        work((LEFT, both_y(0)))
    else:
        work((LEFT, both_y(0), (0,)), (RIGHT, both_y(0), (1,)))
        qtx[RIGHT, 1] = dqa[RIGHT, 1].astype(BF16)
        begin(right_sum[0])
    qtx[LEFT, 0] = dqa[LEFT, 0].astype(BF16)
    begin(left_sum[0])
    if fold:
        work((RIGHT, both_y(0)))
        qtx[RIGHT, 1] = dqa[RIGHT, 1].astype(BF16)
        begin(right_sum[0])
    else:
        work((LEFT, both_y(0), (1,)), (RIGHT, both_y(0), (0,)))
    arrive(*opp_sum)
    qtx[RIGHT, 0] = (dqa[RIGHT, 0] + orx[0].astype(F32)).astype(BF16)
    qtx[LEFT, 1] = (dqa[LEFT, 1] + orx[1].astype(F32)).astype(BF16)
    begin(right_sum[1], left_sum[1])
    pass_mine(1, up_mine[1], up_mine[2], kup.at[1])
    pass_mine(7, down_mine[1], down_mine[2], kdn.at[1])
    start_values(0)
    arrive(up_other[1], down_other[1])
    ktx[0, 1, 0] = (dka[0, 1, 0] + kup[0, 1, 0].astype(F32) + kdn[0, 1, 0].astype(F32)).astype(BF16)
    begin(across_sum)
    arrive(up_mine[1], down_mine[1])
    dk = dka[0, 0, 0] + kup[0, 0, 0].astype(F32) + kdn[0, 0, 0].astype(F32)
    dv = dka[0, 0, 1] + kup[0, 0, 1].astype(F32) + kdn[0, 0, 1].astype(F32)
    arrive(value_sum[0], across_sum)
    dk_out[...] = (dk + yrx[...].astype(F32)) * SCALE
    dv_out[...] = dv + vrx[0].astype(F32)
    for j, (a, b) in enumerate(((1, 0), (0, 1))):
        arrive(right_sum[a], left_sum[b])
        dq = dqa[OWN, j] + qrx[0, j].astype(F32) + qrx[1, j].astype(F32)
        dq_out[j] = dq.T * SCALE

    for copy in to_right + to_left + far_right + far_left + across + own_up + own_down + [across_sum]:
        copy.wait_send()
    for group in up_kv + down_kv:
        for copy in group:
            if copy is not None:
                copy.wait_send()
    for group in (values, up_mine, up_other, down_mine, down_other, value_sum):
        for copy in group.values():
            copy.wait_send()
    for copy in opp_sum + right_sum + left_sum:
        copy.wait_send()


N_COPIES = 16 + 25 + 23


def grads(fold, order, q, do, out, lse, k, v):
    smem = pl.BlockSpec(memory_space=pltpu.SMEM)
    vmem = pl.BlockSpec(memory_space=pltpu.VMEM)
    landing = [pltpu.VMEM((2, 2, ROWS, BLK), BF16)] * 3 + [pltpu.VMEM((2, 2, 1, ROWS), F32)] * 3
    queries = [
        pltpu.VMEM((4, 2, 2, ROWS, BLK), BF16),
        pltpu.VMEM((4, 2, 2, BLK, ROWS), BF16),
        pltpu.VMEM((4, 2, 2, 1, ROWS), F32),
    ]
    return pl.pallas_call(
        functools.partial(kernel, fold),
        out_shape=(
            jax.ShapeDtypeStruct((2, ROWS, BLK), F32),
            jax.ShapeDtypeStruct((TOK, BLK), F32),
            jax.ShapeDtypeStruct((TOK, BLK), F32),
        ),
        in_specs=[smem] + [pl.BlockSpec(memory_space=pltpu.HBM)] * 6,
        out_specs=(vmem, vmem, vmem),
        scratch_shapes=landing + queries + [
            pltpu.VMEM((NZ, NY, 2, TOK, BLK), BF16),
            pltpu.VMEM((NZ, NY, BLK, TOK), BF16),
            pltpu.VMEM((4, 2, BLK, ROWS), F32),
            pltpu.VMEM((NZ, NY, 2, TOK, BLK), F32),
            pltpu.VMEM((NZ, NY, 2, TOK, BLK), BF16),
            pltpu.VMEM((4, NY, 2, TOK, BLK), BF16),
            pltpu.VMEM((4, NY, 2, TOK, BLK), BF16),
            pltpu.VMEM((NZ, TOK, BLK), BF16),
            pltpu.VMEM((TOK, BLK), BF16),
            pltpu.VMEM((4, 2, BLK, ROWS), BF16),
            pltpu.VMEM((2, 2, BLK, ROWS), BF16),
            pltpu.VMEM((2, BLK, ROWS), BF16),
            pltpu.VMEM((2, ROWS, BLK), BF16),
            pltpu.VMEM((4, TOK), F32),
            pltpu.SemaphoreType.DMA((N_COPIES,)),
            pltpu.SemaphoreType.DMA((N_COPIES,)),
            pltpu.SemaphoreType.DMA((8,)),
        ],
        compiler_params=pltpu.CompilerParams(
            collective_id=0 if fold else 1, has_side_effects=True, vmem_limit_bytes=48 * 1024 * 1024
        ),
        name="folded" if fold else "whole",
    )(order, q, do, out, lse, k, v)


def per_device(query, key_proj, value, output, lse, d_output, block_order):
    args = (
        block_order,
        query.reshape(2, ROWS, BLK),
        d_output.reshape(2, ROWS, BLK),
        output.reshape(2, ROWS, BLK),
        lse.T,
        key_proj.reshape(TOK, BLK),
        value.reshape(TOK, BLK),
    )
    slots = jnp.arange(block_order.shape[0], dtype=jnp.int32)
    is_folded = jnp.sum(jnp.where(slots < 2, block_order, 0)) == 2 * NX * NY * NZ - 1
    dq, dk, dv = lax.cond(is_folded, functools.partial(grads, True), functools.partial(grads, False), *args)
    return dq.reshape(query.shape), dk.reshape(key_proj.shape), dv.reshape(value.shape)


def solution(mesh):
    in_specs = (
        P("ctx", "head", None),
        P("ctx", "head", None),
        P("ctx", "head", None),
        P("ctx", "head", None),
        P("ctx", "head"),
        P("ctx", "head", None),
        P(),
    )
    out_specs = (P("ctx", "head", None), P("ctx", "head", None), P("ctx", "head", None))
    return jax.shard_map(
        per_device, mesh=mesh, in_specs=in_specs, out_specs=out_specs, check_vma=False
    )
```

```python
import functools

import jax
import jax.numpy as jnp
from jax import lax
from jax.experimental import pallas as pl
from jax.experimental.pallas import tpu as pltpu
from jax.sharding import PartitionSpec as P

MESH = pl.DeviceIdType.MESH
LOG2E = 1.4426950408889634
F32 = jnp.float32
BF16 = jnp.bfloat16
BLK = 128
TOK = 256
ROWS = 512
SCALE = BLK ** (-0.5)
NX, NY, NZ = 4, 2, 8
OWN, RIGHT, OPP, LEFT = range(4)


def dot(a, b):
    return lax.dot_general(a, b, (((1,), (0,)), ((), ())), preferred_element_type=F32)


def pipelined(chunks):
    made = chunks[0][1](*chunks[0][0]())
    for n, (_, _, end) in enumerate(chunks):
        following = None
        if n + 1 < len(chunks):
            following = chunks[n + 1][1](*chunks[n + 1][0]())
        end(made)
        made = following


def chunk(qt, dot_t, lse2, delta, k, v, end, keep=None):
    def first():
        return dot(k(), qt()), dot(v(), dot_t())

    def middle(s, dp):
        e = s * (SCALE * LOG2E) - lse2()
        if keep is not None:
            e = jnp.where(keep, e, -jnp.inf)
        p = jnp.exp2(e)
        return p.astype(BF16), (p * (dp - delta())).astype(BF16)

    return first, middle, end


def kernel(
    fold, order, q_in, do_in, out_in, lse_in, k_in, v_in, dq_out, dk_out, dv_out,
    from_right, from_opp, from_left, rows_right, rows_opp, rows_left, qn, qt, rw,
    kv, kt, dqa, dka, ktx, kup, kdn, vrx, yrx, qtx, qrx, orx, out_own, lse_own, ssem, rsem, osem,
):
    ctx = lax.axis_index("ctx")
    x, plane = ctx // (NY * NZ), ctx % (NY * NZ)
    y, z = plane // NZ, plane % NZ
    right = (x + 1) % NX * (NY * NZ) + plane
    left = (x + NX - 1) % NX * (NY * NZ) + plane
    partner = x * (NY * NZ) + (1 - y) * NZ + z
    up = ctx - z + (z + 1) % NZ
    down = ctx - z + (z + NZ - 1) % NZ
    used = []

    def send(src, dst, device):
        index = len(used)
        used.append(index)
        copy = pltpu.make_async_remote_copy(
            src_ref=src, dst_ref=dst, send_sem=ssem.at[index], recv_sem=rsem.at[index],
            device_id={"ctx": device}, device_id_type=MESH,
        )
        return copy

    def begin(*copies):
        for copy in copies:
            copy.start()

    def arrive(*copies):
        for copy in copies:
            copy.wait_recv()

    to_right = [send(qn.at[OWN, j], from_left.at[j], right) for j in range(2)]
    to_right += [send(rw.at[OWN], rows_left, right)]
    to_left = [send(qn.at[OWN, j], from_right.at[j], left) for j in range(2)]
    to_left += [send(rw.at[OWN], rows_right, left)]
    far_right = [send(from_left.at[0], from_opp.at[0], right), send(rows_left.at[0], rows_opp.at[0], right)]
    far_left = [send(from_right.at[1], from_opp.at[1], left), send(rows_right.at[1], rows_opp.at[1], left)]
    across = [send(k_in, kv.at[0, 1, 0], partner), send(v_in, kv.at[0, 1, 1], partner)]
    own_up = [send(k_in, kv.at[7, 0, 0], up), send(v_in, kv.at[7, 0, 1], up)]
    own_down = [send(k_in, kv.at[1, 0, 0], down), send(v_in, kv.at[1, 0, 1], down)]
    values = {o: send(kv.at[o, 0, 1], kv.at[o, 1, 1], partner) for o in range(1, NZ)}
    up_kv = [
        [
            send(kv.at[-s % NZ, 0], kv.at[7 - s, 0], up) if s else None,
            send(kv.at[-s % NZ, 1, 0], kv.at[7 - s, 1, 0], up),
        ]
        for s in range(3)
    ]
    up_kv += [[send(kv.at[5, 0], kv.at[4, 0], up)]]
    down_kv = [
        [
            send(kv.at[s, 0], kv.at[s + 1, 0], down) if s else None,
            send(kv.at[s, 1, 0], kv.at[s + 1, 1, 0], down),
        ]
        for s in range(3)
    ]
    down_kv += [[send(kv.at[3, 1, 0], kv.at[4, 1, 0], down)]]
    up_mine = {o: send(ktx.at[o, 0], kup.at[o - 1, 0], up) for o in (4, 3, 2, 1)}
    up_other = {o: send(ktx.at[o, 1, 0], kup.at[o - 1, 1, 0], up) for o in (3, 2, 1)}
    down_mine = {o: send(ktx.at[NZ - o, 0], kdn.at[o - 1, 0], down) for o in (3, 2, 1)}
    down_other = {o: send(ktx.at[NZ - o, 1, 0], kdn.at[o - 1, 1, 0], down) for o in (4, 3, 2, 1)}
    value_sum = {o: send(ktx.at[o, 1, 1], vrx.at[o], partner) for o in range(NZ)}
    across_sum = send(ktx.at[0, 1, 0], yrx, partner)
    opp_sum = [send(qtx.at[OPP, 0], orx.at[0], right), send(qtx.at[OPP, 1], orx.at[1], left)]
    right_sum = [send(qtx.at[RIGHT, j], qrx.at[0, j], right) for j in (1, 0)]
    left_sum = [send(qtx.at[LEFT, j], qrx.at[1, j], left) for j in (0, 1)]

    def lse_row(columns):
        shape = (BLK, ROWS)
        column = lax.broadcasted_iota(jnp.int32, shape, 1)
        spread = jnp.broadcast_to(columns[:, 0:1], shape)
        for head in range(1, 4):
            spread = jnp.where(column % 4 == head, jnp.broadcast_to(columns[:, head : head + 1], shape), spread)
        mine = column // 4 == lax.broadcasted_iota(jnp.int32, shape, 0)
        return jnp.sum(jnp.where(mine, spread, 0.0), axis=0, keepdims=True)

    barrier = pltpu.get_barrier_semaphore()
    for device in (right, left, partner, up, down):
        pl.semaphore_signal(barrier, inc=1, device_id={"ctx": device}, device_id_type=MESH)
    own = [
        (k_in, kv.at[0, 0, 0]), (v_in, kv.at[0, 0, 1]),
        (q_in.at[1], qn.at[OWN, 1, 0]), (do_in.at[1], qn.at[OWN, 1, 1]),
        (q_in.at[0], qn.at[OWN, 0, 0]), (do_in.at[0], qn.at[OWN, 0, 1]),
        (out_in, out_own), (lse_in, lse_own),
    ]
    own = [pltpu.make_async_copy(src, dst, osem.at[n]) for n, (src, dst) in enumerate(own)]
    begin(*own)
    pl.semaphore_wait(barrier, 5)
    begin(across[0], own_up[0], own_down[0], across[1], own_up[1], own_down[1])
    own[2].wait()
    own[3].wait()
    begin(to_left[1], to_right[1])
    own[4].wait()
    own[5].wait()
    begin(to_right[0], to_left[0])

    own[0].wait()
    own[1].wait()
    own[6].wait()
    own[7].wait()
    for j in range(2):
        product = qn[OWN, j, 1].astype(F32) * out_own[j].astype(F32)
        rw[OWN, j, 0] = lse_row(lse_own[:, j * BLK : j * BLK + BLK].T) * LOG2E
        rw[OWN, j, 1] = jnp.sum(product.T, axis=0, keepdims=True)
    begin(to_right[2], to_left[2])

    def turn_queries(i, landed, landed_rows):
        for j in range(2):
            for part in range(2):
                if landed is not None:
                    qn[i, j, part] = landed[j, part]
                    rw[i, j, part] = landed_rows[j, part]
                qt[i, j, part] = qn[i, j, part].T

    def turn_keys(o):
        for j in range(2):
            kt[o, j] = kv[o, j, 0].T

    turn_queries(OWN, None, None)
    kt[0, 0] = kv[0, 0, 0].T
    dqa[...] = jnp.zeros_like(dqa)
    dka[...] = jnp.zeros_like(dka)

    def halves(i, j, h):
        cut = slice(h * TOK, h * TOK + TOK)
        return (
            lambda: qt[i, j, 0, :, cut], lambda: qt[i, j, 1, :, cut],
        )

    def row(i, j, kind, h):
        return lambda: rw[i, j, kind, :, h * TOK : h * TOK + TOK]

    def own_chunks():
        chunks = []
        for j in range(2):
            keys = BLK * (j + 1)
            for h in range(2):
                shape = (keys, TOK)
                keep = lax.broadcasted_iota(jnp.int32, shape, 0) <= (
                    (lax.broadcasted_iota(jnp.int32, shape, 1) + h * TOK) // 4 + j * BLK
                )

                def end(made, j=j, h=h, keys=keys):
                    p, ds = made
                    cut = slice(h * TOK, h * TOK + TOK)
                    dqa[OWN, j, :, cut] += dot(kt[0, 0, :, :keys], ds)
                    dka[0, 0, 0, :keys] += dot(ds, qn[OWN, j, 0, cut])
                    dka[0, 0, 1, :keys] += dot(p, qn[OWN, j, 1, cut])

                chunks.append(
                    chunk(
                        *halves(OWN, j, h), row(OWN, j, 0, h), row(OWN, j, 1, h),
                        lambda keys=keys: kv[0, 0, 0, :keys], lambda keys=keys: kv[0, 0, 1, :keys], end, keep,
                    )
                )
        return chunks

    def first_block(i, o, j):
        owner = x * (NY * NZ) + (y + j) % NY * NZ + (z + o) % NZ
        return order[2 * ((x + i) % NX * (NY * NZ) + plane)], order[2 * owner]

    def folded(i, parts):
        state = {"p": [], "ds": [], "dsb": []}
        chunks = []

        def stack(index):
            return lambda: jnp.concatenate([kv[o, j, index, :BLK] for o, j in parts], axis=0)

        def end_later(made, h):
            state["p"].append(made[0])
            state["ds"].append(made[1])
            if h == 1:
                p = jnp.concatenate(state["p"], axis=1)
                ds = jnp.concatenate(state["ds"], axis=1)
                state["dv"] = dot(p, qn[i, 1, 1])
                state["dk"] = dot(ds, qn[i, 1, 0])
                state["dq"] = dot(jnp.concatenate([kt[o, j, :, :BLK] for o, j in parts], axis=1), ds)

        for h in range(2):
            chunks.append(
                chunk(
                    *halves(i, 1, h), row(i, 1, 0, h), row(i, 1, 1, h), stack(0), stack(1),
                    functools.partial(end_later, h=h),
                )
            )

        weights = []
        for n, (o, j) in enumerate(parts):
            query_first, key_first = first_block(i, o, j)
            later = query_first < key_first
            slot = later.astype(jnp.int32)
            weight = later.astype(F32)
            weights.append(weight)

            def pick(index, later=later, o=o, j=j):
                return lambda: lax.select(later, kv[o, j, index, BLK:], kv[o, j, index, :BLK])

            def end_same(made, n=n, o=o, j=j, slot=slot, weight=weight):
                p, ds = made
                dv, dk = dot(p, qn[i, slot, 1]), dot(ds, qn[i, slot, 0])
                rows = slice(n * BLK, n * BLK + BLK)
                late_dk, late_dv = weight * dk, weight * dv
                dka[o, j, 0, :BLK] += state["dk"][rows] + (dk - late_dk)
                dka[o, j, 1, :BLK] += state["dv"][rows] + (dv - late_dv)
                dka[o, j, 0, BLK:] += late_dk
                dka[o, j, 1, BLK:] += late_dv
                state["dsb"].append(ds)
                if n == len(parts) - 1:
                    turned = []
                    for (om, jm), wm in zip(parts, weights):
                        late = kt[om, jm, :, BLK:] * wm.astype(BF16)
                        early = kt[om, jm, :, :BLK] * (1.0 - wm).astype(BF16)
                        turned.append(jnp.concatenate([late, early], axis=0))
                    both = dot(jnp.concatenate(turned, axis=1), jnp.concatenate(state["dsb"], axis=0))
                    dqa[i, 1] += state["dq"] + both[:BLK]
                    dqa[i, 0] += both[BLK:]

            chunks.append(
                chunk(
                    lambda slot=slot: qt[i, slot, 0], lambda slot=slot: qt[i, slot, 1],
                    lambda slot=slot: rw[i, slot, 0], lambda slot=slot: rw[i, slot, 1],
                    pick(0), pick(1), end_same,
                )
            )
        return chunks

    def whole(i, parts, slots=(0, 1)):
        hidden = []
        for o, j in parts:
            query_first, key_first = first_block(i, o, j)
            hidden.append(jnp.where(query_first > key_first, 0.0, 1e30).astype(F32))
        chunks = []

        def stack(index):
            return lambda: jnp.concatenate([kv[o, j, index] for o, j in parts], axis=0)

        for slot in slots:
            state = {"p": [], "ds": []}
            for h in range(2):
                lse2 = row(i, slot, 0, h)

                def penalised(lse2=lse2):
                    return jnp.concatenate([jnp.broadcast_to(lse2() + up, (TOK, TOK)) for up in hidden], axis=0)

                def end(made, slot=slot, h=h, state=state):
                    state["p"].append(made[0])
                    state["ds"].append(made[1])
                    cut = slice(h * TOK, h * TOK + TOK)
                    dqa[i, slot, :, cut] += dot(jnp.concatenate([kt[o, j] for o, j in parts], axis=1), made[1])
                    if h == 1:
                        dv = dot(jnp.concatenate(state["p"], axis=1), qn[i, slot, 1])
                        dk = dot(jnp.concatenate(state["ds"], axis=1), qn[i, slot, 0])
                        for n, (o, j) in enumerate(parts):
                            dka[o, j, 0] += dk[n * TOK : n * TOK + TOK]
                            dka[o, j, 1] += dv[n * TOK : n * TOK + TOK]

                chunks.append(chunk(*halves(i, slot, h), penalised, row(i, slot, 1, h), stack(0), stack(1), end))
        return chunks

    step = folded if fold else whole

    def work(*steps):
        pipelined([c for at in steps for c in step(*at)])

    def both_y(o):
        return [(o, 0), (o, 1)]

    pipelined(own_chunks())

    arrive(*across)
    begin(up_kv[0][1], down_kv[0][1])
    arrive(*own_up, *own_down)
    begin(up_kv[1][0], down_kv[1][0], values[7], values[1])
    kt[0, 1] = kv[0, 1, 0].T
    work((OWN, [(0, 1)]))

    def neighbours(n, carry):
        @pl.when(n == 1)
        def _():
            arrive(up_kv[0][1], down_kv[0][1])
            begin(up_kv[1][1], down_kv[1][1])
            arrive(values[7], values[1])

        @pl.when(n == 2)
        def _():
            arrive(up_kv[1][0], down_kv[1][0])
            begin(up_kv[2][0], down_kv[2][0], values[6], values[2])

        @pl.when(n == 3)
        def _():
            arrive(up_kv[1][1], down_kv[1][1])
            begin(up_kv[2][1], down_kv[2][1])
            arrive(values[6], values[2])

        distance, j = 1 + n // 2, n % 2
        for o in (distance, NZ - distance):
            kt[o, j] = kv[o, j, 0].T
        work((OWN, [(distance, j), (NZ - distance, j)]))
        return carry

    lax.fori_loop(0, 4, neighbours, jnp.int32(0))

    table = [
        (LEFT, 2), (RIGHT, 2), (LEFT, 1), (OWN, 3),
        (LEFT, 3), (RIGHT, 3), (OPP, 3), (OPP, 2), (RIGHT, 1), (OPP, 1),
    ]

    def before(t):
        @pl.when(t == 0)
        def _():
            arrive(to_right[0], to_right[2], to_left[1], to_left[2])
            begin(*far_right, *far_left)
            arrive(to_right[1], to_left[0])
            turn_queries(LEFT, from_left, rows_left)
            turn_queries(RIGHT, from_right, rows_right)

        @pl.when(t == 1)
        def _():
            arrive(up_kv[2][0])
            begin(up_kv[3][0], values[5])
            arrive(down_kv[2][0], down_kv[2][1])
            begin(down_kv[3][0], values[3])

        @pl.when(t == 2)
        def _():
            arrive(up_kv[2][1])
            turn_keys(3)
            turn_keys(5)

        @pl.when(t == 3)
        def _():
            arrive(up_kv[3][0])
            begin(values[4])
            arrive(values[3], values[5])

        @pl.when(t == 4)
        def _():
            arrive(*far_right, *far_left)
            turn_queries(OPP, from_opp, rows_opp)
            arrive(down_kv[3][0])
            turn_keys(4)
            arrive(values[4])

            def farthest(n, carry):
                work((2 * n, both_y(4)), (2 * n + 1, both_y(4)))
                return carry

            lax.fori_loop(0, 2, farthest, jnp.int32(0))
            start_values(4)
            pass_other(4, down_other[4])

    def start_values(o):
        ktx[o, 1, 1] = dka[o, 1, 1].astype(BF16)
        begin(value_sum[o])

    def pass_other(o, out, inbound=None, landed=None):
        total = dka[o, 1, 0]
        if inbound is not None:
            arrive(inbound)
            total = total + landed[1, 0].astype(F32)
        ktx[o, 1, 0] = total.astype(BF16)
        begin(out)

    def pass_mine(o, out, inbound=None, landed=None):
        arrive(value_sum[o])
        dk, dv = dka[o, 0, 0], dka[o, 0, 1] + vrx[o].astype(F32)
        if inbound is not None:
            arrive(inbound)
            dk, dv = dk + landed[0, 0].astype(F32), dv + landed[0, 1].astype(F32)
        ktx[o, 0, 0] = dk.astype(BF16)
        ktx[o, 0, 1] = dv.astype(BF16)
        begin(out)

    def after(t):
        @pl.when(t == 4)
        def _():
            pass_mine(4, up_mine[4])

        @pl.when(t == 6)
        def _():
            start_values(3)
            start_values(5)
            pass_other(3, up_other[3])
            pass_other(5, down_other[3], down_other[4], kdn.at[3])

        @pl.when(t == 7)
        def _():
            start_values(2)
            start_values(6)
            pass_mine(3, up_mine[3], up_mine[4], kup.at[3])
            pass_mine(5, down_mine[3])
            pass_other(2, up_other[2], up_other[3], kup.at[2])
            pass_other(6, down_other[2], down_other[3], kdn.at[2])

        @pl.when(t == 8)
        def _():
            pass_mine(2, up_mine[2], up_mine[3], kup.at[2])
            pass_mine(6, down_mine[2], down_mine[3], kdn.at[2])

        @pl.when(t == 9)
        def _():
            start_values(1)
            start_values(7)
            pass_other(1, up_other[1], up_other[2], kup.at[1])
            pass_other(7, down_other[1], down_other[2], kdn.at[1])

    def both_ways(t, carry):
        packed = jnp.int32(0)
        for n, (i, distance) in enumerate(table):
            packed = jnp.where(t == n, jnp.int32(i + 4 * distance), packed)
        pl.when(t < 5)(lambda: before(t))

        @pl.when(t == 9)
        def _():
            work((OPP, both_y(0)))

        distance = packed // 4
        work((packed % 4, both_y(distance) + both_y(NZ - distance)))
        pl.when(t > 3)(lambda: after(t))
        return carry

    lax.fori_loop(0, len(table), both_ways, jnp.int32(0))
    qtx[OPP] = dqa[OPP].astype(BF16)
    begin(*opp_sum)
    if fold:
        work((LEFT, both_y(0)))
    else:
        work((LEFT, both_y(0), (0,)), (RIGHT, both_y(0), (1,)))
        qtx[RIGHT, 1] = dqa[RIGHT, 1].astype(BF16)
        begin(right_sum[0])
    qtx[LEFT, 0] = dqa[LEFT, 0].astype(BF16)
    begin(left_sum[0])
    if fold:
        work((RIGHT, both_y(0)))
        qtx[RIGHT, 1] = dqa[RIGHT, 1].astype(BF16)
        begin(right_sum[0])
    else:
        work((LEFT, both_y(0), (1,)), (RIGHT, both_y(0), (0,)))
    arrive(*opp_sum)
    qtx[RIGHT, 0] = (dqa[RIGHT, 0] + orx[0].astype(F32)).astype(BF16)
    qtx[LEFT, 1] = (dqa[LEFT, 1] + orx[1].astype(F32)).astype(BF16)
    begin(right_sum[1], left_sum[1])
    pass_mine(1, up_mine[1], up_mine[2], kup.at[1])
    pass_mine(7, down_mine[1], down_mine[2], kdn.at[1])
    start_values(0)
    arrive(up_other[1], down_other[1])
    ktx[0, 1, 0] = (dka[0, 1, 0] + kup[0, 1, 0].astype(F32) + kdn[0, 1, 0].astype(F32)).astype(BF16)
    begin(across_sum)
    arrive(up_mine[1], down_mine[1])
    dk = dka[0, 0, 0] + kup[0, 0, 0].astype(F32) + kdn[0, 0, 0].astype(F32)
    dv = dka[0, 0, 1] + kup[0, 0, 1].astype(F32) + kdn[0, 0, 1].astype(F32)
    arrive(value_sum[0], across_sum)
    dk_out[...] = (dk + yrx[...].astype(F32)) * SCALE
    dv_out[...] = dv + vrx[0].astype(F32)
    for j, (a, b) in enumerate(((1, 0), (0, 1))):
        arrive(right_sum[a], left_sum[b])
        dq = dqa[OWN, j] + qrx[0, j].astype(F32) + qrx[1, j].astype(F32)
        dq_out[j] = dq.T * SCALE

    for copy in to_right + to_left + far_right + far_left + across + own_up + own_down + [across_sum]:
        copy.wait_send()
    for group in up_kv + down_kv:
        for copy in group:
            if copy is not None:
                copy.wait_send()
    for group in (values, up_mine, up_other, down_mine, down_other, value_sum):
        for copy in group.values():
            copy.wait_send()
    for copy in opp_sum + right_sum + left_sum:
        copy.wait_send()


N_COPIES = 16 + 25 + 23


def grads(fold, order, q, do, out, lse, k, v):
    smem = pl.BlockSpec(memory_space=pltpu.SMEM)
    vmem = pl.BlockSpec(memory_space=pltpu.VMEM)
    landing = [pltpu.VMEM((2, 2, ROWS, BLK), BF16)] * 3 + [pltpu.VMEM((2, 2, 1, ROWS), F32)] * 3
    queries = [
        pltpu.VMEM((4, 2, 2, ROWS, BLK), BF16),
        pltpu.VMEM((4, 2, 2, BLK, ROWS), BF16),
        pltpu.VMEM((4, 2, 2, 1, ROWS), F32),
    ]
    return pl.pallas_call(
        functools.partial(kernel, fold),
        out_shape=(
            jax.ShapeDtypeStruct((2, ROWS, BLK), F32),
            jax.ShapeDtypeStruct((TOK, BLK), F32),
            jax.ShapeDtypeStruct((TOK, BLK), F32),
        ),
        in_specs=[smem] + [pl.BlockSpec(memory_space=pltpu.HBM)] * 6,
        out_specs=(vmem, vmem, vmem),
        scratch_shapes=landing + queries + [
            pltpu.VMEM((NZ, NY, 2, TOK, BLK), BF16),
            pltpu.VMEM((NZ, NY, BLK, TOK), BF16),
            pltpu.VMEM((4, 2, BLK, ROWS), F32),
            pltpu.VMEM((NZ, NY, 2, TOK, BLK), F32),
            pltpu.VMEM((NZ, NY, 2, TOK, BLK), BF16),
            pltpu.VMEM((4, NY, 2, TOK, BLK), BF16),
            pltpu.VMEM((4, NY, 2, TOK, BLK), BF16),
            pltpu.VMEM((NZ, TOK, BLK), BF16),
            pltpu.VMEM((TOK, BLK), BF16),
            pltpu.VMEM((4, 2, BLK, ROWS), BF16),
            pltpu.VMEM((2, 2, BLK, ROWS), BF16),
            pltpu.VMEM((2, BLK, ROWS), BF16),
            pltpu.VMEM((2, ROWS, BLK), BF16),
            pltpu.VMEM((4, TOK), F32),
            pltpu.SemaphoreType.DMA((N_COPIES,)),
            pltpu.SemaphoreType.DMA((N_COPIES,)),
            pltpu.SemaphoreType.DMA((8,)),
        ],
        compiler_params=pltpu.CompilerParams(
            collective_id=0 if fold else 1, has_side_effects=True, vmem_limit_bytes=48 * 1024 * 1024
        ),
        name="folded" if fold else "whole",
    )(order, q, do, out, lse, k, v)


def hand_out(dq_in, dk_in, dv_in, dq_out, dk_out, dv_out, sem):
    copies = [
        pltpu.make_async_copy(src, dst, sem.at[n])
        for n, (src, dst) in enumerate(((dq_in, dq_out), (dk_in, dk_out), (dv_in, dv_out)))
    ]
    for copy in copies:
        copy.start()
    for copy in copies:
        copy.wait()


def per_device(query, key_proj, value, output, lse, d_output, block_order):
    args = (
        block_order,
        query.reshape(2, ROWS, BLK),
        d_output.reshape(2, ROWS, BLK),
        output.reshape(2, ROWS, BLK),
        lse.T,
        key_proj.reshape(TOK, BLK),
        value.reshape(TOK, BLK),
    )
    slots = jnp.arange(block_order.shape[0], dtype=jnp.int32)
    is_folded = jnp.sum(jnp.where(slots < 2, block_order, 0)) == 2 * NX * NY * NZ - 1
    dq, dk, dv = lax.cond(is_folded, functools.partial(grads, True), functools.partial(grads, False), *args)
    anywhere = pl.BlockSpec(memory_space=pl.ANY)
    dq, dk, dv = pl.pallas_call(
        hand_out,
        out_shape=tuple(jax.ShapeDtypeStruct(a.shape, a.dtype) for a in (dq, dk, dv)),
        in_specs=[anywhere] * 3,
        out_specs=(pl.BlockSpec(memory_space=pltpu.HBM),) * 3,
        scratch_shapes=[pltpu.SemaphoreType.DMA((3,))],
        name="hand_out",
    )(dq, dk, dv)
    return dq.reshape(query.shape), dk.reshape(key_proj.shape), dv.reshape(value.shape)


def solution(mesh):
    in_specs = (
        P("ctx", "head", None),
        P("ctx", "head", None),
        P("ctx", "head", None),
        P("ctx", "head", None),
        P("ctx", "head"),
        P("ctx", "head", None),
        P(),
    )
    out_specs = (P("ctx", "head", None), P("ctx", "head", None), P("ctx", "head", None))
    return jax.shard_map(
        per_device, mesh=mesh, in_specs=in_specs, out_specs=out_specs, check_vma=False
    )
```

```python
import functools

import jax
import jax.numpy as jnp
from jax import lax
from jax.experimental import pallas as pl
from jax.experimental.pallas import tpu as pltpu
from jax.sharding import PartitionSpec as P

MESH = pl.DeviceIdType.MESH
LOG2E = 1.4426950408889634
F32 = jnp.float32
BF16 = jnp.bfloat16
BLK = 128
TOK = 256
ROWS = 512
SCALE = BLK ** (-0.5)
NX, NY, NZ = 4, 2, 8
OWN, RIGHT, OPP, LEFT = range(4)


def dot(a, b):
    return lax.dot_general(a, b, (((1,), (0,)), ((), ())), preferred_element_type=F32)


def pipelined(chunks):
    made = chunks[0][1](*chunks[0][0]())
    for n, (_, _, end) in enumerate(chunks):
        following = None
        if n + 1 < len(chunks):
            following = chunks[n + 1][1](*chunks[n + 1][0]())
        end(made)
        made = following


def chunk(qt, dot_t, lse2, delta, k, v, end, keep=None):
    def first():
        return dot(k(), qt()), dot(v(), dot_t())

    def middle(s, dp):
        e = s * (SCALE * LOG2E) - lse2()
        if keep is not None:
            e = jnp.where(keep, e, -jnp.inf)
        p = jnp.exp2(e)
        return p.astype(BF16), (p * (dp - delta())).astype(BF16)

    return first, middle, end


def kernel(
    fold, order, q_in, do_in, out_in, lse_in, k_in, v_in, dq_out, dk_out, dv_out,
    from_right, from_opp, from_left, rows_right, rows_opp, rows_left, qn, qt, rw,
    kv, kt, dqa, dka, ktx, kup, kdn, vrx, yrx, qtx, qrx, orx, out_own, lse_own, ssem, rsem, osem,
):
    ctx = lax.axis_index("ctx")
    x, plane = ctx // (NY * NZ), ctx % (NY * NZ)
    y, z = plane // NZ, plane % NZ
    right = (x + 1) % NX * (NY * NZ) + plane
    left = (x + NX - 1) % NX * (NY * NZ) + plane
    partner = x * (NY * NZ) + (1 - y) * NZ + z
    up = ctx - z + (z + 1) % NZ
    down = ctx - z + (z + NZ - 1) % NZ
    used = []

    def send(src, dst, device):
        index = len(used)
        used.append(index)
        copy = pltpu.make_async_remote_copy(
            src_ref=src, dst_ref=dst, send_sem=ssem.at[index], recv_sem=rsem.at[index],
            device_id={"ctx": device}, device_id_type=MESH,
        )
        return copy

    def begin(*copies):
        for copy in copies:
            copy.start()

    def arrive(*copies):
        for copy in copies:
            copy.wait_recv()

    to_right = [send(qn.at[OWN, j], from_left.at[j], right) for j in range(2)]
    to_right += [send(rw.at[OWN], rows_left, right)]
    to_left = [send(qn.at[OWN, j], from_right.at[j], left) for j in range(2)]
    to_left += [send(rw.at[OWN], rows_right, left)]
    far_right = [send(from_left.at[0], from_opp.at[0], right), send(rows_left.at[0], rows_opp.at[0], right)]
    far_left = [send(from_right.at[1], from_opp.at[1], left), send(rows_right.at[1], rows_opp.at[1], left)]
    across = [send(k_in, kv.at[0, 1, 0], partner), send(v_in, kv.at[0, 1, 1], partner)]
    own_up = [send(k_in, kv.at[7, 0, 0], up), send(v_in, kv.at[7, 0, 1], up)]
    own_down = [send(k_in, kv.at[1, 0, 0], down), send(v_in, kv.at[1, 0, 1], down)]
    values = {o: send(kv.at[o, 0, 1], kv.at[o, 1, 1], partner) for o in range(1, NZ)}
    up_kv = [
        [
            send(kv.at[-s % NZ, 0], kv.at[7 - s, 0], up) if s else None,
            send(kv.at[-s % NZ, 1, 0], kv.at[7 - s, 1, 0], up),
        ]
        for s in range(3)
    ]
    up_kv += [[send(kv.at[5, 0], kv.at[4, 0], up)]]
    down_kv = [
        [
            send(kv.at[s, 0], kv.at[s + 1, 0], down) if s else None,
            send(kv.at[s, 1, 0], kv.at[s + 1, 1, 0], down),
        ]
        for s in range(3)
    ]
    down_kv += [[send(kv.at[3, 1, 0], kv.at[4, 1, 0], down)]]
    up_mine = {o: send(ktx.at[o, 0], kup.at[o - 1, 0], up) for o in (4, 3, 2, 1)}
    up_other = {o: send(ktx.at[o, 1, 0], kup.at[o - 1, 1, 0], up) for o in (3, 2, 1)}
    down_mine = {o: send(ktx.at[NZ - o, 0], kdn.at[o - 1, 0], down) for o in (3, 2, 1)}
    down_other = {o: send(ktx.at[NZ - o, 1, 0], kdn.at[o - 1, 1, 0], down) for o in (4, 3, 2, 1)}
    value_sum = {o: send(ktx.at[o, 1, 1], vrx.at[o], partner) for o in range(NZ)}
    across_sum = send(ktx.at[0, 1, 0], yrx, partner)
    opp_sum = [send(qtx.at[OPP, 0], orx.at[0], right), send(qtx.at[OPP, 1], orx.at[1], left)]
    right_sum = [send(qtx.at[RIGHT, j], qrx.at[0, j], right) for j in (1, 0)]
    left_sum = [send(qtx.at[LEFT, j], qrx.at[1, j], left) for j in (0, 1)]

    def lse_row(columns):
        shape = (BLK, ROWS)
        column = lax.broadcasted_iota(jnp.int32, shape, 1)
        spread = jnp.broadcast_to(columns[:, 0:1], shape)
        for head in range(1, 4):
            spread = jnp.where(column % 4 == head, jnp.broadcast_to(columns[:, head : head + 1], shape), spread)
        mine = column // 4 == lax.broadcasted_iota(jnp.int32, shape, 0)
        return jnp.sum(jnp.where(mine, spread, 0.0), axis=0, keepdims=True)

    barrier = pltpu.get_barrier_semaphore()
    for device in (right, left, partner, up, down):
        pl.semaphore_signal(barrier, inc=1, device_id={"ctx": device}, device_id_type=MESH)
    own = [
        (k_in, kv.at[0, 0, 0]), (v_in, kv.at[0, 0, 1]),
        (q_in.at[1], qn.at[OWN, 1, 0]), (do_in.at[1], qn.at[OWN, 1, 1]),
        (q_in.at[0], qn.at[OWN, 0, 0]), (do_in.at[0], qn.at[OWN, 0, 1]),
        (out_in, out_own), (lse_in, lse_own),
    ]
    own = [pltpu.make_async_copy(src, dst, osem.at[n]) for n, (src, dst) in enumerate(own)]
    begin(*own)
    pl.semaphore_wait(barrier, 5)
    begin(across[0], own_up[0], own_down[0], across[1], own_up[1], own_down[1])
    own[2].wait()
    own[3].wait()
    begin(to_left[1], to_right[1])
    for n in (0, 1, 4, 5, 6, 7):
        own[n].wait()
    for j in range(2):
        product = qn[OWN, j, 1].astype(F32) * out_own[j].astype(F32)
        rw[OWN, j, 0] = lse_row(lse_own[:, j * BLK : j * BLK + BLK].T) * LOG2E
        rw[OWN, j, 1] = jnp.sum(product.T, axis=0, keepdims=True)
    begin(to_right[2], to_left[2], to_right[0], to_left[0])

    def turn_queries(i, landed, landed_rows, slots=(0, 1)):
        for j in slots:
            for part in range(2):
                if landed is not None:
                    qn[i, j, part] = landed[j, part]
                    rw[i, j, part] = landed_rows[j, part]
                qt[i, j, part] = qn[i, j, part].T

    def turn_keys(o):
        for j in range(2):
            kt[o, j] = kv[o, j, 0].T

    turn_queries(OWN, None, None)
    kt[0, 0] = kv[0, 0, 0].T
    dqa[...] = jnp.zeros_like(dqa)
    dka[...] = jnp.zeros_like(dka)

    def halves(i, j, h):
        cut = slice(h * TOK, h * TOK + TOK)
        return (
            lambda: qt[i, j, 0, :, cut], lambda: qt[i, j, 1, :, cut],
        )

    def row(i, j, kind, h):
        return lambda: rw[i, j, kind, :, h * TOK : h * TOK + TOK]

    def own_chunks():
        chunks = []
        for j in range(2):
            keys = BLK * (j + 1)
            for h in range(2):
                shape = (keys, TOK)
                keep = lax.broadcasted_iota(jnp.int32, shape, 0) <= (
                    (lax.broadcasted_iota(jnp.int32, shape, 1) + h * TOK) // 4 + j * BLK
                )

                def end(made, j=j, h=h, keys=keys):
                    p, ds = made
                    cut = slice(h * TOK, h * TOK + TOK)
                    dqa[OWN, j, :, cut] += dot(kt[0, 0, :, :keys], ds)
                    dka[0, 0, 0, :keys] += dot(ds, qn[OWN, j, 0, cut])
                    dka[0, 0, 1, :keys] += dot(p, qn[OWN, j, 1, cut])

                chunks.append(
                    chunk(
                        *halves(OWN, j, h), row(OWN, j, 0, h), row(OWN, j, 1, h),
                        lambda keys=keys: kv[0, 0, 0, :keys], lambda keys=keys: kv[0, 0, 1, :keys], end, keep,
                    )
                )
        return chunks

    def first_block(i, o, j):
        owner = x * (NY * NZ) + (y + j) % NY * NZ + (z + o) % NZ
        return order[2 * ((x + i) % NX * (NY * NZ) + plane)], order[2 * owner]

    def folded(i, parts):
        state = {"p": [], "ds": [], "dsb": []}
        chunks = []

        def stack(index):
            return lambda: jnp.concatenate([kv[o, j, index, :BLK] for o, j in parts], axis=0)

        def end_later(made, h):
            state["p"].append(made[0])
            state["ds"].append(made[1])
            if h == 1:
                p = jnp.concatenate(state["p"], axis=1)
                ds = jnp.concatenate(state["ds"], axis=1)
                state["dv"] = dot(p, qn[i, 1, 1])
                state["dk"] = dot(ds, qn[i, 1, 0])
                state["dq"] = dot(jnp.concatenate([kt[o, j, :, :BLK] for o, j in parts], axis=1), ds)

        for h in range(2):
            chunks.append(
                chunk(
                    *halves(i, 1, h), row(i, 1, 0, h), row(i, 1, 1, h), stack(0), stack(1),
                    functools.partial(end_later, h=h),
                )
            )

        weights = []
        for n, (o, j) in enumerate(parts):
            query_first, key_first = first_block(i, o, j)
            later = query_first < key_first
            slot = later.astype(jnp.int32)
            weight = later.astype(F32)
            weights.append(weight)

            def pick(index, later=later, o=o, j=j):
                return lambda: lax.select(later, kv[o, j, index, BLK:], kv[o, j, index, :BLK])

            def end_same(made, n=n, o=o, j=j, slot=slot, weight=weight):
                p, ds = made
                dv, dk = dot(p, qn[i, slot, 1]), dot(ds, qn[i, slot, 0])
                rows = slice(n * BLK, n * BLK + BLK)
                late_dk, late_dv = weight * dk, weight * dv
                dka[o, j, 0, :BLK] += state["dk"][rows] + (dk - late_dk)
                dka[o, j, 1, :BLK] += state["dv"][rows] + (dv - late_dv)
                dka[o, j, 0, BLK:] += late_dk
                dka[o, j, 1, BLK:] += late_dv
                state["dsb"].append(ds)
                if n == len(parts) - 1:
                    turned = []
                    for (om, jm), wm in zip(parts, weights):
                        late = kt[om, jm, :, BLK:] * wm.astype(BF16)
                        early = kt[om, jm, :, :BLK] * (1.0 - wm).astype(BF16)
                        turned.append(jnp.concatenate([late, early], axis=0))
                    both = dot(jnp.concatenate(turned, axis=1), jnp.concatenate(state["dsb"], axis=0))
                    dqa[i, 1] += state["dq"] + both[:BLK]
                    dqa[i, 0] += both[BLK:]

            chunks.append(
                chunk(
                    lambda slot=slot: qt[i, slot, 0], lambda slot=slot: qt[i, slot, 1],
                    lambda slot=slot: rw[i, slot, 0], lambda slot=slot: rw[i, slot, 1],
                    pick(0), pick(1), end_same,
                )
            )
        return chunks

    def whole(i, parts, slots=(0, 1)):
        hidden = []
        for o, j in parts:
            query_first, key_first = first_block(i, o, j)
            hidden.append(jnp.where(query_first > key_first, 0.0, 1e30).astype(F32))
        chunks = []

        def stack(index):
            return lambda: jnp.concatenate([kv[o, j, index] for o, j in parts], axis=0)

        state = {"p": [], "ds": []}
        for slot in slots:
            for h in range(2):
                lse2 = row(i, slot, 0, h)

                def penalised(lse2=lse2):
                    return jnp.concatenate([jnp.broadcast_to(lse2() + up, (TOK, TOK)) for up in hidden], axis=0)

                def end(made, slot=slot, h=h):
                    state["p"].append(made[0])
                    state["ds"].append(made[1])
                    cut = slice(h * TOK, h * TOK + TOK)
                    dqa[i, slot, :, cut] += dot(jnp.concatenate([kt[o, j] for o, j in parts], axis=1), made[1])
                    if h == 1 and slot == slots[-1]:
                        do = jnp.concatenate([qn[i, at, 1] for at in slots], axis=0)
                        q = jnp.concatenate([qn[i, at, 0] for at in slots], axis=0)
                        dv = dot(jnp.concatenate(state["p"], axis=1), do)
                        dk = dot(jnp.concatenate(state["ds"], axis=1), q)
                        for n, (o, j) in enumerate(parts):
                            dka[o, j, 0] += dk[n * TOK : n * TOK + TOK]
                            dka[o, j, 1] += dv[n * TOK : n * TOK + TOK]

                chunks.append(chunk(*halves(i, slot, h), penalised, row(i, slot, 1, h), stack(0), stack(1), end))
        return chunks

    step = folded if fold else whole

    def work(*steps):
        pipelined([c for at in steps for c in step(*at)])

    def both_y(o):
        return [(o, 0), (o, 1)]

    pipelined(own_chunks())

    arrive(*across)
    begin(up_kv[0][1], down_kv[0][1])
    arrive(*own_up, *own_down)
    begin(up_kv[1][0], down_kv[1][0], values[7], values[1])
    kt[0, 1] = kv[0, 1, 0].T
    work((OWN, [(0, 1)]))

    def neighbours(n, carry):
        @pl.when(n == 1)
        def _():
            arrive(up_kv[0][1], down_kv[0][1])
            begin(up_kv[1][1], down_kv[1][1])
            arrive(values[7], values[1])

        @pl.when(n == 2)
        def _():
            arrive(up_kv[1][0], down_kv[1][0])
            begin(up_kv[2][0], down_kv[2][0], values[6], values[2])

        @pl.when(n == 3)
        def _():
            arrive(up_kv[1][1], down_kv[1][1])
            begin(up_kv[2][1], down_kv[2][1])
            arrive(values[6], values[2])

        distance, j = 1 + n // 2, n % 2
        for o in (distance, NZ - distance):
            kt[o, j] = kv[o, j, 0].T
        work((OWN, [(distance, j), (NZ - distance, j)]))
        return carry

    lax.fori_loop(0, 4, neighbours, jnp.int32(0))

    table = [
        (LEFT, 2), (RIGHT, 2), (LEFT, 1), (OWN, 3),
        (LEFT, 3), (RIGHT, 3), (OPP, 3), (OPP, 2), (RIGHT, 1), (OPP, 1),
    ]

    def later_queries():
        arrive(to_right[1], to_left[1], to_right[2], to_left[2])
        begin(*far_left)
        turn_queries(LEFT, from_left, rows_left, (1,))
        turn_queries(RIGHT, from_right, rows_right, (1,))

    def earlier_queries():
        arrive(to_right[0], to_left[0])
        begin(*far_right)
        turn_queries(LEFT, from_left, rows_left, (0,))
        turn_queries(RIGHT, from_right, rows_right, (0,))

    def pass_third():
        arrive(up_kv[2][0])
        begin(up_kv[3][0], values[5])
        arrive(down_kv[2][0], down_kv[2][1])
        begin(down_kv[3][0], values[3])

    start = 0
    if not fold:
        second = both_y(2) + both_y(6)
        later_queries()
        work((LEFT, second, (1,)), (RIGHT, second, (1,)))
        earlier_queries()
        pass_third()
        work((LEFT, second, (0,)), (RIGHT, second, (0,)))
        start = 2

    def before(t):
        if fold:
            @pl.when(t == 0)
            def _():
                later_queries()
                earlier_queries()

            pl.when(t == 1)(pass_third)

        @pl.when(t == 2)
        def _():
            arrive(up_kv[2][1])
            turn_keys(3)
            turn_keys(5)

        @pl.when(t == 3)
        def _():
            arrive(up_kv[3][0])
            begin(values[4])
            arrive(values[3], values[5])

        @pl.when(t == 4)
        def _():
            arrive(*far_right, *far_left)
            turn_queries(OPP, from_opp, rows_opp)
            arrive(down_kv[3][0])
            turn_keys(4)
            arrive(values[4])

            def farthest(n, carry):
                work((2 * n, both_y(4)), (2 * n + 1, both_y(4)))
                return carry

            lax.fori_loop(0, 2, farthest, jnp.int32(0))
            start_values(4)
            pass_other(4, down_other[4])

    def start_values(o):
        ktx[o, 1, 1] = dka[o, 1, 1].astype(BF16)
        begin(value_sum[o])

    def pass_other(o, out, inbound=None, landed=None):
        total = dka[o, 1, 0]
        if inbound is not None:
            arrive(inbound)
            total = total + landed[1, 0].astype(F32)
        ktx[o, 1, 0] = total.astype(BF16)
        begin(out)

    def pass_mine(o, out, inbound=None, landed=None):
        arrive(value_sum[o])
        dk, dv = dka[o, 0, 0], dka[o, 0, 1] + vrx[o].astype(F32)
        if inbound is not None:
            arrive(inbound)
            dk, dv = dk + landed[0, 0].astype(F32), dv + landed[0, 1].astype(F32)
        ktx[o, 0, 0] = dk.astype(BF16)
        ktx[o, 0, 1] = dv.astype(BF16)
        begin(out)

    def after(t):
        @pl.when(t == 4)
        def _():
            pass_mine(4, up_mine[4])

        @pl.when(t == 6)
        def _():
            start_values(3)
            start_values(5)
            pass_other(3, up_other[3])
            pass_other(5, down_other[3], down_other[4], kdn.at[3])

        @pl.when(t == 7)
        def _():
            start_values(2)
            start_values(6)
            pass_mine(3, up_mine[3], up_mine[4], kup.at[3])
            pass_mine(5, down_mine[3])
            pass_other(2, up_other[2], up_other[3], kup.at[2])
            pass_other(6, down_other[2], down_other[3], kdn.at[2])

        @pl.when(t == 8)
        def _():
            pass_mine(2, up_mine[2], up_mine[3], kup.at[2])
            pass_mine(6, down_mine[2], down_mine[3], kdn.at[2])

        @pl.when(t == 9)
        def _():
            start_values(1)
            start_values(7)
            pass_other(1, up_other[1], up_other[2], kup.at[1])
            pass_other(7, down_other[1], down_other[2], kdn.at[1])

    def both_ways(t, carry):
        packed = jnp.int32(0)
        for n, (i, distance) in enumerate(table):
            packed = jnp.where(t == n, jnp.int32(i + 4 * distance), packed)
        pl.when(t < 5)(lambda: before(t))

        @pl.when(t == 9)
        def _():
            work((OPP, both_y(0)))

        distance = packed // 4
        work((packed % 4, both_y(distance) + both_y(NZ - distance)))
        pl.when(t > 3)(lambda: after(t))
        return carry

    lax.fori_loop(start, len(table), both_ways, jnp.int32(0))
    qtx[OPP] = dqa[OPP].astype(BF16)
    begin(*opp_sum)
    if fold:
        work((LEFT, both_y(0)))
    else:
        work((LEFT, both_y(0), (0,)), (RIGHT, both_y(0), (1,)))
        qtx[RIGHT, 1] = dqa[RIGHT, 1].astype(BF16)
        begin(right_sum[0])
    qtx[LEFT, 0] = dqa[LEFT, 0].astype(BF16)
    begin(left_sum[0])
    if fold:
        work((RIGHT, both_y(0)))
        qtx[RIGHT, 1] = dqa[RIGHT, 1].astype(BF16)
        begin(right_sum[0])
    else:
        work((LEFT, both_y(0), (1,)), (RIGHT, both_y(0), (0,)))
    arrive(*opp_sum)
    qtx[RIGHT, 0] = (dqa[RIGHT, 0] + orx[0].astype(F32)).astype(BF16)
    qtx[LEFT, 1] = (dqa[LEFT, 1] + orx[1].astype(F32)).astype(BF16)
    begin(right_sum[1], left_sum[1])
    pass_mine(1, up_mine[1], up_mine[2], kup.at[1])
    pass_mine(7, down_mine[1], down_mine[2], kdn.at[1])
    start_values(0)
    arrive(up_other[1], down_other[1])
    ktx[0, 1, 0] = (dka[0, 1, 0] + kup[0, 1, 0].astype(F32) + kdn[0, 1, 0].astype(F32)).astype(BF16)
    begin(across_sum)
    arrive(up_mine[1], down_mine[1])
    dk = dka[0, 0, 0] + kup[0, 0, 0].astype(F32) + kdn[0, 0, 0].astype(F32)
    dv = dka[0, 0, 1] + kup[0, 0, 1].astype(F32) + kdn[0, 0, 1].astype(F32)
    arrive(value_sum[0], across_sum)
    dk_out[...] = (dk + yrx[...].astype(F32)) * SCALE
    dv_out[...] = dv + vrx[0].astype(F32)
    for j, (a, b) in enumerate(((1, 0), (0, 1))):
        arrive(right_sum[a], left_sum[b])
        dq = dqa[OWN, j] + qrx[0, j].astype(F32) + qrx[1, j].astype(F32)
        dq_out[j] = dq.T * SCALE

    for copy in to_right + to_left + far_right + far_left + across + own_up + own_down + [across_sum]:
        copy.wait_send()
    for group in up_kv + down_kv:
        for copy in group:
            if copy is not None:
                copy.wait_send()
    for group in (values, up_mine, up_other, down_mine, down_other, value_sum):
        for copy in group.values():
            copy.wait_send()
    for copy in opp_sum + right_sum + left_sum:
        copy.wait_send()


N_COPIES = 16 + 25 + 23


def grads(fold, order, q, do, out, lse, k, v):
    smem = pl.BlockSpec(memory_space=pltpu.SMEM)
    vmem = pl.BlockSpec(memory_space=pltpu.VMEM)
    landing = [pltpu.VMEM((2, 2, ROWS, BLK), BF16)] * 3 + [pltpu.VMEM((2, 2, 1, ROWS), F32)] * 3
    queries = [
        pltpu.VMEM((4, 2, 2, ROWS, BLK), BF16),
        pltpu.VMEM((4, 2, 2, BLK, ROWS), BF16),
        pltpu.VMEM((4, 2, 2, 1, ROWS), F32),
    ]
    return pl.pallas_call(
        functools.partial(kernel, fold),
        out_shape=(
            jax.ShapeDtypeStruct((2, ROWS, BLK), F32),
            jax.ShapeDtypeStruct((TOK, BLK), F32),
            jax.ShapeDtypeStruct((TOK, BLK), F32),
        ),
        in_specs=[smem] + [pl.BlockSpec(memory_space=pltpu.HBM)] * 6,
        out_specs=(vmem, vmem, vmem),
        scratch_shapes=landing + queries + [
            pltpu.VMEM((NZ, NY, 2, TOK, BLK), BF16),
            pltpu.VMEM((NZ, NY, BLK, TOK), BF16),
            pltpu.VMEM((4, 2, BLK, ROWS), F32),
            pltpu.VMEM((NZ, NY, 2, TOK, BLK), F32),
            pltpu.VMEM((NZ, NY, 2, TOK, BLK), BF16),
            pltpu.VMEM((4, NY, 2, TOK, BLK), BF16),
            pltpu.VMEM((4, NY, 2, TOK, BLK), BF16),
            pltpu.VMEM((NZ, TOK, BLK), BF16),
            pltpu.VMEM((TOK, BLK), BF16),
            pltpu.VMEM((4, 2, BLK, ROWS), BF16),
            pltpu.VMEM((2, 2, BLK, ROWS), BF16),
            pltpu.VMEM((2, BLK, ROWS), BF16),
            pltpu.VMEM((2, ROWS, BLK), BF16),
            pltpu.VMEM((4, TOK), F32),
            pltpu.SemaphoreType.DMA((N_COPIES,)),
            pltpu.SemaphoreType.DMA((N_COPIES,)),
            pltpu.SemaphoreType.DMA((8,)),
        ],
        compiler_params=pltpu.CompilerParams(
            collective_id=0 if fold else 1, has_side_effects=True, vmem_limit_bytes=48 * 1024 * 1024
        ),
        name="folded" if fold else "whole",
    )(order, q, do, out, lse, k, v)


def hand_out(dq_in, dk_in, dv_in, dq_out, dk_out, dv_out, sem):
    copies = [
        pltpu.make_async_copy(src, dst, sem.at[n])
        for n, (src, dst) in enumerate(((dq_in, dq_out), (dk_in, dk_out), (dv_in, dv_out)))
    ]
    for copy in copies:
        copy.start()
    for copy in copies:
        copy.wait()


def per_device(query, key_proj, value, output, lse, d_output, block_order):
    args = (
        block_order,
        query.reshape(2, ROWS, BLK),
        d_output.reshape(2, ROWS, BLK),
        output.reshape(2, ROWS, BLK),
        lse.T,
        key_proj.reshape(TOK, BLK),
        value.reshape(TOK, BLK),
    )
    slots = jnp.arange(block_order.shape[0], dtype=jnp.int32)
    is_folded = jnp.sum(jnp.where(slots < 2, block_order, 0)) == 2 * NX * NY * NZ - 1
    dq, dk, dv = lax.cond(is_folded, functools.partial(grads, True), functools.partial(grads, False), *args)
    anywhere = pl.BlockSpec(memory_space=pl.ANY)
    dq, dk, dv = pl.pallas_call(
        hand_out,
        out_shape=tuple(jax.ShapeDtypeStruct(a.shape, a.dtype) for a in (dq, dk, dv)),
        in_specs=[anywhere] * 3,
        out_specs=(pl.BlockSpec(memory_space=pltpu.HBM),) * 3,
        scratch_shapes=[pltpu.SemaphoreType.DMA((3,))],
        name="hand_out",
    )(dq, dk, dv)
    return dq.reshape(query.shape), dk.reshape(key_proj.shape), dv.reshape(value.shape)


def solution(mesh):
    in_specs = (
        P("ctx", "head", None),
        P("ctx", "head", None),
        P("ctx", "head", None),
        P("ctx", "head", None),
        P("ctx", "head"),
        P("ctx", "head", None),
        P(),
    )
    out_specs = (P("ctx", "head", None), P("ctx", "head", None), P("ctx", "head", None))
    return jax.shard_map(
        per_device, mesh=mesh, in_specs=in_specs, out_specs=out_specs, check_vma=False
    )
```
